32 devices in a mesh: row: 4 (over y, x), col: 8 (over z, core).
Axes of the slice: x: 2, y: 2, z: 4, core: 2. Of those that a mesh axis runs over, the one named last changes fastest.
Arguments:
- tokens: bfloat16 [32768, 1024], P(('row', 'col')), may hold values from -6 to 6
- lengths: int32 [32, 4], replicated, may hold values from 1 to 330, 992 in all within a row
- positives: int32 [32], replicated, may hold values from 0 to 127
- w_qkv: bfloat16 [1024, 3072], P(('row', 'col')), may hold values from -0.1875 to 0.1875
- b_qkv: bfloat16 [3072], P(('row', 'col')), may hold values from -1.75 to 1.75
- w_out: bfloat16 [1024, 1024], P(('row', 'col')), may hold values from -0.75 to 0.75
- b_out: bfloat16 [1024], P(('row', 'col')), may hold values from -1.75 to 1.75
- norm1_gain: bfloat16 [1024], P(('row', 'col')), may hold values from 0.25 to 1.75
- norm1_bias: bfloat16 [1024], P(('row', 'col')), may hold values from -1.75 to 1.75
- w_up: bfloat16 [1024, 4096], P(('row', 'col')), may hold values from -0.1875 to 0.1875
- b_up: bfloat16 [4096], P(('row', 'col')), may hold values from -1.75 to 1.75
- w_down: bfloat16 [4096, 1024], P(('row', 'col')), may hold values from -0.09375 to 0.09375
- b_down: bfloat16 [1024], P(('row', 'col')), may hold values from -1.75 to 1.75
- norm2_gain: bfloat16 [1024], P(('row', 'col')), may hold values from 0.25 to 1.75
- norm2_bias: bfloat16 [1024], P(('row', 'col')), may hold values from -1.75 to 1.75
- w_proj: bfloat16 [1024, 288], P(('row', 'col')), may hold values from -0.1875 to 0.1875
Outputs:
- loss_terms: float32 [3, 32], P(None, 'row')
- activations: bfloat16 [32768, 1024], P(('row', 'col'))
- input_grad: float32 [32768, 1024], P(('row', 'col'))
- grad_w_qkv: float32 [1024, 3072], P(('row', 'col'))
- grad_b_qkv: float32 [3072], P(('row', 'col'))
- grad_w_out: float32 [1024, 1024], P(('row', 'col'))
- grad_b_out: float32 [1024], P(('row', 'col'))
- grad_norm1_gain: float32 [1024], P(('row', 'col'))
- grad_norm1_bias: float32 [1024], P(('row', 'col'))
- grad_w_up: float32 [1024, 4096], P(('row', 'col'))
- grad_b_up: float32 [4096], P(('row', 'col'))
- grad_w_down: float32 [4096, 1024], P(('row', 'col'))
- grad_b_down: float32 [1024], P(('row', 'col'))
- grad_norm2_gain: float32 [1024], P(('row', 'col'))
- grad_norm2_bias: float32 [1024], P(('row', 'col'))
- grad_w_proj: float32 [1024, 288], P(('row', 'col'))
The draws below stay inside these ranges and needn't reach their ends.
Inputs may be any that keep to these rules, and one draw needn't show every extreme that they name: Each row's 4 document lengths sum to 992; in every row the longest is exactly 330.
All inputs are finite; a program needn't handle non-finite values.
Results may differ from the reference program's by a relative error of at most 0.015.
Values may be sent and summed in bfloat16 or wider, within the bound.
No kernel may reach another device: no remote copies, remote signals or barrier semaphores. Data moves between devices by JAX's collectives and lax.ppermute only.
A program may use at most 448 MiB of HBM per device.

```python
import math
import jax
import jax.numpy as jnp
import numpy as np
from jax import lax

D = 1024
HEADS = 16
HEAD_DIM = 64
FF = 4096
PROJ_A = 128
PROJ_B = 96
PROJ_C = 64
QLEN = 32
ROW_LEN = 1024
DPR = 4
QPR = 1
EMB = 288
DTOK = 992
DMOST = 330
ROWS = 32
TOKENS = 32768
NQ = 32
DOCS = 128


def set_ends(entries, own_key, smallest, high):
    shape = entries.shape
    place = [jax.random.randint(jax.random.fold_in(own_key, axis), (), 0, shape[axis]) for axis in range(len(shape))]
    entries = entries.at[tuple(place)].set(smallest)
    longest = shape.index(max(shape))
    place[longest] = (place[longest] + 1) % shape[longest]
    return entries.at[tuple(place)].set(high)


def steps_of(rng, extent, cuts, least, top_value):
    loudness = 1.0
    for axis_at, blocks in cuts:
        draws = jax.random.uniform(jax.random.fold_in(jax.random.fold_in(rng, 6), axis_at), (blocks,), jnp.float32, least / len(cuts), top_value / len(cuts))
        loudness = loudness * jnp.repeat(jnp.exp(draws), extent[axis_at] // blocks).reshape((-1,) + (1,) * (len(extent) - 1 - axis_at))
    return loudness


def profile(amount, total, bound, slope):
    weights = [(1 << 20) // math.isqrt(grade ** slope) + 1 for grade in range(2, amount + 1)]
    surplus, counts = total - bound - (amount - 1), [1] * (amount - 1)
    while surplus > 0:
        movable = [i for i in range(amount - 1) if counts[i] < bound]
        pool, left = sum([weights[i] for i in movable]), surplus
        for i in movable:
            more = min(bound - counts[i], max(1, left * weights[i] // pool), surplus)
            counts[i] = counts[i] + more
            surplus = surplus - more
    return np.array([bound] + counts)


def uneven(rng, number_of, total, bound, skew):
    if number_of == 2:
        one = jax.random.randint(rng, (), max(1, total - bound), min(bound, total - 1) + 1)
        return jnp.stack([one, total - one])
    sizes = jnp.asarray(profile(number_of, total, bound, skew), jnp.int32)
    couples = (number_of - 1) // 2
    donor, sink = sizes[1:1 + 2 * couples:2], sizes[2:2 + 2 * couples:2]
    margin = jnp.minimum(donor - 1, bound - sink)
    shifted = jax.random.randint(jax.random.fold_in(rng, 1), (couples,), 0, 1 << 20) % (margin + 1)
    sizes = sizes.at[1:1 + 2 * couples:2].set(donor - shifted).at[2:2 + 2 * couples:2].set(sink + shifted)
    return sizes[jax.random.permutation(jax.random.fold_in(rng, 2), number_of)]


def noise(rng, extent, spread, limit, split=(), held_as=jnp.bfloat16):
    array = spread * jax.random.normal(rng, extent, jnp.float32)
    if split:
        array = array * steps_of(rng, extent, split, -0.22, 0.18)
    return jnp.clip(array, -limit, limit).astype(held_as)


def setup_inputs(seed: int = 0) -> dict:
    seeds = jax.random.split(jax.random.key(seed), 17)
    tokens = noise(seeds[0], (TOKENS, D), 1.0, 6.0, ((0, 32),))
    lengths = jax.vmap(lambda own: uneven(own, DPR, DTOK, DMOST, 1))(jax.random.split(seeds[1], ROWS)).reshape((ROWS, DPR)).astype(jnp.int32)
    positives = set_ends(jax.random.randint(seeds[2], (NQ,), 0, DOCS), jax.random.fold_in(seeds[2], 1), 0, DOCS - 1).astype(jnp.int32)
    w_qkv = noise(seeds[3], (D, 3 * D), D ** -0.5, 0.1875, ((0, 32),))
    b_qkv = noise(seeds[4], (3 * D,), 0.3, 1.75, ((0, 32),))
    w_out = noise(seeds[5], (D, D), (D // 16) ** -0.5, 0.75, ((0, 32),))
    b_out = noise(seeds[6], (D,), 0.3, 1.75, ((0, 32),))
    norm1_gain = jnp.clip(1.0 + 0.15 * jax.random.normal(seeds[7], (D,), jnp.float32), 0.25, 1.75).astype(jnp.bfloat16)
    norm1_bias = noise(seeds[8], (D,), 0.3, 1.75, ((0, 32),))
    w_up = noise(seeds[9], (D, FF), D ** -0.5, 0.1875, ((0, 32),))
    b_up = noise(seeds[10], (FF,), 0.3, 1.75, ((0, 32),))
    w_down = noise(seeds[11], (FF, D), FF ** -0.5, 0.09375, ((0, 32),))
    b_down = noise(seeds[12], (D,), 0.3, 1.75, ((0, 32),))
    norm2_gain = jnp.clip(1.0 + 0.15 * jax.random.normal(seeds[13], (D,), jnp.float32), 0.25, 1.75).astype(jnp.bfloat16)
    norm2_bias = noise(seeds[14], (D,), 0.3, 1.75, ((0, 32),))
    w_proj = noise(seeds[15], (D, EMB), D ** -0.5, 0.1875, ((0, 32),))
    return {"tokens": tokens, "lengths": lengths, "positives": positives, "w_qkv": w_qkv, "b_qkv": b_qkv, "w_out": w_out, "b_out": b_out, "norm1_gain": norm1_gain, "norm1_bias": norm1_bias, "w_up": w_up, "b_up": b_up, "w_down": w_down, "b_down": b_down, "norm2_gain": norm2_gain, "norm2_bias": norm2_bias, "w_proj": w_proj}


@jax.custom_vjp
def low(v):
    return lax.optimization_barrier(v.astype(jnp.bfloat16)).astype(jnp.float32)

@jax.custom_vjp
def low_back(v):
    return v

def low_keep(v):
    return (low(v), None)

def low_pass(kept, grad):
    return (grad,)

def back_keep(v):
    return (v, None)

def back_low(kept, grad):
    return (low(grad),)
low.defvjp(low_keep, low_pass)
low_back.defvjp(back_keep, back_low)
highest = lax.Precision.HIGHEST
eps_norm = 1e-05
eps_vec = 1e-06
score_scale = 16.0

def head_slices():
    return ((0, PROJ_A), (PROJ_A, PROJ_B), (PROJ_A + PROJ_B, PROJ_C))

def layout(lengths, row_len, q_tokens):
    doc_count = lengths.shape[1]
    places = jnp.arange(row_len, dtype=jnp.int32)
    doc_ends = jnp.cumsum(lengths, axis=1)
    doc_starts = doc_ends - lengths
    offset = places[None, :] - q_tokens
    doc_index = lax.optimization_barrier(jnp.sum((offset[:, :, None] >= doc_ends[:, None, :]).astype(jnp.int32), axis=2))
    chosen = (doc_index[:, :, None] == jnp.arange(doc_count, dtype=jnp.int32)[None, None, :]).astype(jnp.int32)
    doc_start = lax.optimization_barrier(jnp.sum(chosen * doc_starts[:, None, :], axis=2))
    is_query = places[None, :] < q_tokens
    segment = jnp.where(is_query, places[None, :] // QLEN, q_tokens // QLEN + doc_index)
    position = jnp.where(is_query, places[None, :] % QLEN, offset - doc_start)
    return (segment, position, doc_index)

def rotate(values, position):
    half_dim = values.shape[-1] // 2
    frequency = 10000.0 ** (-jnp.arange(half_dim, dtype=jnp.float32) / half_dim)
    angles = position.astype(jnp.float32)[:, None] * frequency[None, :]
    cosine = jnp.cos(angles)[:, None, :]
    sine_part = jnp.sin(angles)[:, None, :]
    first_half = values[..., :half_dim]
    second = values[..., half_dim:]
    return jnp.concatenate([first_half * cosine - second * sine_part, second * cosine + first_half * sine_part], axis=-1)

def layer_norm(resid_in, gain_vec, shift_vec):
    mean_val = lax.optimization_barrier(jnp.mean(resid_in, axis=-1, keepdims=True))
    centered = resid_in - mean_val
    variance = lax.optimization_barrier(jnp.mean(centered * centered, axis=-1, keepdims=True))
    return centered * lax.rsqrt(variance + eps_norm) * gain_vec + shift_vec

def normalize_heads(raw_vecs):
    pieces = []
    for head_start, head_width in head_slices():
        head_part = raw_vecs[:, head_start:head_start + head_width]
        pieces.append(head_part * lax.rsqrt(lax.optimization_barrier(jnp.sum(head_part * head_part, axis=1, keepdims=True)) + eps_vec))
    return jnp.concatenate(pieces, axis=1)

def layer_row(layer_params, x_row, seg_row, pos_row):
    w_qkv, b_qkv, w_out, b_out, gain_one, bias_one, w_up, b_up, w_down, b_down, gain_two, bias_two = layer_params
    length = x_row.shape[0]
    qkv_all = low_back(jnp.dot(x_row, w_qkv, precision=highest) + b_qkv)
    queries = low(rotate(qkv_all[:, :D].reshape(length, HEADS, HEAD_DIM), pos_row))
    key_vecs = low(rotate(qkv_all[:, D:2 * D].reshape(length, HEADS, HEAD_DIM), pos_row))
    values = low(qkv_all[:, 2 * D:].reshape(length, HEADS, HEAD_DIM))
    logits = low_back(jnp.einsum('qhd,khd->hqk', queries, key_vecs, precision=highest)) * HEAD_DIM ** (-0.5)
    allowed = seg_row[:, None] == seg_row[None, :]
    logits = jnp.where(allowed[None], logits, -1e+30)
    attn_probs = jax.nn.softmax(logits, axis=-1)
    attended = low(low_back(jnp.einsum('hqk,khd->qhd', low(attn_probs), values, precision=highest).reshape(length, D)))
    out_proj = low_back(jnp.dot(attended, w_out, precision=highest) + b_out)
    hidden_one = layer_norm(x_row + out_proj, gain_one, bias_one)
    inner_pre = low_back(jnp.dot(low(hidden_one), w_up, precision=highest) + b_up)
    gelu_out = low(jax.nn.gelu(inner_pre, approximate=False))
    branch = low_back(jnp.dot(gelu_out, w_down, precision=highest) + b_down)
    return layer_norm(hidden_one + branch, gain_two, bias_two)

def forward(x_all, params, lengths, positives):
    layer_params = tuple(params[:12])
    w_proj = params[12]
    q_tokens = QPR * QLEN
    segment, position, doc_index = layout(lengths, ROW_LEN, q_tokens)
    rows_in = x_all.reshape(ROWS, ROW_LEN, D)
    row_step = jax.checkpoint(lambda packed: layer_row(layer_params, packed[0], packed[1], packed[2]))
    outputs = lax.map(row_step, (rows_in, segment, position))
    rounded = low(outputs.reshape(TOKENS, D))
    raw_vecs = low_back(jnp.dot(rounded, w_proj, precision=highest))
    vectors = low(normalize_heads(raw_vecs)).reshape(ROWS, ROW_LEN, EMB)
    query_vecs = vectors[:, :q_tokens].reshape(NQ * QLEN, EMB)
    doc_vecs = vectors[:, q_tokens:].reshape(ROWS * DTOK, EMB)
    doc_ids = (doc_index[:, q_tokens:] + DPR * jnp.arange(ROWS, dtype=jnp.int32)[:, None]).reshape(ROWS * DTOK).astype(jnp.int32)
    log_count = jnp.log(lengths.reshape(DOCS).astype(jnp.float32))
    block_rows = math.gcd(NQ * QLEN, 256)

    def block_scores(query_block):
        per_head = []
        for head_start, head_width in head_slices():
            tok_scores = low_back(jnp.dot(query_block[:, head_start:head_start + head_width], doc_vecs[:, head_start:head_start + head_width].T, precision=highest)) * score_scale
            row_peak = lax.optimization_barrier(jnp.max(tok_scores, axis=1))
            exp_vals = jnp.exp(tok_scores - row_peak[:, None])
            doc_sums = jax.ops.segment_sum(exp_vals.T, doc_ids, num_segments=DOCS).T
            smooth = row_peak[:, None] + jnp.log(doc_sums) - log_count[None, :]
            per_head.append(lax.optimization_barrier(jnp.sum(smooth.reshape(block_rows // QLEN, QLEN, DOCS), axis=1)))
        return jnp.stack(per_head)
    doc_scores = lax.map(jax.checkpoint(block_scores), query_vecs.reshape(-1, block_rows, EMB))
    doc_scores = jnp.transpose(doc_scores, (1, 0, 2, 3)).reshape(3, NQ, DOCS)
    score_top = lax.optimization_barrier(jnp.max(doc_scores, axis=2, keepdims=True))
    total_lse = score_top[..., 0] + jnp.log(lax.optimization_barrier(jnp.sum(jnp.exp(doc_scores - score_top), axis=2)))
    positive_hot = (positives[:, None] == jnp.arange(DOCS, dtype=jnp.int32)[None, :]).astype(jnp.float32)
    positive_score = lax.optimization_barrier(jnp.sum(doc_scores * positive_hot[None], axis=2))
    losses = total_lse - positive_score
    return (jnp.sum(losses), (outputs.reshape(TOKENS, D), losses))

def reference(tokens, lengths, positives, w_qkv, b_qkv, w_out, b_out, norm1_gain, norm1_bias, w_up, b_up, w_down, b_down, norm2_gain, norm2_bias, w_proj):
    params = [item.astype(jnp.float32) for item in (w_qkv, b_qkv, w_out, b_out, norm1_gain, norm1_bias, w_up, b_up, w_down, b_down, norm2_gain, norm2_bias, w_proj)]

    def objective(x_all, param_list):
        return forward(x_all, param_list, lengths, positives)
    total_value, pullback, aux_out = jax.vjp(objective, tokens.astype(jnp.float32), params, has_aux=True)
    grad_x, grad_params = pullback(jnp.ones((), jnp.float32))
    outputs, losses = aux_out
    return (losses, outputs.astype(jnp.bfloat16), grad_x, grad_params[0], grad_params[1], grad_params[2], grad_params[3], grad_params[4], grad_params[5], grad_params[6], grad_params[7], grad_params[8], grad_params[9], grad_params[10], grad_params[11], grad_params[12])
```

```python
import functools

import jax
import jax.numpy as jnp
from jax import lax
from jax.experimental import pallas as pl
from jax.experimental.pallas import tpu as pltpu
from jax.sharding import PartitionSpec as P

D = 1024
HEADS = 16
HEAD_DIM = 64
PROJ_A = 128
PROJ_B = 96
PROJ_C = 64
QLEN = 32
DPR = 4
QPR = 1
DMOST = 330

AXES = ("row", "col")
highest = lax.Precision.HIGHEST
eps_norm = 1e-05
eps_vec = 1e-06
score_scale = 16.0
f32 = jnp.float32
bf16 = jnp.bfloat16


def sizes():
    n_rows = lax.axis_size("row")
    n_z = lax.axis_size("col") // 2
    return n_rows, n_z, n_rows.bit_length() - 1, n_z.bit_length() - 1


def place():
    col = lax.axis_index("col")
    return lax.axis_index("row"), col // 2, col % 2


def exchange(value, row_masks=(0, 0), z_mask=0, swap_core=False):
    n_rows, n_z, _, _ = sizes()
    pairs = []
    for r in range(n_rows):
        for z in range(n_z):
            for c in range(2):
                here = (r * n_z + z) * 2 + c
                there = ((r ^ row_masks[c]) * n_z + (z ^ z_mask)) * 2 + (
                    1 - c if swap_core else c
                )
                pairs.append((here, there))
    return lax.ppermute(value, AXES, pairs)


def stage_bit(core, stage, row_bits):
    return (stage + core) % row_bits


def stage_masks(stage):
    _, _, row_bits, _ = sizes()
    return tuple(1 << stage_bit(c, stage, row_bits) for c in range(2))


def piece_mask(core, piece):
    _, _, row_bits, _ = sizes()
    return sum(
        1 << stage_bit(core, j, row_bits) for j in range(row_bits) if piece >> j & 1
    )


def ordered(bit, own, other, axis):
    return jnp.stack([jnp.where(bit == 0, own, other), jnp.where(bit == 0, other, own)], axis)


def gather_pieces(shard):
    n_rows, n_z, row_bits, z_bits = sizes()
    _, z, _ = place()
    held = shard
    for count, bit in enumerate(reversed(range(z_bits))):
        other = exchange(held, z_mask=1 << bit)
        held = ordered(z >> bit & 1, held, other, count)
    pieces = [held.reshape((n_z,) + shard.shape)]
    for stage in range(row_bits):
        pieces = pieces + [exchange(p, row_masks=stage_masks(stage)) for p in pieces]
    return pieces, [exchange(p, swap_core=True) for p in pieces]


def piece_table():
    n_rows, _, _, _ = sizes()
    row, _, core = place()
    tables = [
        jnp.array([piece_mask(c, k) for k in range(n_rows)], jnp.int32) for c in range(2)
    ]
    own = row ^ jnp.where(core == 0, tables[0], tables[1])
    sib = row ^ jnp.where(core == 0, tables[1], tables[0])
    return jnp.concatenate([own, sib, core[None]]).astype(jnp.int32)


def assemble_kernel(n_rows, table, *refs):
    pieces, out, sems = refs[: 2 * n_rows], refs[2 * n_rows], refs[2 * n_rows + 1]
    core = table[2 * n_rows]
    copies = []
    for k in range(n_rows):
        for half in range(2):
            index = half * n_rows + k
            side = core if half == 0 else 1 - core
            copies.append(
                pltpu.make_async_copy(
                    pieces[index], out.at[table[index], :, side], sems.at[index]
                )
            )
    for c in copies:
        c.start()
    for c in copies:
        c.wait()


def assemble(table, pieces, sibs):
    n_rows, n_z, _, _ = sizes()
    _, r, n = pieces[0].shape
    out = pl.pallas_call(
        functools.partial(assemble_kernel, n_rows),
        grid_spec=pltpu.PrefetchScalarGridSpec(
            num_scalar_prefetch=1,
            grid=(1,),
            in_specs=[pl.BlockSpec(memory_space=pl.ANY)] * (2 * n_rows),
            out_specs=pl.BlockSpec(memory_space=pltpu.VMEM),
            scratch_shapes=[pltpu.SemaphoreType.DMA((2 * n_rows,))],
        ),
        compiler_params=pltpu.CompilerParams(vmem_limit_bytes=32 << 20),
        out_shape=jax.ShapeDtypeStruct((n_rows, n_z, 2, r, n), pieces[0].dtype),
        cost_estimate=pl.CostEstimate(
            flops=0, bytes_accessed=n_rows * n_z * 8 * r * n, transcendentals=0
        ),
        name="assemble",
    )(table, *pieces, *sibs)
    return out.reshape(n_rows * n_z * 2 * r, n)


def gather_small(shard):
    n_rows, n_z, row_bits, z_bits = sizes()
    row, z, core = place()
    held = shard
    for count, bit in enumerate(reversed(range(z_bits))):
        held = ordered(z >> bit & 1, held, exchange(held, z_mask=1 << bit), count)
    for count, bit in enumerate(reversed(range(row_bits))):
        other = exchange(held, row_masks=(1 << bit, 1 << bit))
        held = ordered(row >> bit & 1, held, other, count)
    held = ordered(core, held, exchange(held, swap_core=True), row_bits + z_bits)
    return held.reshape((n_rows * n_z * 2,) + shard.shape)


def scatter_small(blocks, dtype):
    n_rows, n_z, row_bits, z_bits = sizes()
    row, z, core = place()
    held = blocks.reshape((2,) * (row_bits + z_bits + 1) + blocks.shape[1:])

    def halve(held, axis, bit, **move):
        send = lax.dynamic_index_in_dim(held, 1 - bit, axis, keepdims=False)
        keep = lax.dynamic_index_in_dim(held, bit, axis, keepdims=False)
        return keep.astype(f32) + exchange(send.astype(dtype), **move).astype(f32)

    held = halve(held, row_bits + z_bits, core, swap_core=True)
    for bit in range(row_bits):
        held = halve(held, row_bits - 1 - bit, row >> bit & 1, row_masks=(1 << bit, 1 << bit))
    for bit in range(z_bits):
        held = halve(held, z_bits - 1 - bit, z >> bit & 1, z_mask=1 << bit)
    return held


def scatter_pieces(own, sib):
    n_rows, n_z, row_bits, z_bits = sizes()
    _, z, _ = place()
    terms = [own, exchange(sib, swap_core=True)]

    def total(parts):
        out = parts[0].astype(f32)
        for part in parts[1:]:
            out = out + part.astype(f32)
        return out

    for stage in reversed(range(row_bits)):
        half = 1 << stage
        send = total([t[half : 2 * half] for t in terms]).astype(bf16)
        terms = [t[:half] for t in terms] + [exchange(send, row_masks=stage_masks(stage))]
    terms = [t.reshape((2,) * z_bits + t.shape[2:]) for t in terms]
    for bit in range(z_bits):
        axis = z_bits - 1 - bit
        take = lambda t, b: lax.dynamic_index_in_dim(t, b, axis, keepdims=False)
        mine = z >> bit & 1
        send = total([take(t, 1 - mine) for t in terms]).astype(bf16)
        terms = [take(t, mine) for t in terms] + [exchange(send, z_mask=1 << bit)]
    return total(terms)


def scatter_matrix(table, grad):
    n_rows, n_z, _, _ = sizes()
    _, _, core = place()
    rows, n = grad.shape
    grad = grad.reshape(n_rows, n_z, 2, rows // (n_rows * n_z * 2), n)

    def picked(offset, side):
        return jnp.stack(
            [
                lax.dynamic_slice(
                    grad,
                    (table[offset + k], 0, side, 0, 0),
                    (1, n_z, 1, grad.shape[3], n),
                )[0, :, 0]
                for k in range(n_rows)
            ]
        )

    return scatter_pieces(picked(0, core), picked(n_rows, 1 - core))


WIN = -(-(DMOST + 15) // 32) * 32
NEG = -1e30


def contract(a, b, ca, cb):
    return lax.dot_general(a, b, (((ca,), (cb,)), ((), ())), preferred_element_type=f32)


def spans(len_ref, row_len):
    found = []
    start = jnp.int32(QPR * QLEN)
    for d in range(DPR):
        size = len_ref[d]
        base = pl.multiple_of(jnp.minimum((start // 16) * 16, row_len - WIN), 16)
        found.append((base, start - base, start - base + size))
        start = start + size
    return found


def head_pair(x):
    lane = lax.broadcasted_iota(jnp.int32, x.shape, 1)
    zero = jnp.zeros_like(x)
    return jnp.concatenate(
        [jnp.where(lane < HEAD_DIM, x, zero), jnp.where(lane < HEAD_DIM, zero, x)], axis=0
    )


def pair_heads(x):
    n = x.shape[0] // 2
    lane = lax.broadcasted_iota(jnp.int32, (n, x.shape[1]), 1)
    return jnp.where(lane < HEAD_DIM, x[:n], x[n:])


def inside(n, low, high, axis):
    shape = (n, 1) if axis == 0 else (1, n)
    at = lax.broadcasted_iota(jnp.int32, shape, axis)
    return (at >= low) & (at < high)


def attend(q, k, v, low, high):
    s = contract(head_pair(q), k, 1, 1)
    s = s + jnp.where(inside(k.shape[0], low, high, 1), 0.0, NEG)
    p = jnp.exp(s - jnp.max(s, axis=1, keepdims=True))
    total = jnp.sum(p, axis=1, keepdims=True)
    return pair_heads(contract(p.astype(bf16), v, 1, 0) / total)


def attention_kernel(len_ref, q_ref, k_ref, v_ref, o_ref):
    row_len = q_ref.shape[0]
    for base, low, high in spans(len_ref, row_len):
        w = pl.ds(base, WIN)
        o = attend(q_ref[w, :], k_ref[w, :], v_ref[w, :], low, high)
        keep = inside(WIN, low, high, 0)
        o_ref[w, :] = jnp.where(keep, o, o_ref[w, :].astype(f32)).astype(bf16)
    o_ref[:QLEN, :] = attend(q_ref[:QLEN, :], k_ref[:128, :], v_ref[:128, :], 0, QLEN).astype(bf16)


def attention(lengths, q, k, v):
    t = q.shape[0]
    spec = pl.BlockSpec((t, 128), lambda i, _: (0, i))
    return pl.pallas_call(
        attention_kernel,
        grid_spec=pltpu.PrefetchScalarGridSpec(
            num_scalar_prefetch=1, grid=(HEADS // 2,), in_specs=[spec] * 3, out_specs=spec
        ),
        out_shape=jax.ShapeDtypeStruct(q.shape, bf16),
        compiler_params=pltpu.CompilerParams(vmem_limit_bytes=48 << 20),
        cost_estimate=pl.CostEstimate(
            flops=2 * 10**10, bytes_accessed=8 << 20, transcendentals=10**7
        ),
        name="attention",
    )(lengths, q, k, v)


def attend_back(q, k, v, g, low, high):
    n = q.shape[0]
    g = jnp.where(inside(n, low, high, 0), g, jnp.zeros_like(g))
    qq = head_pair(q)
    gg = head_pair(g)
    st = contract(k, qq, 1, 1)
    st = st + jnp.where(inside(k.shape[0], low, high, 0), 0.0, NEG)
    p = jnp.exp(st - jnp.max(st, axis=0, keepdims=True))
    p = p * (1.0 / jnp.sum(p, axis=0, keepdims=True))
    dp = contract(v, gg, 1, 1)
    delta = jnp.sum(p * dp, axis=0, keepdims=True)
    ds = (p * (dp - delta)).astype(bf16)
    dv = contract(p.astype(bf16), gg, 1, 0)
    dk = contract(ds, qq, 1, 0)
    dq = contract(ds, k, 0, 0) * (HEAD_DIM**-0.5)
    return pair_heads(dq), dk, dv


def attention_back_kernel(len_ref, q_ref, k_ref, v_ref, g_ref, dq_ref, dk_ref, dv_ref):
    row_len = q_ref.shape[0]
    outs = (dq_ref, dk_ref, dv_ref)
    for ref in outs:
        ref[...] = jnp.zeros_like(ref)
    parts = attend_back(
        q_ref[:QLEN, :], k_ref[:128, :], v_ref[:128, :], g_ref[:QLEN, :], 0, QLEN
    )
    dq_ref[:QLEN, :] = parts[0].astype(bf16)
    dk_ref[:128, :] = parts[1].astype(bf16)
    dv_ref[:128, :] = parts[2].astype(bf16)
    for base, low, high in spans(len_ref, row_len):
        w = pl.ds(base, WIN)
        parts = attend_back(q_ref[w, :], k_ref[w, :], v_ref[w, :], g_ref[w, :], low, high)
        for ref, x in zip(outs, parts):
            ref[w, :] = (ref[w, :].astype(f32) + x).astype(bf16)


def attention_back(lengths, q, k, v, g):
    t = q.shape[0]
    spec = pl.BlockSpec((t, 128), lambda i, _: (0, i))
    out = jax.ShapeDtypeStruct(q.shape, bf16)
    return pl.pallas_call(
        attention_back_kernel,
        grid_spec=pltpu.PrefetchScalarGridSpec(
            num_scalar_prefetch=1, grid=(HEADS // 2,), in_specs=[spec] * 4, out_specs=[spec] * 3
        ),
        out_shape=[out] * 3,
        compiler_params=pltpu.CompilerParams(vmem_limit_bytes=48 << 20),
        cost_estimate=pl.CostEstimate(
            flops=5 * 10**10, bytes_accessed=16 << 20, transcendentals=10**7
        ),
        name="attention_back",
    )(lengths, q, k, v, g)


def head_slices():
    return ((0, PROJ_A), (PROJ_A, PROJ_B), (PROJ_A + PROJ_B, PROJ_C))


def layout(lengths, row_len, q_tokens):
    count = lengths.shape[0]
    before = jnp.arange(count)[:, None] <= jnp.arange(count)[None, :]
    ends = jnp.sum(jnp.where(before, lengths[:, None], 0), axis=0)
    offset = jnp.arange(row_len, dtype=jnp.int32) - q_tokens
    doc = jnp.sum((offset[:, None] >= ends[None, :]).astype(jnp.int32), axis=1)
    chosen = (doc[:, None] == jnp.arange(count, dtype=jnp.int32)[None, :]).astype(
        jnp.int32
    )
    begin = jnp.sum(chosen * (ends - lengths)[None, :], axis=1)
    is_query = offset < 0
    position = jnp.where(is_query, (offset + q_tokens) % QLEN, offset - begin)
    return position, doc


def turn(values, cosine, sine):
    x = values.reshape(values.shape[0], -1, HEAD_DIM)
    half = HEAD_DIM // 2
    a, b = x[..., :half], x[..., half:]
    c, s = cosine[:, None, :], sine[:, None, :]
    return jnp.concatenate([a * c - b * s, b * c + a * s], axis=-1).reshape(values.shape)


def layer_norm(resid_in, gain_vec, shift_vec):
    mean_val = jnp.mean(resid_in, axis=-1, keepdims=True)
    centered = resid_in - mean_val
    variance = jnp.mean(centered * centered, axis=-1, keepdims=True)
    return centered * lax.rsqrt(variance + eps_norm) * gain_vec + shift_vec


def normalize_heads(raw_vecs):
    pieces = []
    for head_start, head_width in head_slices():
        part = raw_vecs[:, head_start : head_start + head_width]
        pieces.append(part * lax.rsqrt(jnp.sum(part * part, axis=1, keepdims=True) + eps_vec))
    return jnp.concatenate(pieces, axis=1)


def matmul(a, b):
    return jnp.dot(a, b, preferred_element_type=f32)


def matmul_tn(a, b):
    return jnp.einsum("td,te->de", a, b, preferred_element_type=f32)


def matmul_nt(a, b):
    return jnp.einsum("te,de->td", a, b, preferred_element_type=f32)


def combine_stats(one, two):
    top = jnp.maximum(one[0], two[0])
    den = one[1] * jnp.exp(one[0] - top) + two[1] * jnp.exp(two[0] - top)
    return jnp.stack([top, den, one[2] + two[2]])


def reduce_stats(stats):
    _, _, row_bits, z_bits = sizes()
    stats = combine_stats(stats, exchange(stats, swap_core=True))
    for bit in range(row_bits):
        stats = combine_stats(stats, exchange(stats, row_masks=(1 << bit, 1 << bit)))
    for bit in range(z_bits):
        stats = combine_stats(stats, exchange(stats, z_mask=1 << bit))
    return stats


def on_device(
    tokens,
    lengths,
    positives,
    w_qkv,
    b_qkv,
    w_out,
    b_out,
    norm1_gain,
    norm1_bias,
    w_up,
    b_up,
    w_down,
    b_down,
    norm2_gain,
    norm2_bias,
    w_proj,
):
    n_rows, n_z, _, _ = sizes()
    n_devices = n_rows * n_z * 2
    row, z, core = place()
    device = (row * n_z + z) * 2 + core
    table = piece_table()
    row_len = tokens.shape[0]
    q_tokens = QPR * QLEN

    vectors = (b_qkv, b_out, norm1_gain, norm1_bias, b_up, b_down, norm2_gain, norm2_bias)
    widths = [v.shape[0] for v in vectors]
    packed = jnp.concatenate(vectors)
    pad = -packed.shape[0] % 128
    packed = jnp.pad(packed, (0, pad)).reshape(-1, 128)
    packed = gather_small(packed).reshape(n_devices, -1)
    whole = []
    at = 0
    for width in widths:
        whole.append(packed[:, at : at + width].reshape(-1).astype(f32))
        at += width
    full_bqkv, full_bout, gain_one, bias_one, full_bup, full_bdown, gain_two, bias_two = whole
    full_qkv = assemble(table, *gather_pieces(w_qkv))
    full_out = assemble(table, *gather_pieces(w_out))
    full_up = assemble(table, *gather_pieces(w_up))
    full_down = assemble(table, *gather_pieces(w_down))
    full_proj = gather_small(w_proj).reshape(-1, w_proj.shape[1])

    own_lengths = lax.dynamic_index_in_dim(lengths, device, 0, keepdims=False)
    position, doc_index = layout(own_lengths, row_len, q_tokens)
    frequency = 10000.0 ** (-jnp.arange(HEAD_DIM // 2, dtype=f32) / (HEAD_DIM // 2))
    angles = position.astype(f32)[:, None] * frequency[None, :]
    cosine, sine = jnp.cos(angles), jnp.sin(angles)
    qkv = matmul(tokens, full_qkv) + full_bqkv
    attn_scale = HEAD_DIM**-0.5
    queries = (turn(qkv[:, :D], cosine, sine) * attn_scale).astype(bf16)
    keys = turn(qkv[:, D : 2 * D], cosine, sine).astype(bf16)
    values = qkv[:, 2 * D :].astype(bf16)
    attended = attention(own_lengths, queries, keys, values)
    resid_one = tokens.astype(f32) + matmul(attended, full_out) + full_bout
    hidden_one, first_pull = jax.vjp(layer_norm, resid_one, gain_one, bias_one)

    hidden_low = hidden_one.astype(bf16)
    inner_pre = matmul(hidden_low, full_up) + full_bup
    gelu_out = jax.nn.gelu(inner_pre, approximate=False).astype(bf16)
    resid_two = hidden_one + matmul(gelu_out, full_down) + full_bdown
    result, second_pull = jax.vjp(layer_norm, resid_two, gain_two, bias_two)
    result_low = result.astype(bf16)

    normed, norm_pull = jax.vjp(normalize_heads, matmul(result_low, full_proj))
    vecs = normed.astype(bf16)
    query_all = gather_small(vecs[:q_tokens]).reshape(n_devices * q_tokens, -1)
    docs = vecs[q_tokens:]
    n_queries = n_devices * QPR
    doc_hot = (
        doc_index[q_tokens:][:, None] == jnp.arange(DPR, dtype=jnp.int32)[None, :]
    ).astype(f32)
    log_count = jnp.log(own_lengths.astype(f32))
    exps, sums, scores = [], [], []
    for start, width in head_slices():
        t = matmul_nt(query_all[:, start : start + width], docs[:, start : start + width])
        e = jnp.exp(t * score_scale)
        total = jnp.dot(e, doc_hot, precision=highest)
        smooth = jnp.log(total) - log_count
        exps.append(e)
        sums.append(total)
        scores.append(jnp.sum(smooth.reshape(n_queries, QLEN, DPR), axis=1))
    doc_scores = jnp.stack(scores)
    doc_ids = device * DPR + jnp.arange(DPR, dtype=jnp.int32)
    positive_hot = (positives[:, None] == doc_ids[None, :]).astype(f32)
    local_top = jnp.max(doc_scores, axis=2)
    local_den = jnp.sum(jnp.exp(doc_scores - local_top[..., None]), axis=2)
    local_pos = jnp.sum(doc_scores * positive_hot, axis=2)
    top, den, pos = reduce_stats(jnp.stack([local_top, local_den, local_pos]))
    query_count = n_z * 2 * QPR
    losses = lax.dynamic_slice_in_dim(
        top + jnp.log(den) - pos, row * query_count, query_count, 1
    )
    score_grad = jnp.exp(doc_scores - top[..., None]) / den[..., None] - positive_hot
    query_parts, doc_parts = [], []
    for head, (start, width) in enumerate(head_slices()):
        coef = score_scale * jnp.repeat(score_grad[head], QLEN, axis=0) / sums[head]
        spread = jnp.dot(coef, doc_hot.T, precision=highest)
        back = (exps[head] * spread).astype(bf16)
        query_parts.append(matmul(back, docs[:, start : start + width]))
        doc_parts.append(matmul_tn(back, query_all[:, start : start + width]))
    query_grads = jnp.concatenate(query_parts, axis=1)
    query_grad = scatter_small(query_grads.reshape(n_devices, q_tokens, -1), bf16)
    vector_grad = jnp.concatenate([query_grad, jnp.concatenate(doc_parts, axis=1)], axis=0)
    raw_grad = norm_pull(vector_grad)[0].astype(bf16)

    grad_proj = matmul_tn(result_low, raw_grad)
    result_grad = matmul_nt(raw_grad, full_proj)
    resid_two_grad, grad_gain2, grad_bias2 = second_pull(result_grad)
    branch_grad = resid_two_grad.astype(bf16)
    grad_bdown = jnp.sum(branch_grad.astype(f32), axis=0)
    sum_down = scatter_matrix(table, matmul_tn(gelu_out, branch_grad).astype(bf16))
    act_grad = matmul_nt(branch_grad, full_down)
    _, gelu_pull = jax.vjp(functools.partial(jax.nn.gelu, approximate=False), inner_pre)
    inner_grad = gelu_pull(act_grad)[0].astype(bf16)
    grad_bup = jnp.sum(inner_grad.astype(f32), axis=0)
    sum_up = scatter_matrix(table, matmul_tn(hidden_low, inner_grad).astype(bf16))
    hidden_grad = resid_two_grad + matmul_nt(inner_grad, full_up)
    resid_one_grad, grad_gain1, grad_bias1 = first_pull(hidden_grad)
    out_grad = resid_one_grad.astype(bf16)
    grad_bout = jnp.sum(out_grad.astype(f32), axis=0)
    sum_out = scatter_matrix(table, matmul_tn(attended, out_grad).astype(bf16))
    attended_grad = matmul_nt(out_grad, full_out).astype(bf16)
    dq, dk, dv = attention_back(own_lengths, queries, keys, values, attended_grad)
    qkv_grad = jnp.concatenate(
        [
            turn(dq.astype(f32), cosine, -sine).astype(bf16),
            turn(dk.astype(f32), cosine, -sine).astype(bf16),
            dv,
        ],
        axis=1,
    )
    grad_bqkv = jnp.sum(qkv_grad.astype(f32), axis=0)
    sum_qkv = scatter_matrix(table, matmul_tn(tokens, qkv_grad).astype(bf16))
    input_grad = resid_one_grad + matmul_nt(qkv_grad, full_qkv)
    sum_proj = scatter_small(grad_proj.reshape(n_devices, -1, grad_proj.shape[1]), bf16)
    small = [
        g.reshape(n_devices, -1)
        for g in (
            grad_bqkv,
            grad_bout,
            grad_gain1,
            grad_bias1,
            grad_bup,
            grad_bdown,
            grad_gain2,
            grad_bias2,
        )
    ]
    small = jnp.pad(jnp.concatenate(small, axis=1), ((0, 0), (0, pad)))
    small = scatter_small(small.reshape(n_devices, -1, 128), f32).reshape(-1)
    sums_small = []
    at = 0
    for width in widths:
        sums_small.append(small[at : at + width])
        at += width
    s_bqkv, s_bout, s_gain1, s_bias1, s_bup, s_bdown, s_gain2, s_bias2 = sums_small
    return (
        losses,
        result_low,
        input_grad,
        sum_qkv,
        s_bqkv,
        sum_out,
        s_bout,
        s_gain1,
        s_bias1,
        sum_up,
        s_bup,
        sum_down,
        s_bdown,
        s_gain2,
        s_bias2,
        sum_proj,
    )


def solution(mesh):
    shard = P(AXES, None)
    vec = P(AXES)
    in_specs = (
        shard,
        P(),
        P(),
        shard,
        vec,
        shard,
        vec,
        vec,
        vec,
        shard,
        vec,
        shard,
        vec,
        vec,
        vec,
        shard,
    )
    out_specs = (P(None, "row"), shard) + (shard,) + in_specs[3:]
    return jax.shard_map(
        on_device, mesh=mesh, in_specs=in_specs, out_specs=out_specs, check_vma=False
    )
```

```python
import functools

import jax
import jax.numpy as jnp
from jax import lax
from jax.experimental import pallas as pl
from jax.experimental.pallas import tpu as pltpu
from jax.sharding import PartitionSpec as P

D = 1024
HEADS = 16
HEAD_DIM = 64
PROJ_A = 128
PROJ_B = 96
PROJ_C = 64
QLEN = 32
DPR = 4
QPR = 1
DMOST = 330

AXES = ("row", "col")
highest = lax.Precision.HIGHEST
eps_norm = 1e-05
eps_vec = 1e-06
score_scale = 16.0
f32 = jnp.float32
bf16 = jnp.bfloat16


def sizes():
    n_rows = lax.axis_size("row")
    n_z = lax.axis_size("col") // 2
    return n_rows, n_z, n_rows.bit_length() - 1, n_z.bit_length() - 1


def after(value, *before):
    return lax.optimization_barrier((value,) + before)[0] if before else value


def place():
    col = lax.axis_index("col")
    return lax.axis_index("row"), col // 2, col % 2


def exchange(value, row_masks=(0, 0), z_mask=0, swap_core=False):
    n_rows, n_z, _, _ = sizes()
    pairs = []
    for r in range(n_rows):
        for z in range(n_z):
            for c in range(2):
                here = (r * n_z + z) * 2 + c
                there = ((r ^ row_masks[c]) * n_z + (z ^ z_mask)) * 2 + (
                    1 - c if swap_core else c
                )
                pairs.append((here, there))
    return lax.ppermute(value, AXES, pairs)


def stage_bit(core, stage, row_bits):
    return (stage + core) % row_bits


def stage_masks(stage):
    _, _, row_bits, _ = sizes()
    return tuple(1 << stage_bit(c, stage, row_bits) for c in range(2))


def piece_mask(core, piece):
    _, _, row_bits, _ = sizes()
    return sum(
        1 << stage_bit(core, j, row_bits) for j in range(row_bits) if piece >> j & 1
    )


def ordered(bit, own, other, axis):
    return jnp.stack([jnp.where(bit == 0, own, other), jnp.where(bit == 0, other, own)], axis)


def transfer(value, start=(), use=(), **move):
    return after(exchange(after(value, *start), **move), *use)


class Gather:
    def __init__(self, shard):
        self.held, self.count, self.shard = shard, 0, shard

    def along_z(self, start=(), use=()):
        _, n_z, _, z_bits = sizes()
        _, z, _ = place()
        bit = z_bits - 1 - self.count
        other = transfer(self.held, start, use, z_mask=1 << bit)
        self.held = ordered(z >> bit & 1, self.held, other, self.count)
        self.count += 1
        if self.count == z_bits:
            self.pieces = [self.held.reshape((n_z,) + self.shard.shape)]

    def all_z(self, *bounds):
        _, _, _, z_bits = sizes()
        for i in range(z_bits):
            self.along_z(*bounds[min(i, len(bounds) - 1)])

    def all_rows(self, first, rest):
        _, _, row_bits, _ = sizes()
        for stage in range(row_bits):
            self.pieces = self.pieces + [
                transfer(p, *(rest if i else first), row_masks=stage_masks(stage))
                for i, p in enumerate(self.pieces)
            ]

    def whole(self, table, early=(), late=()):
        last = len(self.pieces) - 1
        sibs = [
            transfer(p, *(late if i == last else early), swap_core=True)
            for i, p in enumerate(self.pieces)
        ]
        return Weight(table, self.pieces + sibs)


def piece_table():
    n_rows, _, _, _ = sizes()
    row, _, core = place()
    tables = [
        jnp.array([piece_mask(c, k) for k in range(n_rows)], jnp.int32) for c in range(2)
    ]
    own = row ^ jnp.where(core == 0, tables[0], tables[1])
    sib = row ^ jnp.where(core == 0, tables[1], tables[0])
    steps = jnp.arange(n_rows)

    def piece_of(rows):
        return jnp.sum(jnp.where(rows[None, :] == steps[:, None], steps[None, :], 0), axis=1)

    return jnp.concatenate([own, sib, core[None], piece_of(own), piece_of(sib)]).astype(jnp.int32)


class Weight:
    def __init__(self, table, pieces):
        n_rows, n_z, _, _ = sizes()
        self.table, self.pieces = table, pieces
        r, n = pieces[0].shape[1:]
        self.shape = (n_rows, n_z, 2, r, n)
        self.rows = n_rows * n_z * 2 * r

    def specs(self):
        return [pl.BlockSpec(memory_space=pl.ANY)] * len(self.pieces)

    def scratch(self):
        return [
            pltpu.VMEM(self.shape, self.pieces[0].dtype),
            pltpu.SemaphoreType.DMA((len(self.pieces) + 1,)),
        ]

    def out_shape(self):
        return jax.ShapeDtypeStruct(self.shape, self.pieces[0].dtype)


def load_weight(table, pieces, out_ref, w_ref, sems):
    n_rows = len(pieces) // 2
    core = table[2 * n_rows]
    out = pltpu.make_async_copy(w_ref, out_ref, sems.at[2 * n_rows])

    @pl.when(pl.program_id(0) == 0)
    def _():
        copies = [
            pltpu.make_async_copy(
                piece,
                w_ref.at[table[i], :, core if i < n_rows else 1 - core],
                sems.at[i],
            )
            for i, piece in enumerate(pieces)
        ]
        for c in copies:
            c.start()
        for c in copies:
            c.wait()
        out.start()

    @pl.when(pl.program_id(0) == pl.num_programs(0) - 1)
    def _():
        out.wait()


def gather_small(shard):
    n_rows, n_z, row_bits, z_bits = sizes()
    row, z, core = place()
    held = shard
    for count, bit in enumerate(reversed(range(z_bits))):
        held = ordered(z >> bit & 1, held, exchange(held, z_mask=1 << bit), count)
    for count, bit in enumerate(reversed(range(row_bits))):
        other = exchange(held, row_masks=(1 << bit, 1 << bit))
        held = ordered(row >> bit & 1, held, other, count)
    held = ordered(core, held, exchange(held, swap_core=True), row_bits + z_bits)
    return held.reshape((n_rows * n_z * 2,) + shard.shape)


def scatter_small(blocks, dtype):
    n_rows, n_z, row_bits, z_bits = sizes()
    row, z, core = place()
    held = blocks.reshape((2,) * (row_bits + z_bits + 1) + blocks.shape[1:])

    def halve(held, axis, bit, **move):
        send = lax.dynamic_index_in_dim(held, 1 - bit, axis, keepdims=False)
        keep = lax.dynamic_index_in_dim(held, bit, axis, keepdims=False)
        return keep.astype(f32) + exchange(send.astype(dtype), **move).astype(f32)

    held = halve(held, row_bits + z_bits, core, swap_core=True)
    for bit in range(row_bits):
        held = halve(held, row_bits - 1 - bit, row >> bit & 1, row_masks=(1 << bit, 1 << bit))
    for bit in range(z_bits):
        held = halve(held, z_bits - 1 - bit, z >> bit & 1, z_mask=1 << bit)
    return held


def gather_relative(block):
    n_rows, n_z, _, _ = sizes()
    held = jnp.stack([block] + [exchange(block, z_mask=m) for m in range(1, n_z)])
    held = jnp.stack([held] + [exchange(held, row_masks=(m, m)) for m in range(1, n_rows)])
    return jnp.stack([held, exchange(held, swap_core=True)])


def scatter_relative(blocks, dtype):
    n_rows, n_z, _, _ = sizes()

    def step(held, count, move):
        parts = [exchange(held[m].astype(dtype), **move(m)) for m in range(1, count)]
        total = held[0]
        for part in parts:
            total = total + part.astype(f32)
        return total

    held = step(blocks, 2, lambda m: dict(swap_core=True))
    held = step(held, n_rows, lambda m: dict(row_masks=(m, m)))
    return step(held, n_z, lambda m: dict(z_mask=m))


def relative_order():
    n_rows, n_z, _, _ = sizes()
    row, z, core = place()
    at = jnp.arange(n_rows * n_z * 2)
    there_core = core ^ at // (n_rows * n_z)
    there_row = row ^ at // n_z % n_rows
    return ((there_row * n_z + (z ^ at % n_z)) * 2 + there_core).astype(jnp.int32)


class Scatter:
    def __init__(self, send, keep, wide=False):
        _, _, row_bits, z_bits = sizes()
        self.send, self.keep = send, keep
        self.wide = ("z", z_bits - 1) if wide else None
        self.stages = [("row", j) for j in reversed(range(row_bits))]
        self.stages += [("z", b) for b in range(sizes()[3])]

    def step(self, *use):
        _, _, _, z_bits = sizes()
        _, z, _ = place()
        kind, at = self.stages.pop(0)
        move = dict(row_masks=stage_masks(at)) if kind == "row" else dict(z_mask=1 << at)
        parts = (self.keep, after(exchange(self.send, **move), *use))
        if not self.stages:
            return parts[0] + parts[1].astype(f32)
        kind, at = self.stages[0]
        if kind == "row":
            half = 1 << at
            pick = lambda x, other: x[half:] if other else x[:half]
        else:
            if at == 0:
                parts = tuple(x.reshape((2,) * z_bits + x.shape[2:]) for x in parts)
            mine = z >> at & 1
            pick = lambda x, other: lax.dynamic_index_in_dim(
                x, 1 - mine if other else mine, z_bits - 1 - at, keepdims=False
            )
        total = lambda other: pick(parts[0], other) + pick(parts[1], other).astype(f32)
        self.send, self.keep = total(True), total(False)
        if self.stages[0] != self.wide:
            self.send = self.send.astype(bf16)
        return self.send

    def finish(self, *use):
        while self.stages:
            out = self.step(*use)
        return out


def head_slices():
    return ((0, PROJ_A), (PROJ_A, PROJ_B), (PROJ_A + PROJ_B, PROJ_C))


LANES = 128


def whole_spec(shape):
    return pl.BlockSpec(
        shape, lambda *_: (0,) * len(shape), pipeline_mode=pl.Buffered(buffer_count=1)
    )


def row_spec(rows, width):
    return pl.BlockSpec((rows, width), lambda i, *_: (i, 0))


def col_spec(rows, width):
    return pl.BlockSpec((rows, width), lambda i, *_: (0, i))


def like(shape, dtype):
    return jax.ShapeDtypeStruct(shape, dtype)


def call(
    kernel, name, grid, in_specs, out_specs, out_shape, flops, moved, scratch=(), table=None, wait=(), aliases=None
):
    first = len(in_specs) + (0 if table is None else 1)
    in_specs = list(in_specs) + [pl.BlockSpec(memory_space=pl.ANY)] * len(wait)

    def body(*refs):
        kernel(*refs[:first], *refs[first + len(wait) :])

    run = pl.pallas_call(
        body,
        grid_spec=pltpu.PrefetchScalarGridSpec(
            num_scalar_prefetch=0 if table is None else 1,
            grid=grid,
            in_specs=in_specs,
            out_specs=out_specs,
            scratch_shapes=list(scratch),
        ),
        out_shape=out_shape,
        input_output_aliases=aliases or {},
        compiler_params=pltpu.CompilerParams(vmem_limit_bytes=56 << 20),
        cost_estimate=pl.CostEstimate(
            flops=int(flops), bytes_accessed=int(moved), transcendentals=0
        ),
        name=name,
    )
    return lambda *operands: run(*operands, *wait)


def swap_halves(x):
    lane = lax.broadcasted_iota(jnp.int32, x.shape, 1)
    half = HEAD_DIM // 2
    return jnp.where(
        lane % HEAD_DIM < half, pltpu.roll(x, LANES - half, 1), pltpu.roll(x, half, 1)
    )


QKV_TILE = 1024


def qkv_kernel(n_pieces, table, x_ref, b_ref, cos_ref, sin_ref, *refs):
    pieces, (o_ref, w_out, acc_ref, w_ref, sems) = refs[:n_pieces], refs[n_pieces:]
    load_weight(table, pieces, w_out, w_ref, sems)
    tile = pl.program_id(0)
    per_part = D // QKV_TILE
    cols = pl.ds(pl.multiple_of(tile * QKV_TILE, LANES), QKV_TILE)
    w = w_ref[:, :, :, :, cols].reshape(x_ref.shape[1], QKV_TILE)
    acc_ref[...] = contract(x_ref[...], w, 1, 0) + b_ref[...]

    @pl.when(tile < 2 * per_part)
    def _():
        scale = jnp.where(tile < per_part, HEAD_DIM**-0.5, 1.0)
        cosine = cos_ref[...] * scale
        sine = sin_ref[...] * scale
        for j in range(QKV_TILE // LANES):
            at = slice(j * LANES, (j + 1) * LANES)
            a = acc_ref[:, at]
            o_ref[:, at] = (a * cosine + swap_halves(a) * sine).astype(bf16)

    @pl.when(tile >= 2 * per_part)
    def _():
        o_ref[...] = acc_ref[...].astype(bf16)


def project_qkv(x, w, b, cosine, sine, wait=()):
    t = x.shape[0]
    any_out = pl.BlockSpec(memory_space=pl.ANY)
    return call(
        functools.partial(qkv_kernel, len(w.pieces)),
        "project_qkv",
        (3 * D // QKV_TILE,),
        [
            whole_spec((t, D)),
            pl.BlockSpec((1, QKV_TILE), lambda i, _: (0, i)),
            whole_spec((t, LANES)),
            whole_spec((t, LANES)),
        ]
        + w.specs(),
        [col_spec(t, QKV_TILE), any_out],
        [like((t, 3 * D), bf16), w.out_shape()],
        6 * t * D * D,
        20 * t * D,
        [pltpu.VMEM((t, QKV_TILE), f32)] + w.scratch(),
        table=w.table,
        wait=wait,
    )(w.table, x, b, cosine, sine, *w.pieces)


TILE = 256


def normalized(v):
    mean = jnp.mean(v, axis=1, keepdims=True)
    centered = v - mean
    rstd = lax.rsqrt(jnp.mean(centered * centered, axis=1, keepdims=True) + eps_norm)
    return centered * rstd, rstd


def norm_back(g, hat, rstd, gain):
    y = g * gain
    return rstd * (
        y - jnp.mean(y, axis=1, keepdims=True) - hat * jnp.mean(y * hat, axis=1, keepdims=True)
    )


def add_up(ref, value):
    @pl.when(pl.program_id(0) == 0)
    def _():
        ref[...] = jnp.zeros_like(ref)

    ref[...] += value


def column_sum(x):
    return jnp.sum(x, axis=0, keepdims=True)


def out_norm_kernel(n_pieces, table, a_ref, b_ref, x_ref, gain_ref, bias_ref, *refs):
    pieces = refs[:n_pieces]
    hat_ref, rstd_ref, low_ref, w_out, w_ref, sems = refs[n_pieces:]
    load_weight(table, pieces, w_out, w_ref, sems)
    w = w_ref[...].reshape(a_ref.shape[1], -1)
    v = x_ref[...].astype(f32) + contract(a_ref[...], w, 1, 0) + b_ref[...]
    hat, rstd = normalized(v)
    hat_ref[...] = hat
    rstd_ref[...] = jnp.broadcast_to(rstd, rstd_ref.shape)
    low_ref[...] = (hat * gain_ref[...] + bias_ref[...]).astype(bf16)


def out_norm(attended, w, b, x, gain, bias, wait=()):
    t = x.shape[0]
    vec = whole_spec((1, D))
    return call(
        functools.partial(out_norm_kernel, len(w.pieces)),
        "out_norm",
        (t // TILE,),
        [row_spec(TILE, D), vec, row_spec(TILE, D), vec, vec] + w.specs(),
        [row_spec(TILE, D), row_spec(TILE, LANES), row_spec(TILE, D), pl.BlockSpec(memory_space=pl.ANY)],
        [like((t, D), f32), like((t, LANES), f32), like((t, D), bf16), w.out_shape()],
        2 * t * D * D,
        12 * t * D,
        w.scratch(),
        table=w.table,
        wait=wait,
    )(w.table, attended, b, x, gain, bias, *w.pieces)


UP_TILE = 1024
CHUNK = 16


def gelu_pair(x):
    u = jnp.abs(x)
    e = jnp.exp(x * x * -0.5)
    t = 1.0 / (1.0 + (0.3275911 * 0.5**0.5) * u)
    poly = t * (
        0.254829592 * 0.5
        + t
        * (
            -0.284496736 * 0.5
            + t * (1.421413741 * 0.5 + t * (-1.453152027 * 0.5 + t * (1.061405429 * 0.5)))
        )
    )
    tail = poly * e
    phi = jnp.where(x < 0, tail, 1.0 - tail)
    return x * phi, phi + x * e * (2.0 * jnp.pi) ** -0.5


def up_kernel(n_pieces, first, table, h_ref, b_ref, *refs):
    pieces = refs[:n_pieces]
    act_ref, slope_ref, w_out, acc_ref, w_ref, sems = refs[-6:]
    n = w_ref.shape[-1]
    if first:
        pieces = [p.at[:, :, pl.ds(n, n)] for p in pieces]
        w_out = w_out.at[:, :, :, :, pl.ds(n, n)]
    else:
        pieces = [p.at[:, :, pl.ds(0, n)] for p in pieces]
        w_out = w_out.at[:, :, :, :, pl.ds(0, n)]
    load_weight(table, pieces, w_out, w_ref, sems)
    cols = pl.ds(pl.multiple_of(pl.program_id(0) * UP_TILE, LANES), UP_TILE)
    acc_ref[...] = contract(h_ref[...], w_ref[:, :, :, :, cols].reshape(-1, UP_TILE), 1, 0)
    bias = b_ref[...]

    def step(i, _):
        rows = pl.ds(pl.multiple_of(i * CHUNK, CHUNK), CHUNK)
        act, slope = gelu_pair(acc_ref[rows, :] + bias)
        act_ref[rows, :] = act.astype(bf16)
        slope_ref[rows, :] = slope.astype(bf16)
        return 0

    lax.fori_loop(0, h_ref.shape[0] // CHUNK, step, 0)


def up_gelu(hidden, w, b, before=None, wait=()):
    t, ff = hidden.shape[0], w.shape[-1]
    any_space = pl.BlockSpec(memory_space=pl.ANY)
    steps = ff // UP_TILE // 2
    first = 0 if before is None else steps
    before = [] if before is None else list(before)
    n_in = 3 + len(w.pieces)
    w_ref, sems = w.scratch()
    half = pltpu.VMEM(w.shape[:-1] + (ff // 2,), bf16)
    return call(
        functools.partial(up_kernel, len(w.pieces), first),
        "up_gelu",
        (steps,),
        [whole_spec((t, D)), pl.BlockSpec((1, UP_TILE), lambda i, _: (0, first + i))]
        + w.specs()
        + [any_space] * len(before),
        [pl.BlockSpec((t, UP_TILE), lambda i, _: (0, first + i))] * 2 + [any_space],
        [like((t, ff), bf16)] * 2 + [w.out_shape()],
        t * D * ff,
        2 * t * ff + D * ff,
        [pltpu.VMEM((t, UP_TILE), f32), half, sems],
        table=w.table,
        wait=wait,
        aliases={n_in + i: i for i in range(len(before))},
    )(w.table, hidden, b, *w.pieces, *before)


def head_masks(width):
    lane = lax.broadcasted_iota(jnp.int32, (1, width), 1)
    return [(lane >= start) & (lane < start + size) for start, size in head_slices()]


def head_sums(x):
    out = jnp.zeros_like(x)
    for mask in head_masks(x.shape[1]):
        total = jnp.sum(jnp.where(mask, x, 0.0), axis=1, keepdims=True)
        out = jnp.where(mask, total, out)
    return out


def down_norm_kernel(
    n_pieces, table, a_ref, b_ref, hat1_ref, gain1_ref, bias1_ref, gain_ref, bias_ref, proj_ref, *refs
):
    pieces = refs[:n_pieces]
    hat_ref, rstd_ref, low_ref, raw_ref, vec_ref, w_out, w_ref, sems = refs[n_pieces:]
    load_weight(table, pieces, w_out, w_ref, sems)
    hidden = hat1_ref[...] * gain1_ref[...] + bias1_ref[...]
    w = w_ref[...].reshape(a_ref.shape[1], -1)
    hat, rstd = normalized(hidden + contract(a_ref[...], w, 1, 0) + b_ref[...])
    hat_ref[...] = hat
    rstd_ref[...] = jnp.broadcast_to(rstd, rstd_ref.shape)
    low = (hat * gain_ref[...] + bias_ref[...]).astype(bf16)
    low_ref[...] = low
    raw = contract(low, proj_ref[...], 1, 0)
    raw_ref[...] = raw
    vec_ref[...] = (raw * lax.rsqrt(head_sums(raw * raw) + eps_vec)).astype(bf16)


def down_norm(act, w, b, hat1, gain1, bias1, gain, bias, proj, wait=()):
    t, ff = act.shape
    e = proj.shape[1]
    vec = whole_spec((1, D))
    return call(
        functools.partial(down_norm_kernel, len(w.pieces)),
        "down_norm",
        (t // TILE,),
        [row_spec(TILE, ff), vec, row_spec(TILE, D), vec, vec, vec, vec, whole_spec((D, e))]
        + w.specs(),
        [
            row_spec(TILE, D),
            row_spec(TILE, LANES),
            row_spec(TILE, D),
            row_spec(TILE, e),
            row_spec(TILE, e),
            pl.BlockSpec(memory_space=pl.ANY),
        ],
        [
            like((t, D), f32),
            like((t, LANES), f32),
            like((t, D), bf16),
            like((t, e), f32),
            like((t, e), bf16),
            w.out_shape(),
        ],
        2 * t * D * ff,
        20 * t * D,
        w.scratch(),
        table=w.table,
        wait=wait,
    )(w.table, act, b, hat1, gain1, bias1, gain, bias, proj, *w.pieces)


def head_back_kernel(
    g_ref, raw_ref, low_ref, proj_ref, hat_ref, rstd_ref, gain_ref,
    grad_ref, branch_ref, dproj_ref, sums_ref,
):
    g, raw = g_ref[...], raw_ref[...]
    scale = lax.rsqrt(head_sums(raw * raw) + eps_vec)
    y = raw * scale
    raw_grad = (scale * (g - y * head_sums(y * g))).astype(bf16)
    result_grad = contract(raw_grad, proj_ref[...], 1, 1)
    hat = hat_ref[...]
    grad = norm_back(result_grad, hat, rstd_ref[:, :1], gain_ref[...])
    branch = grad.astype(bf16)
    grad_ref[...] = grad
    branch_ref[...] = branch
    add_up(dproj_ref, contract(low_ref[...], raw_grad, 0, 0))
    add_up(
        sums_ref,
        jnp.concatenate(
            [
                column_sum(result_grad * hat),
                column_sum(result_grad),
                column_sum(branch.astype(f32)),
            ],
            axis=0,
        ),
    )


def head_back(g, raw, low, proj, hat, rstd, gain, wait=()):
    t, e = raw.shape
    return call(
        head_back_kernel,
        "head_back",
        (t // TILE,),
        [
            row_spec(TILE, e),
            row_spec(TILE, e),
            row_spec(TILE, D),
            whole_spec((D, e)),
            row_spec(TILE, D),
            row_spec(TILE, LANES),
            whole_spec((1, D)),
        ],
        [row_spec(TILE, D), row_spec(TILE, D), whole_spec((D, e)), whole_spec((3, D))],
        [like((t, D), f32), like((t, D), bf16), like((D, e), f32), like((3, D), f32)],
        4 * t * D * e,
        16 * t * D,
        wait=wait,
    )(g, raw, low, proj, hat, rstd, gain)


def act_back_kernel(g_ref, w_ref, slope_ref, o_ref, sum_ref):
    back = (contract(g_ref[...], w_ref[...], 1, 1) * slope_ref[...].astype(f32)).astype(bf16)
    o_ref[...] = back
    sum_ref[...] = column_sum(back.astype(f32))


def act_back(branch, w, slope, wait=()):
    t, ff = slope.shape
    return call(
        act_back_kernel,
        "act_back",
        (ff // UP_TILE,),
        [whole_spec((t, D)), row_spec(UP_TILE, D), col_spec(t, UP_TILE)],
        [col_spec(t, UP_TILE), col_spec(1, UP_TILE)],
        [like((t, ff), bf16), like((1, ff), f32)],
        2 * t * D * ff,
        4 * t * ff + 2 * D * ff,
        wait=wait,
    )(branch, w, slope)


def hidden_back_kernel(
    g_ref, w_ref, resid_ref, hat_ref, rstd_ref, gain_ref, wout_ref,
    grad_ref, out_ref, att_ref, sums_ref,
):
    hidden_grad = resid_ref[...] + contract(g_ref[...], w_ref[...], 1, 1)
    hat = hat_ref[...]
    grad = norm_back(hidden_grad, hat, rstd_ref[:, :1], gain_ref[...])
    low = grad.astype(bf16)
    grad_ref[...] = grad
    out_ref[...] = low
    att_ref[...] = contract(low, wout_ref[...], 1, 1).astype(bf16)
    add_up(
        sums_ref,
        jnp.concatenate(
            [column_sum(hidden_grad * hat), column_sum(hidden_grad), column_sum(low.astype(f32))],
            axis=0,
        ),
    )


def hidden_back(inner, w, resid, hat, rstd, gain, w_out, wait=()):
    t, ff = inner.shape
    return call(
        hidden_back_kernel,
        "hidden_back",
        (t // TILE,),
        [
            row_spec(TILE, ff),
            whole_spec((D, ff)),
            row_spec(TILE, D),
            row_spec(TILE, D),
            row_spec(TILE, LANES),
            whole_spec((1, D)),
            whole_spec((D, D)),
        ],
        [row_spec(TILE, D)] * 3 + [whole_spec((3, D))],
        [like((t, D), f32), like((t, D), bf16), like((t, D), bf16), like((3, D), f32)],
        2 * t * D * ff + 2 * t * D * D,
        2 * t * ff + 24 * t * D,
        wait=wait,
    )(inner, w, resid, hat, rstd, gain, w_out)


def input_back_kernel(groups, *refs):
    g_refs, (w_ref, resid_ref, o_ref) = refs[:groups], refs[groups:]
    total = resid_ref[...]
    for part in range(3):
        for i, g_ref in enumerate(g_refs):
            width = g_ref.shape[2]
            at = part * D + i * width
            total = total + contract(g_ref[part], w_ref[:, at : at + width], 1, 1)
    o_ref[...] = total


def input_back(grads, w, resid, wait=()):
    t = resid.shape[0]
    return call(
        functools.partial(input_back_kernel, len(grads)),
        "input_back",
        (t // TILE,),
        [pl.BlockSpec((3, TILE, g.shape[2]), lambda i: (0, i, 0)) for g in grads]
        + [whole_spec((D, 3 * D)), row_spec(TILE, D)],
        row_spec(TILE, D),
        like((t, D), f32),
        6 * t * D * D,
        20 * t * D,
        wait=wait,
    )(*grads, w, resid)


def unpack_kernel(n_devices, widths, p_ref, *o_refs):
    at = 0
    for width, o_ref in zip(widths, o_refs):
        n = width * n_devices
        x = p_ref[:, at : at + width]
        copies = (
            lax.broadcasted_iota(jnp.int32, (width, n), 1) % width
            == lax.broadcasted_iota(jnp.int32, (width, n), 0)
        ).astype(bf16)
        mine = (
            lax.broadcasted_iota(jnp.int32, (n_devices, n), 1) // width
            == lax.broadcasted_iota(jnp.int32, (n_devices, n), 0)
        )
        o_ref[...] = column_sum(jnp.where(mine, contract(x, copies, 1, 0), 0.0))
        at += width


def unpack(packed, widths, wait=()):
    n_devices = packed.shape[0]
    return call(
        functools.partial(unpack_kernel, n_devices, widths),
        "unpack",
        (1,),
        [whole_spec(packed.shape)],
        [whole_spec((1, w * n_devices)) for w in widths],
        [like((1, w * n_devices), f32) for w in widths],
        10**8,
        10**5,
        wait=wait,
    )(packed)


def pack_kernel(n_devices, widths, *refs):
    o_ref = refs[-1]
    o_ref[...] = jnp.zeros_like(o_ref)
    at = 0
    for width, ref in zip(widths, refs):
        n = width * n_devices
        mine = (
            lax.broadcasted_iota(jnp.int32, (n_devices, n), 1) // width
            == lax.broadcasted_iota(jnp.int32, (n_devices, n), 0)
        )
        copies = (
            lax.broadcasted_iota(jnp.int32, (n, width), 0) % width
            == lax.broadcasted_iota(jnp.int32, (n, width), 1)
        ).astype(f32)
        o_ref[:, at : at + width] = lax.dot_general(
            jnp.where(mine, ref[...], 0.0),
            copies,
            (((1,), (0,)), ((), ())),
            precision=highest,
            preferred_element_type=f32,
        )
        at += width


def pack(vectors, n_devices, wait=()):
    widths = [v.shape[1] // n_devices for v in vectors]
    total = sum(widths)
    total += -total % LANES
    return call(
        functools.partial(pack_kernel, n_devices, widths),
        "pack",
        (1,),
        [whole_spec(v.shape) for v in vectors],
        whole_spec((n_devices, total)),
        like((n_devices, total), f32),
        10**8,
        10**5,
        wait=wait,
    )(*vectors)


def weight_kernel(n_rows, n_z, offset, table, a_ref, b_ref, *refs):
    t, k = a_ref.shape
    block = k // n_rows
    r = block // (2 * n_z)
    turned = refs[-1]

    @pl.when(pl.program_id(0) == 0)
    def _():
        core = table[2 * n_rows]
        side = core if offset == 0 else 1 - core
        for piece in range(n_rows):
            mesh_row = table[offset + piece]
            cols = pl.ds(pl.multiple_of(mesh_row * block, block), block)
            x = a_ref[:, cols].T.reshape(n_z, 2, r, t)
            half = jnp.where(side == 0, x[:, 0], x[:, 1]).reshape(n_z * r, t)
            turned[piece * n_z * r : (piece + 1) * n_z * r, :] = half

    total = contract(turned[...], b_ref[...].reshape(b_ref.shape[-2:]), 1, 0)
    total = total.reshape(n_rows, n_z, r, total.shape[1])
    if offset:
        refs[0][...] = total.astype(refs[0].dtype)
    else:
        other, send_ref, keep_ref = refs[:3]
        total += other[...].astype(f32)
        send_ref[...] = total[n_rows // 2 :].astype(send_ref.dtype)
        keep_ref[...] = total[: n_rows // 2]


def weight_half(
    name, table, a, b, n_rows, n_z, tile, other=None, other_type=bf16, wait=()
):
    t, k = a.shape
    per_part = b.shape[-1] // tile
    n = b.shape[-1] * (b.shape[0] if b.ndim == 3 else 1)
    r = k // (n_rows * n_z * 2)
    if b.ndim == 3:
        b_spec = pl.BlockSpec((1, t, tile), lambda i, _: (i // per_part, 0, i % per_part))
    else:
        b_spec = col_spec(t, tile)

    def block(rows):
        return pl.BlockSpec((rows, n_z, r, tile), lambda i, _: (0, 0, 0, i))

    def shape(rows, dtype):
        return like((rows, n_z, r, n), dtype)

    own = other is not None
    return call(
        functools.partial(weight_kernel, n_rows, n_z, 0 if own else n_rows),
        name,
        (n // tile,),
        [whole_spec((t, k)), b_spec] + ([block(n_rows)] if own else []),
        [block(n_rows // 2)] * 2 if own else block(n_rows),
        [shape(n_rows // 2, bf16), shape(n_rows // 2, f32)] if own else shape(n_rows, other_type),
        t * k * n,
        2 * t * (k + n) + 3 * k * n,
        [pltpu.VMEM((k // 2, t), bf16)],
        table=table,
        wait=wait,
    )(table, a, b, *([other] if own else []))


WIN = -(-(DMOST + 15) // 32) * 32
NEG = -1e30


def contract(a, b, ca, cb):
    return lax.dot_general(a, b, (((ca,), (cb,)), ((), ())), preferred_element_type=f32)


def spans(len_ref, row_len):
    found = []
    start = jnp.int32(QPR * QLEN)
    for d in range(DPR):
        size = len_ref[d]
        base = pl.multiple_of(jnp.minimum((start // 16) * 16, row_len - WIN), 16)
        found.append((base, start - base, start - base + size))
        start = start + size
    return found


def head_pair(x):
    lane = lax.broadcasted_iota(jnp.int32, x.shape, 1)
    zero = jnp.zeros_like(x)
    return jnp.concatenate(
        [jnp.where(lane < HEAD_DIM, x, zero), jnp.where(lane < HEAD_DIM, zero, x)], axis=0
    )


def pair_heads(x):
    n = x.shape[0] // 2
    lane = lax.broadcasted_iota(jnp.int32, (n, x.shape[1]), 1)
    return jnp.where(lane < HEAD_DIM, x[:n], x[n:])


def inside(n, low, high, axis):
    shape = (n, 1) if axis == 0 else (1, n)
    at = lax.broadcasted_iota(jnp.int32, shape, axis)
    return (at >= low) & (at < high)


def attend(q, k, v, low, high):
    s = contract(head_pair(q), k, 1, 1)
    s = s + jnp.where(inside(k.shape[0], low, high, 1), 0.0, NEG)
    p = jnp.exp(s - jnp.max(s, axis=1, keepdims=True))
    total = jnp.sum(p, axis=1, keepdims=True)
    return pair_heads(contract(p.astype(bf16), v, 1, 0) / total)


def attention_kernel(len_ref, q_ref, k_ref, v_ref, o_ref):
    row_len = q_ref.shape[0]
    for base, low, high in spans(len_ref, row_len):
        w = pl.ds(base, WIN)
        o = attend(q_ref[w, :], k_ref[w, :], v_ref[w, :], low, high)
        keep = inside(WIN, low, high, 0)
        o_ref[w, :] = jnp.where(keep, o, o_ref[w, :].astype(f32)).astype(bf16)
    o_ref[:QLEN, :] = attend(q_ref[:QLEN, :], k_ref[:128, :], v_ref[:128, :], 0, QLEN).astype(bf16)


def qkv_specs(t):
    per_part = D // LANES
    return [
        pl.BlockSpec((t, LANES), lambda i, _, p=p: (0, p * per_part + i)) for p in range(3)
    ]


def attention(lengths, qkv, wait=()):
    t = qkv.shape[0]
    return call(
        attention_kernel,
        "attention",
        (HEADS // 2,),
        qkv_specs(t),
        col_spec(t, LANES),
        like((t, D), bf16),
        2 * 10**10,
        8 * t * D,
        table=lengths,
        wait=wait,
    )(lengths, qkv, qkv, qkv)


def attend_back(q, k, v, g, low, high):
    n = q.shape[0]
    g = jnp.where(inside(n, low, high, 0), g, jnp.zeros_like(g))
    qq = head_pair(q)
    gg = head_pair(g)
    st = contract(k, qq, 1, 1)
    st = st + jnp.where(inside(k.shape[0], low, high, 0), 0.0, NEG)
    p = jnp.exp(st - jnp.max(st, axis=0, keepdims=True))
    p = p * (1.0 / jnp.sum(p, axis=0, keepdims=True))
    dp = contract(v, gg, 1, 1)
    delta = jnp.sum(p * dp, axis=0, keepdims=True)
    ds = (p * (dp - delta)).astype(bf16)
    dv = contract(p.astype(bf16), gg, 1, 0)
    dk = contract(ds, qq, 1, 0)
    dq = contract(ds, k, 0, 0) * (HEAD_DIM**-0.5)
    return pair_heads(dq), dk, dv


def attention_back_kernel(len_ref, q_ref, k_ref, v_ref, g_ref, cos_ref, sin_ref, o_ref, sum_ref, *sums):
    row_len = q_ref.shape[0]
    for ref in sums:
        ref[...] = jnp.zeros_like(ref)
    parts = attend_back(
        q_ref[:QLEN, :], k_ref[:128, :], v_ref[:128, :], g_ref[:QLEN, :], 0, QLEN
    )
    for ref, x in zip(sums, parts):
        ref[: x.shape[0], :] = x
    for base, low, high in spans(len_ref, row_len):
        w = pl.ds(base, WIN)
        parts = attend_back(q_ref[w, :], k_ref[w, :], v_ref[w, :], g_ref[w, :], low, high)
        for ref, x in zip(sums, parts):
            ref[w, :] += x
    cosine, sine = cos_ref[...], sin_ref[...]
    for part in range(3):
        x = sums[part][...]
        if part < 2:
            x = x * cosine - swap_halves(x) * sine
        x = x.astype(bf16)
        o_ref[part] = x
        sum_ref[part] = column_sum(x.astype(f32))


def attention_back(lengths, qkv, g, cosine, sine, group, groups, wait=()):
    t = qkv.shape[0]
    table = whole_spec((t, LANES))
    pairs = HEADS // 2 // groups
    first = group * pairs
    per_part = D // LANES
    specs = [
        pl.BlockSpec((t, LANES), lambda i, _, p=p: (0, p * per_part + first + i)) for p in range(3)
    ]
    return call(
        attention_back_kernel,
        "attention_back",
        (pairs,),
        specs + [pl.BlockSpec((t, LANES), lambda i, _: (0, first + i)), table, table],
        [
            pl.BlockSpec((3, t, LANES), lambda i, _: (0, 0, i)),
            pl.BlockSpec((3, 1, LANES), lambda i, _: (0, 0, i)),
        ],
        [like((3, t, D // groups), bf16), like((3, 1, D // groups), f32)],
        5 * 10**10 // groups,
        14 * t * D // groups,
        [pltpu.VMEM((t, LANES), f32)] * 3,
        table=lengths,
        wait=wait,
    )(lengths, qkv, qkv, qkv, g, cosine, sine)


SCORE_TILE = 256


def doc_inside(doc_ref, d):
    return doc_ref[...] == d


def score_exps(docs, queries, mask):
    picked = jnp.where(mask, docs, jnp.zeros_like(docs))
    return picked, jnp.exp(contract(picked, queries, 1, 1) * score_scale)


def split_dot(hot, x):
    high = x.astype(bf16)
    rest = (x - high.astype(f32)).astype(bf16)
    return contract(hot, high, 1, 0) + contract(hot, rest, 1, 0)


def score_kernel(
    doc_ref, query_ref, id_ref, hot_ref, count_ref, pos_ref, sum_ref, score_ref, stat_ref
):
    docs = doc_ref[...]
    n_queries = score_ref.shape[2]
    live = lax.broadcasted_iota(jnp.int32, (8, n_queries), 0) < DPR
    for head, mask in enumerate(head_masks(docs.shape[1])):
        scores = jnp.zeros((8, n_queries), f32)
        for at in range(0, query_ref.shape[0], SCORE_TILE):
            _, e = score_exps(docs, query_ref[at : at + SCORE_TILE, :], mask)
            total = split_dot(hot_ref[...], e)
            sum_ref[head, :, at : at + SCORE_TILE] = total
            smooth = jnp.log(total) - count_ref[:, :1]
            query = lax.broadcasted_iota(jnp.int32, (SCORE_TILE, n_queries), 1)
            hot = (id_ref[at : at + SCORE_TILE, :] == query).astype(f32)
            scores += lax.dot_general(
                jnp.where(lax.broadcasted_iota(jnp.int32, smooth.shape, 0) < DPR, smooth, 0.0),
                hot,
                (((1,), (0,)), ((), ())),
                precision=highest,
                preferred_element_type=f32,
            )
        score_ref[head] = scores
        top = jnp.max(jnp.where(live, scores, NEG), axis=0, keepdims=True)
        den = column_sum(jnp.where(live, jnp.exp(scores - top), 0.0))
        pos = column_sum(jnp.where(live, scores * pos_ref[...], 0.0))
        stat_ref[head] = jnp.concatenate([top, den, pos], axis=0)


def score_grad_kernel(
    doc_ref, query_ref, id_ref, index_ref, sum_ref, score_ref, stat_ref, pos_ref, dq_ref, dd_ref
):
    docs = doc_ref[...]
    n_queries = score_ref.shape[2]
    dd_ref[...] = jnp.zeros_like(dd_ref)
    dq_ref[...] = jnp.zeros_like(dq_ref)
    index = index_ref[...]
    for head, mask in enumerate(head_masks(docs.shape[1])):
        stats = stat_ref[head]
        grad = jnp.exp(score_ref[head] - stats[0:1]) / stats[1:2] - pos_ref[...]
        for at in range(0, query_ref.shape[0], SCORE_TILE):
            queries = query_ref[at : at + SCORE_TILE, :]
            picked, e = score_exps(docs, queries, mask)
            query = lax.broadcasted_iota(jnp.int32, (n_queries, SCORE_TILE), 0)
            hot = (id_ref[:, at : at + SCORE_TILE] == query).astype(f32)
            spread = lax.dot_general(
                grad, hot, (((1,), (0,)), ((), ())), precision=highest, preferred_element_type=f32
            )
            coef = score_scale * spread / sum_ref[head, :, at : at + SCORE_TILE]
            wide = coef[0:1]
            for d in range(1, DPR):
                wide = jnp.where(index == d, coef[d : d + 1], wide)
            back = (e * wide).astype(bf16)
            dd_ref[...] += jnp.where(mask, contract(back, queries, 1, 0), 0.0)
            dq_ref[at : at + SCORE_TILE, :] += contract(back, picked, 0, 0)


def score_stats(docs, queries, ids, hot, counts, positive, wait=()):
    n, e = docs.shape
    n_tokens = queries.shape[0]
    n_queries = n_tokens // QLEN
    return call(
        score_kernel,
        "scores",
        (1,),
        [
            whole_spec((n, e)),
            whole_spec((n_tokens, e)),
            whole_spec((n_tokens, 1)),
            whole_spec((8, n)),
            whole_spec((8, LANES)),
            whole_spec((8, n_queries)),
        ],
        [
            whole_spec((3, 8, n_tokens)),
            whole_spec((3, 8, n_queries)),
            whole_spec((3, 3, n_queries)),
        ],
        [
            like((3, 8, n_tokens), f32),
            like((3, 8, n_queries), f32),
            like((3, 3, n_queries), f32),
        ],
        12 * n * n_tokens * e,
        10**6,
        wait=wait,
    )(docs, queries, ids[:, None], hot, counts, positive)


def score_grads(docs, queries, ids, index, sums, scores, stats, positive, wait=()):
    n, e = docs.shape
    n_tokens = queries.shape[0]
    n_queries = n_tokens // QLEN
    return call(
        score_grad_kernel,
        "score_grads",
        (1,),
        [
            whole_spec((n, e)),
            whole_spec((n_tokens, e)),
            whole_spec((1, n_tokens)),
            whole_spec((n, 1)),
            whole_spec((3, 8, n_tokens)),
            whole_spec((3, 8, n_queries)),
            whole_spec((3, 3, n_queries)),
            whole_spec((8, n_queries)),
        ],
        [whole_spec((n_tokens, e)), whole_spec((n, e))],
        [like((n_tokens, e), f32), like((n, e), f32)],
        24 * n * n_tokens * e,
        10**6,
        wait=wait,
    )(docs, queries, ids[None], index, sums, scores, stats, positive)


def layout(lengths, row_len, q_tokens):
    count = lengths.shape[0]
    before = jnp.arange(count)[:, None] <= jnp.arange(count)[None, :]
    ends = jnp.sum(jnp.where(before, lengths[:, None], 0), axis=0)
    offset = jnp.arange(row_len, dtype=jnp.int32) - q_tokens
    doc = jnp.sum((offset[:, None] >= ends[None, :]).astype(jnp.int32), axis=1)
    chosen = (doc[:, None] == jnp.arange(count, dtype=jnp.int32)[None, :]).astype(
        jnp.int32
    )
    begin = jnp.sum(chosen * (ends - lengths)[None, :], axis=1)
    is_query = offset < 0
    position = jnp.where(is_query, (offset + q_tokens) % QLEN, offset - begin)
    return position, doc


def combine_stats(one, two):
    top = jnp.maximum(one[:, 0], two[:, 0])
    den = one[:, 1] * jnp.exp(one[:, 0] - top) + two[:, 1] * jnp.exp(two[:, 0] - top)
    return jnp.stack([top, den, one[:, 2] + two[:, 2]], axis=1)


def reduce_stats(stats):
    n_rows, n_z, _, _ = sizes()
    moves = [[dict(swap_core=True)]]
    moves.append([dict(row_masks=(m, m)) for m in range(1, n_rows)])
    moves.append([dict(z_mask=m) for m in range(1, n_z)])
    for level in moves:
        parts = [exchange(stats, **move) for move in level]
        for part in parts:
            stats = combine_stats(stats, part)
    return stats


def on_device(
    tokens,
    lengths,
    positives,
    w_qkv,
    b_qkv,
    w_out,
    b_out,
    norm1_gain,
    norm1_bias,
    w_up,
    b_up,
    w_down,
    b_down,
    norm2_gain,
    norm2_bias,
    w_proj,
):
    n_rows, n_z, _, _ = sizes()
    n_devices = n_rows * n_z * 2
    row, z, core = place()
    device = (row * n_z + z) * 2 + core
    table = piece_table()
    row_len = tokens.shape[0]
    q_tokens = QPR * QLEN

    g_qkv, g_out, g_up, g_down = (Gather(w) for w in (w_qkv, w_out, w_up, w_down))
    g_qkv.all_z(())
    g_out.all_z([[g_qkv.held]])
    g_qkv.all_rows((), ())
    first, last = g_qkv.pieces[1:-1], g_qkv.pieces[-1]
    vectors = (b_qkv, b_out, norm1_gain, norm1_bias, b_up, b_down, norm2_gain, norm2_bias)
    widths = [v.shape[0] for v in vectors]
    packed = jnp.concatenate([after(v, g_qkv.held) for v in vectors])
    packed = jnp.pad(packed, (0, -packed.shape[0] % LANES)).reshape(-1, LANES)
    packed = gather_small(packed).reshape(n_devices, -1)
    full_bqkv, full_bout, gain_one, bias_one, full_bup, full_bdown, gain_two, bias_two = unpack(
        packed, widths
    )
    full_proj = gather_small(after(w_proj, *first)).reshape(-1, w_proj.shape[1])
    g_up.all_z([[g_out.held, *first]], [[last]])
    g_out.all_rows([first], [[last]])
    w_qkv_all = g_qkv.whole(table)

    own_lengths = lax.dynamic_index_in_dim(lengths, device, 0, keepdims=False)
    position, doc_index = layout(own_lengths, row_len, q_tokens)
    half = HEAD_DIM // 2
    frequency = 10000.0 ** (-jnp.arange(half, dtype=f32) / half)
    angles = position.astype(f32)[:, None] * frequency[None, :]
    cosine, sine = jnp.cos(angles), jnp.sin(angles)
    cosine = jnp.concatenate([cosine] * 4, axis=1)
    sine = jnp.concatenate([-sine, sine] * 2, axis=1)
    qkv, full_qkv = project_qkv(
        tokens, w_qkv_all, full_bqkv, cosine, sine, wait=[g_up.held, full_proj]
    )
    g_up.all_rows([[g_out.pieces[1], last], [qkv]], [[qkv]])
    w_out_all = g_out.whole(table, [[qkv]], [[qkv]])
    g_up_first = g_up.pieces[1:-1]
    attended = attention(own_lengths, qkv, wait=g_up_first)
    g_down.all_z([[g_up.held], [qkv]], [[qkv], [attended]])
    hat1, rstd1, hidden_low, full_out = out_norm(
        attended, w_out_all, full_bout, tokens, gain_one, bias_one, wait=[g_down.held]
    )

    w_up_all = g_up.whole(table, [[qkv], [attended]], [[attended]])
    part = up_gelu(hidden_low, w_up_all, full_bup)
    g_down.all_rows([[attended], [part[0]]], [[part[0]]])
    act, slope, full_up = up_gelu(hidden_low, w_up_all, full_bup, part, wait=g_down.pieces[1:-1])
    w_down_all = g_down.whole(table, [[part[0]], [act]], [[act]])
    hat2, rstd2, result_low, raw, vecs, full_down = down_norm(
        act, w_down_all, full_bdown, hat1, gain_one, bias_one, gain_two, bias_two, full_proj
    )
    full_qkv, full_out, full_up, full_down = (
        w.reshape(-1, w.shape[-1]) for w in (full_qkv, full_out, full_up, full_down)
    )

    query_all = gather_relative(vecs[:q_tokens]).reshape(n_devices * q_tokens, -1)
    query_ids = relative_order()[:, None] * QPR + jnp.arange(q_tokens, dtype=jnp.int32)[None, :] // QLEN
    query_ids = query_ids.reshape(-1)
    docs = vecs[q_tokens:]
    doc_index = doc_index[q_tokens:]
    slots = jnp.arange(8, dtype=jnp.int32)
    hot = (slots[:, None] == doc_index[None, :]).astype(bf16)
    counts = jnp.broadcast_to(
        jnp.log(jnp.pad(own_lengths, (0, 8 - DPR), constant_values=1).astype(f32))[:, None],
        (8, LANES),
    )
    positive = ((positives[None, :] == device * DPR + slots[:, None]) & (slots < DPR)[:, None]).astype(f32)
    sums, doc_scores, stats = score_stats(docs, query_all, query_ids, hot, counts, positive)
    stats = reduce_stats(stats)
    query_count = n_z * 2 * QPR
    losses = lax.dynamic_slice_in_dim(
        stats[:, 0] + jnp.log(stats[:, 1]) - stats[:, 2], row * query_count, query_count, 1
    )
    query_grads, doc_grads = score_grads(
        docs, query_all, query_ids, doc_index[:, None], sums, doc_scores, stats, positive
    )
    query_grad = scatter_relative(query_grads.reshape(2, n_rows, n_z, q_tokens, -1), bf16)
    vector_grad = jnp.concatenate([query_grad, doc_grads], axis=0)

    resid_two_grad, branch_grad, grad_proj, sums2 = head_back(
        vector_grad, raw, result_low, full_proj, hat2, rstd2, gain_two
    )
    def sib_half(name, a, b, tile, dtype=bf16, wait=()):
        return weight_half(
            name + "_sib", table, a, b, n_rows, n_z, tile, other_type=dtype, wait=wait
        )

    def own_half(name, a, b, tile, sib, wide=False, wait=()):
        other = exchange(sib, swap_core=True)
        return Scatter(*weight_half(name, table, a, b, n_rows, n_z, tile, other, wait=wait), wide)

    def attention_part(i, wait):
        return attention_back(own_lengths, qkv, attended_grad, cosine, sine, i, 2, wait=wait)

    down_sib = sib_half("grad_down", act, branch_grad, 512)
    inner_grad, grad_bup = act_back(branch_grad, full_down, slope, wait=[down_sib])
    down = own_half("grad_down", act, branch_grad, 512, down_sib, True, wait=[grad_bup])
    up_sib = sib_half("grad_up", hidden_low, inner_grad, 1024, f32, wait=[down.send])
    resid_one_grad, out_grad, attended_grad, sums1 = hidden_back(
        inner_grad, full_up, resid_two_grad, hat1, rstd1, gain_one, full_out, wait=[up_sib]
    )
    d2 = down.step(sums1)
    up = own_half("grad_up", hidden_low, inner_grad, 1024, up_sib, wait=[sums1, d2])
    d3 = down.step(up.send)
    grad_a, sums_a = attention_part(0, [up.send, d3])
    sib_a = sib_half("grad_qkv", tokens, grad_a, 512)
    d4 = down.step(sums_a)
    u2 = up.step(sums_a)
    out_sib = sib_half("grad_out", attended, out_grad, 1024, wait=[sib_a])
    grad_b, sums_b = attention_part(1, [out_sib, d4, u2])
    qkv_a = own_half("grad_qkv", tokens, grad_a, 512, sib_a, wait=[sums_b])
    sum_down = down.finish(sums_b)
    u3 = up.step(sums_b)
    out = own_half("grad_out", attended, out_grad, 1024, out_sib, True, wait=[qkv_a.send, u3])
    sib_b = sib_half("grad_qkv", tokens, grad_b, 512, wait=[out.send])
    u4 = up.step(sib_b)
    a2 = qkv_a.step(sib_b)
    qkv_b = own_half("grad_qkv", tokens, grad_b, 512, sib_b, wait=[u4, a2])
    a3 = qkv_a.step(qkv_b.send)
    o2 = out.step(qkv_b.send)
    input_grad = input_back([grad_a, grad_b], full_qkv, resid_one_grad, wait=[qkv_b.send, a3, o2])
    sum_up = up.finish(input_grad)
    grads = [sums_a[i] if j == 0 else sums_b[i] for i in range(3) for j in range(2)]
    grad_bqkv = jnp.concatenate(grads, axis=1)
    small = pack(
        [grad_bqkv, sums1[2:3], sums1[0:1], sums1[1:2], grad_bup, sums2[2:3], sums2[0:1], sums2[1:2]],
        n_devices,
        wait=[input_grad],
    )
    small = scatter_small(small.reshape(n_devices, -1, LANES), f32).reshape(-1)
    sum_proj = scatter_small(
        after(grad_proj, input_grad).reshape(n_devices, -1, grad_proj.shape[1]), bf16
    )
    sum_out = out.finish()
    sum_a, sum_b = qkv_a.finish(), qkv_b.finish()
    width = sum_a.shape[1] // 3
    sum_qkv = jnp.concatenate(
        [x[:, i * width : (i + 1) * width] for i in range(3) for x in (sum_a, sum_b)], axis=1
    )
    pieces = []
    at = 0
    for width in widths:
        pieces.append(small[at : at + width])
        at += width
    s_bqkv, s_bout, s_gain1, s_bias1, s_bup, s_bdown, s_gain2, s_bias2 = pieces
    return (
        losses,
        result_low,
        input_grad,
        sum_qkv,
        s_bqkv,
        sum_out,
        s_bout,
        s_gain1,
        s_bias1,
        sum_up,
        s_bup,
        sum_down,
        s_bdown,
        s_gain2,
        s_bias2,
        sum_proj,
    )


def solution(mesh):
    shard = P(AXES, None)
    vec = P(AXES)
    in_specs = (
        shard,
        P(),
        P(),
        shard,
        vec,
        shard,
        vec,
        vec,
        vec,
        shard,
        vec,
        shard,
        vec,
        vec,
        vec,
        shard,
    )
    out_specs = (P(None, "row"), shard) + (shard,) + in_specs[3:]
    return jax.shard_map(
        on_device, mesh=mesh, in_specs=in_specs, out_specs=out_specs, check_vma=False
    )
```

```python
import functools

import jax
import jax.numpy as jnp
from jax import lax
from jax.experimental import pallas as pl
from jax.experimental.pallas import tpu as pltpu
from jax.sharding import PartitionSpec as P

D = 1024
HEADS = 16
HEAD_DIM = 64
PROJ_A = 128
PROJ_B = 96
PROJ_C = 64
QLEN = 32
DPR = 4
QPR = 1
DMOST = 330

AXES = ("row", "col")
highest = lax.Precision.HIGHEST
eps_norm = 1e-05
eps_vec = 1e-06
score_scale = 16.0
f32 = jnp.float32
bf16 = jnp.bfloat16


def sizes():
    n_rows = lax.axis_size("row")
    n_z = lax.axis_size("col") // 2
    return n_rows, n_z, n_rows.bit_length() - 1, n_z.bit_length() - 1


def after(value, *before):
    return lax.optimization_barrier((value,) + before)[0] if before else value


def place():
    col = lax.axis_index("col")
    return lax.axis_index("row"), col // 2, col % 2


def exchange(value, row_masks=(0, 0), z_mask=0, swap_core=False):
    n_rows, n_z, _, _ = sizes()
    pairs = []
    for r in range(n_rows):
        for z in range(n_z):
            for c in range(2):
                here = (r * n_z + z) * 2 + c
                there = ((r ^ row_masks[c]) * n_z + (z ^ z_mask)) * 2 + (
                    1 - c if swap_core else c
                )
                pairs.append((here, there))
    return lax.ppermute(value, AXES, pairs)


def stage_bit(core, stage, row_bits):
    return (stage + core) % row_bits


def stage_masks(stage):
    _, _, row_bits, _ = sizes()
    return tuple(1 << stage_bit(c, stage, row_bits) for c in range(2))


def piece_mask(core, piece):
    _, _, row_bits, _ = sizes()
    return sum(
        1 << stage_bit(core, j, row_bits) for j in range(row_bits) if piece >> j & 1
    )


def ordered(bit, own, other, axis):
    return jnp.stack([jnp.where(bit == 0, own, other), jnp.where(bit == 0, other, own)], axis)


def transfer(value, start=(), use=(), **move):
    return after(exchange(after(value, *start), **move), *use)


class Gather:
    def __init__(self, shard):
        self.held, self.count, self.shard, self.received = shard, 0, shard, []

    def along_z(self, start=(), use=()):
        _, n_z, _, z_bits = sizes()
        _, z, _ = place()
        bit = z_bits - 1 - self.count
        other = transfer(self.held, start, use, z_mask=1 << bit)
        self.received.append(other)
        self.held = ordered(z >> bit & 1, self.held, other, self.count)
        self.count += 1
        if self.count == z_bits:
            self.pieces = [self.held.reshape((n_z,) + self.shard.shape)]

    def all_z(self, *bounds):
        _, _, _, z_bits = sizes()
        for i in range(z_bits):
            self.along_z(*bounds[min(i, len(bounds) - 1)])

    def own_rows(self, start=(), use=()):
        _, _, row_bits, _ = sizes()
        self.own = [
            transfer(self.pieces[0], start, use, row_masks=stage_masks(stage))
            for stage in range(row_bits)
        ]
        self.pieces = self.pieces + self.own

    def other_rows(self, start=(), use=()):
        _, _, row_bits, _ = sizes()
        pieces = [self.pieces[0], self.own[0]]
        for stage in range(1, row_bits):
            pieces = pieces + [self.own[stage]] + [
                transfer(p, start, use, row_masks=stage_masks(stage)) for p in pieces[1:]
            ]
        self.pieces = pieces

    def all_rows(self, own, other):
        self.own_rows(*own)
        self.other_rows(*other)

    def whole(self, table, early=(), late=()):
        last = len(self.pieces) - 1
        sibs = [
            transfer(p, *(late if i == last else early), swap_core=True)
            for i, p in enumerate(self.pieces)
        ]
        return Weight(table, self.pieces + sibs)


def piece_table():
    n_rows, _, _, _ = sizes()
    row, _, core = place()
    tables = [
        jnp.array([piece_mask(c, k) for k in range(n_rows)], jnp.int32) for c in range(2)
    ]
    own = row ^ jnp.where(core == 0, tables[0], tables[1])
    sib = row ^ jnp.where(core == 0, tables[1], tables[0])
    steps = jnp.arange(n_rows)

    def piece_of(rows):
        return jnp.sum(jnp.where(rows[None, :] == steps[:, None], steps[None, :], 0), axis=1)

    return jnp.concatenate([own, sib, core[None], piece_of(own), piece_of(sib)]).astype(jnp.int32)


class Weight:
    def __init__(self, table, pieces, start=0, size=None):
        self.table, self.pieces = table, pieces
        self.start, self.size = start, size or pieces[0].shape[2]

    def columns(self, start, size):
        return Weight(self.table, self.pieces, self.start + start, size)

    @property
    def shape(self):
        n_rows, n_z, _, _ = sizes()
        return (n_rows, n_z, 2, self.pieces[0].shape[1], self.size)

    def specs(self):
        return [pl.BlockSpec(memory_space=pl.ANY)] * len(self.pieces)

    def scratch(self):
        return [
            pltpu.VMEM(self.shape, self.pieces[0].dtype),
            pltpu.SemaphoreType.DMA((len(self.pieces) + 1,)),
        ]

    def out_shape(self):
        return jax.ShapeDtypeStruct(self.shape, self.pieces[0].dtype)

    def load(self, table, pieces, out_ref, w_ref, sems):
        n_rows = len(pieces) // 2
        core = table[2 * n_rows]
        out = pltpu.make_async_copy(w_ref, out_ref, sems.at[2 * n_rows])
        if self.size != pieces[0].shape[2]:
            pieces = [p.at[:, :, pl.ds(self.start, self.size)] for p in pieces]

        @pl.when(pl.program_id(0) == 0)
        def _():
            copies = [
                pltpu.make_async_copy(
                    piece,
                    w_ref.at[table[i], :, core if i < n_rows else 1 - core],
                    sems.at[i],
                )
                for i, piece in enumerate(pieces)
            ]
            for c in copies:
                c.start()
            for c in copies:
                c.wait()
            out.start()

        @pl.when(pl.program_id(0) == pl.num_programs(0) - 1)
        def _():
            out.wait()


def gather_small(shard, uses=()):
    n_rows, n_z, row_bits, z_bits = sizes()
    row, z, core = place()
    uses = list(uses)

    def arrive(**move):
        other = exchange(held, **move)
        return after(other, uses.pop(0)) if uses else other

    held = shard
    for count, bit in enumerate(reversed(range(z_bits))):
        held = ordered(z >> bit & 1, held, arrive(z_mask=1 << bit), count)
    for count, bit in enumerate(reversed(range(row_bits))):
        held = ordered(row >> bit & 1, held, arrive(row_masks=(1 << bit, 1 << bit)), count)
    held = ordered(core, held, arrive(swap_core=True), row_bits + z_bits)
    return held.reshape((n_rows * n_z * 2,) + shard.shape)


def scatter_small(blocks, dtype):
    n_rows, n_z, row_bits, z_bits = sizes()
    row, z, core = place()
    held = blocks.reshape((2,) * (row_bits + z_bits + 1) + blocks.shape[1:])

    def halve(held, axis, bit, **move):
        send = lax.dynamic_index_in_dim(held, 1 - bit, axis, keepdims=False)
        keep = lax.dynamic_index_in_dim(held, bit, axis, keepdims=False)
        return keep.astype(f32) + exchange(send.astype(dtype), **move).astype(f32)

    held = halve(held, row_bits + z_bits, core, swap_core=True)
    for bit in range(row_bits):
        held = halve(held, row_bits - 1 - bit, row >> bit & 1, row_masks=(1 << bit, 1 << bit))
    for bit in range(z_bits):
        held = halve(held, z_bits - 1 - bit, z >> bit & 1, z_mask=1 << bit)
    return held


def gather_relative(block):
    n_rows, n_z, _, _ = sizes()
    held = jnp.stack([block] + [exchange(block, z_mask=m) for m in range(1, n_z)])
    held = jnp.stack([held] + [exchange(held, row_masks=(m, m)) for m in range(1, n_rows)])
    return jnp.stack([held, exchange(held, swap_core=True)])


def scatter_relative(blocks, dtype, use=()):
    n_rows, n_z, _, _ = sizes()

    def step(held, count, move, use=()):
        parts = [after(exchange(held[m].astype(dtype), **move(m)), *use) for m in range(1, count)]
        total = held[0]
        for part in parts:
            total = total + part.astype(f32)
        return total

    held = step(blocks, 2, lambda m: dict(swap_core=True), use)
    held = step(held, n_rows, lambda m: dict(row_masks=(m, m)))
    return step(held, n_z, lambda m: dict(z_mask=m))


def relative_order():
    n_rows, n_z, _, _ = sizes()
    row, z, core = place()
    at = jnp.arange(n_rows * n_z * 2)
    there_core = core ^ at // (n_rows * n_z)
    there_row = row ^ at // n_z % n_rows
    return ((there_row * n_z + (z ^ at % n_z)) * 2 + there_core).astype(jnp.int32)


class Scatter:
    def __init__(self, send, keep, wide=False):
        _, _, row_bits, z_bits = sizes()
        flat = lambda x: x.reshape((-1,) + x.shape[-2:])
        self.send, self.keep = flat(send), flat(keep)
        self.stages = [("row", j) for j in reversed(range(row_bits))]
        self.stages += [("z", b) for b in range(z_bits)]
        self.wide = self.stages[-1] if wide else None

    def receive(self):
        kind, at = self.stages.pop(0)
        move = dict(row_masks=stage_masks(at)) if kind == "row" else dict(z_mask=1 << at)
        return exchange(self.send, **move)

    def step(self, *use):
        _, z, _ = place()
        parts = (self.keep, after(self.receive(), *use))
        if not self.stages:
            return (parts[0] + parts[1].astype(f32))[0]
        kind, at = self.stages[0]
        half = self.keep.shape[0] // 2
        if kind == "row":
            pick = lambda x, other: x[half:] if other else x[:half]
        else:
            mine = z >> at & 1
            parts = tuple(x.reshape((half, 2) + x.shape[1:]) for x in parts)
            pick = lambda x, other: lax.dynamic_index_in_dim(
                x, 1 - mine if other else mine, 1, keepdims=False
            )
        total = lambda other: pick(parts[0], other) + pick(parts[1], other).astype(f32)
        self.send, self.keep = total(True), total(False)
        if self.stages[0] != self.wide:
            self.send = self.send.astype(bf16)
        return self.send

    def merge(self, other):
        self.send = jnp.concatenate([self.send, other.send], axis=-1)
        self.keep = jnp.concatenate([self.keep, other.keep], axis=-1)
        return self

    def finish(self, *use):
        while self.stages:
            out = self.step(*use)
        return out


def head_slices():
    return ((0, PROJ_A), (PROJ_A, PROJ_B), (PROJ_A + PROJ_B, PROJ_C))


LANES = 128


def whole_spec(shape):
    return pl.BlockSpec(
        shape, lambda *_: (0,) * len(shape), pipeline_mode=pl.Buffered(buffer_count=1)
    )


def row_spec(rows, width):
    return pl.BlockSpec((rows, width), lambda i, *_: (i, 0))


def col_spec(rows, width):
    return pl.BlockSpec((rows, width), lambda i, *_: (0, i))


def like(shape, dtype):
    return jax.ShapeDtypeStruct(shape, dtype)


def call(
    kernel, name, grid, in_specs, out_specs, out_shape, flops, moved, scratch=(), table=None, wait=(), aliases=None
):
    first = len(in_specs) + (0 if table is None else 1)
    in_specs = list(in_specs) + [pl.BlockSpec(memory_space=pl.ANY)] * len(wait)

    def body(*refs):
        kernel(*refs[:first], *refs[first + len(wait) :])

    run = pl.pallas_call(
        body,
        grid_spec=pltpu.PrefetchScalarGridSpec(
            num_scalar_prefetch=0 if table is None else 1,
            grid=grid,
            in_specs=in_specs,
            out_specs=out_specs,
            scratch_shapes=list(scratch),
        ),
        out_shape=out_shape,
        input_output_aliases=aliases or {},
        compiler_params=pltpu.CompilerParams(vmem_limit_bytes=56 << 20),
        cost_estimate=pl.CostEstimate(
            flops=int(flops), bytes_accessed=int(moved), transcendentals=0
        ),
        name=name,
    )
    return lambda *operands: run(*operands, *wait)


def swap_halves(x):
    lane = lax.broadcasted_iota(jnp.int32, x.shape, 1)
    half = HEAD_DIM // 2
    return jnp.where(
        lane % HEAD_DIM < half, pltpu.roll(x, LANES - half, 1), pltpu.roll(x, half, 1)
    )


QKV_TILE = 1024


def qkv_kernel(weight, table, x_ref, b_ref, cos_ref, sin_ref, *refs):
    pieces, (o_ref, w_out, w_ref, sems) = refs[:-4], refs[-4:]
    weight.load(table, pieces, w_out, w_ref, sems)
    tile = pl.program_id(0)
    per_part = D // QKV_TILE
    cols = pl.ds(pl.multiple_of(tile * QKV_TILE, LANES), QKV_TILE)
    w = w_ref[:, :, :, :, cols].reshape(x_ref.shape[1], QKV_TILE)
    bias = b_ref[...]

    @pl.when(tile < 2 * per_part)
    def _():
        scale = jnp.where(tile < per_part, HEAD_DIM**-0.5, 1.0)
        for row in range(0, x_ref.shape[0], TILE):
            rows = slice(row, row + TILE)
            acc = contract(x_ref[rows, :], w, 1, 0) + bias
            cosine = cos_ref[rows, :] * scale
            sine = sin_ref[rows, :] * scale
            for j in range(QKV_TILE // LANES):
                at = slice(j * LANES, (j + 1) * LANES)
                a = acc[:, at]
                o_ref[rows, at] = (a * cosine + swap_halves(a) * sine).astype(bf16)

    @pl.when(tile >= 2 * per_part)
    def _():
        for row in range(0, x_ref.shape[0], TILE):
            rows = slice(row, row + TILE)
            o_ref[rows, :] = (contract(x_ref[rows, :], w, 1, 0) + bias).astype(bf16)


def project_qkv(x, w, b, cosine, sine, wait=()):
    t = x.shape[0]
    any_out = pl.BlockSpec(memory_space=pl.ANY)
    return call(
        functools.partial(qkv_kernel, w),
        "project_qkv",
        (3 * D // QKV_TILE,),
        [
            whole_spec((t, D)),
            pl.BlockSpec((1, QKV_TILE), lambda i, _: (0, i)),
            whole_spec((t, LANES)),
            whole_spec((t, LANES)),
        ]
        + w.specs(),
        [col_spec(t, QKV_TILE), any_out],
        [like((t, 3 * D), bf16), w.out_shape()],
        6 * t * D * D,
        20 * t * D,
        w.scratch(),
        table=w.table,
        wait=wait,
    )(w.table, x, b, cosine, sine, *w.pieces)


TILE = 256


def normalized(v):
    mean = jnp.mean(v, axis=1, keepdims=True)
    centered = v - mean
    rstd = lax.rsqrt(jnp.mean(centered * centered, axis=1, keepdims=True) + eps_norm)
    return centered * rstd, rstd


def norm_back(g, hat, rstd, gain):
    y = g * gain
    return rstd * (
        y - jnp.mean(y, axis=1, keepdims=True) - hat * jnp.mean(y * hat, axis=1, keepdims=True)
    )


def add_up(ref, value):
    @pl.when(pl.program_id(0) == 0)
    def _():
        ref[...] = jnp.zeros_like(ref)

    ref[...] += value


def column_sum(x):
    return jnp.sum(x, axis=0, keepdims=True)


def out_norm_kernel(weight, table, a_ref, b_ref, x_ref, gain_ref, bias_ref, *refs):
    hat_ref, rstd_ref, low_ref, w_out, w_ref, sems = refs[-6:]
    weight.load(table, refs[:-6], w_out, w_ref, sems)
    w = w_ref[...].reshape(a_ref.shape[1], -1)
    v = x_ref[...].astype(f32) + contract(a_ref[...], w, 1, 0) + b_ref[...]
    hat, rstd = normalized(v)
    hat_ref[...] = hat
    rstd_ref[...] = jnp.broadcast_to(rstd, rstd_ref.shape)
    low_ref[...] = (hat * gain_ref[...] + bias_ref[...]).astype(bf16)


def out_norm(attended, w, b, x, gain, bias, wait=()):
    t = x.shape[0]
    vec = whole_spec((1, D))
    return call(
        functools.partial(out_norm_kernel, w),
        "out_norm",
        (t // TILE,),
        [row_spec(TILE, D), vec, row_spec(TILE, D), vec, vec] + w.specs(),
        [row_spec(TILE, D), row_spec(TILE, LANES), row_spec(TILE, D), pl.BlockSpec(memory_space=pl.ANY)],
        [like((t, D), f32), like((t, LANES), f32), like((t, D), bf16), w.out_shape()],
        2 * t * D * D,
        12 * t * D,
        w.scratch(),
        table=w.table,
        wait=wait,
    )(w.table, attended, b, x, gain, bias, *w.pieces)


UP_TILE = 1024
CHUNK = 32


def gelu_pair(x):
    phi = 0.5 + 0.5 * lax.erf(x * 0.5**0.5)
    return x * phi, phi + x * jnp.exp(x * x * -0.5) * (2.0 * jnp.pi) ** -0.5


def up_kernel(weight, table, h_ref, b_ref, *refs):
    act_ref, slope_ref, w_out, acc_ref, w_ref, sems = refs[-6:]
    out = w_out.at[:, :, :, :, pl.ds(weight.start, weight.size)]
    weight.load(table, refs[: len(weight.pieces)], out, w_ref, sems)
    cols = pl.ds(pl.multiple_of(pl.program_id(0) * UP_TILE, LANES), UP_TILE)
    acc_ref[...] = contract(h_ref[...], w_ref[:, :, :, :, cols].reshape(-1, UP_TILE), 1, 0)
    bias = b_ref[...]

    def step(i, _):
        rows = pl.ds(pl.multiple_of(i * CHUNK, CHUNK), CHUNK)
        act, slope = gelu_pair(acc_ref[rows, :] + bias)
        act_ref[rows, :] = act.astype(bf16)
        slope_ref[rows, :] = slope.astype(bf16)
        return 0

    lax.fori_loop(0, h_ref.shape[0] // CHUNK, step, 0)


def up_gelu(hidden, w, b, before=None, wait=()):
    t, ff = hidden.shape[0], w.size
    any_space = pl.BlockSpec(memory_space=pl.ANY)
    steps = ff // UP_TILE // 2
    first = 0 if before is None else steps
    before = [] if before is None else list(before)
    n_in = 3 + len(w.pieces)
    half = w.columns(first * UP_TILE, ff // 2)
    return call(
        functools.partial(up_kernel, half),
        "up_gelu",
        (steps,),
        [whole_spec((t, D)), pl.BlockSpec((1, UP_TILE), lambda i, _: (0, first + i))]
        + w.specs()
        + [any_space] * len(before),
        [pl.BlockSpec((t, UP_TILE), lambda i, _: (0, first + i))] * 2 + [any_space],
        [like((t, ff), bf16)] * 2 + [w.out_shape()],
        t * D * ff,
        2 * t * ff + D * ff,
        [pltpu.VMEM((t, UP_TILE), f32)] + half.scratch(),
        table=w.table,
        wait=wait,
        aliases={n_in + i: i for i in range(len(before))},
    )(w.table, hidden, b, *w.pieces, *before)


def head_masks(width):
    lane = lax.broadcasted_iota(jnp.int32, (1, width), 1)
    return [(lane >= start) & (lane < start + size) for start, size in head_slices()]


def head_lanes():
    for start, size in head_slices():
        low = start // LANES * LANES
        high = -(-(start + size) // LANES) * LANES
        lane = lax.broadcasted_iota(jnp.int32, (1, high - low), 1) + low
        yield slice(low, high), (lane >= start) & (lane < start + size)


def head_sums(x):
    out = jnp.zeros_like(x)
    for mask in head_masks(x.shape[1]):
        total = jnp.sum(jnp.where(mask, x, 0.0), axis=1, keepdims=True)
        out = jnp.where(mask, total, out)
    return out


def down_norm_kernel(
    weight, proj, table, a_ref, b_ref, hat1_ref, gain1_ref, bias1_ref, gain_ref, bias_ref, *refs
):
    n = len(weight.pieces)
    hat_ref, rstd_ref, low_ref, raw_ref, vec_ref = refs[-11:-6]
    w_out, p_out, w_ref, w_sems, p_ref, p_sems = refs[-6:]
    proj.load(table, refs[n : 2 * n], p_out, p_ref, p_sems)
    weight.load(table, refs[:n], w_out, w_ref, w_sems)
    w = w_ref[...].reshape(a_ref.shape[1], -1)
    p = p_ref[...].reshape(w.shape[1], -1)
    for row in range(0, a_ref.shape[0], TILE):
        rows = slice(row, row + TILE)
        hidden = hat1_ref[rows, :] * gain1_ref[...] + bias1_ref[...]
        hat, rstd = normalized(hidden + contract(a_ref[rows, :], w, 1, 0) + b_ref[...])
        hat_ref[rows, :] = hat
        rstd_ref[rows, :] = jnp.broadcast_to(rstd, (TILE, LANES))
        low = (hat * gain_ref[...] + bias_ref[...]).astype(bf16)
        low_ref[rows, :] = low
        raw = contract(low, p, 1, 0)
        raw_ref[rows, :] = raw
        vec_ref[rows, :] = (raw * lax.rsqrt(head_sums(raw * raw) + eps_vec)).astype(bf16)


def down_norm(act, w, b, hat1, gain1, bias1, gain, bias, proj, wait=()):
    t, ff = act.shape
    e = proj.size
    vec = whole_spec((1, D))
    any_space = pl.BlockSpec(memory_space=pl.ANY)
    return call(
        functools.partial(down_norm_kernel, w, proj),
        "down_norm",
        (t // TILE,),
        [row_spec(TILE, ff), vec, row_spec(TILE, D), vec, vec, vec, vec] + w.specs() + proj.specs(),
        [
            row_spec(TILE, D),
            row_spec(TILE, LANES),
            row_spec(TILE, D),
            row_spec(TILE, e),
            row_spec(TILE, e),
            any_space,
            any_space,
        ],
        [
            like((t, D), f32),
            like((t, LANES), f32),
            like((t, D), bf16),
            like((t, e), f32),
            like((t, e), bf16),
            w.out_shape(),
            proj.out_shape(),
        ],
        2 * t * D * ff,
        20 * t * D,
        w.scratch() + proj.scratch(),
        table=w.table,
        wait=wait,
    )(w.table, act, b, hat1, gain1, bias1, gain, bias, *w.pieces, *proj.pieces)


def head_back_kernel(
    has_query, g_ref, raw_ref, proj_ref, hat_ref, rstd_ref, gain_ref, *refs
):
    grad_ref, branch_ref, raw_out, sums_ref = refs[-4:]
    g, raw = g_ref[...], raw_ref[...]
    if has_query:
        q = refs[0][...]
        g = g + jnp.concatenate([q, jnp.zeros((g.shape[0] - q.shape[0], q.shape[1]), f32)], axis=0)
    scale = lax.rsqrt(head_sums(raw * raw) + eps_vec)
    y = raw * scale
    raw_grad = (scale * (g - y * head_sums(y * g))).astype(bf16)
    result_grad = contract(raw_grad, proj_ref[...], 1, 1)
    hat = hat_ref[...]
    grad = norm_back(result_grad, hat, rstd_ref[:, :1], gain_ref[...])
    branch = grad.astype(bf16)
    grad_ref[...] = grad
    branch_ref[...] = branch
    raw_out[...] = raw_grad
    add_up(
        sums_ref,
        jnp.concatenate(
            [
                column_sum(result_grad * hat),
                column_sum(result_grad),
                column_sum(branch.astype(f32)),
            ],
            axis=0,
        ),
    )


def head_back(g, raw, proj, hat, rstd, gain, query=None, before=(), wait=()):
    t, e = raw.shape
    first, steps = (1, t // TILE - 1) if query is None else (0, 1)
    extra = [] if query is None else [query]
    rows = lambda width: pl.BlockSpec((TILE, width), lambda i, *_: (first + i, 0))
    return call(
        functools.partial(head_back_kernel, query is not None),
        "head_back",
        (steps,),
        [
            rows(e),
            rows(e),
            whole_spec((D, e)),
            rows(D),
            rows(LANES),
            whole_spec((1, D)),
        ]
        + [whole_spec(x.shape) for x in extra]
        + [pl.BlockSpec(memory_space=pl.ANY)] * len(before),
        [rows(D), rows(D), rows(e), whole_spec((3, D))],
        [like((t, D), f32), like((t, D), bf16), like((t, e), bf16), like((3, D), f32)],
        2 * steps * TILE * D * e,
        16 * steps * TILE * D,
        wait=wait,
        aliases={6 + len(extra) + i: i for i in range(len(before))},
    )(g, raw, proj, hat, rstd, gain, *extra, *before)


def act_back_kernel(g_ref, w_ref, slope_ref, o_ref, sum_ref):
    total = jnp.zeros(sum_ref.shape, f32)
    for row in range(0, g_ref.shape[0], TILE):
        rows = slice(row, row + TILE)
        back = contract(g_ref[rows, :], w_ref[...], 1, 1) * slope_ref[rows, :].astype(f32)
        back = back.astype(bf16)
        o_ref[rows, :] = back
        total = total + column_sum(back.astype(f32))
    sum_ref[...] = total


def act_back(branch, w, slope, wait=()):
    t, ff = slope.shape
    return call(
        act_back_kernel,
        "act_back",
        (ff // UP_TILE,),
        [whole_spec((t, D)), row_spec(UP_TILE, D), col_spec(t, UP_TILE)],
        [col_spec(t, UP_TILE), col_spec(1, UP_TILE)],
        [like((t, ff), bf16), like((1, ff), f32)],
        2 * t * D * ff,
        4 * t * ff + 2 * D * ff,
        wait=wait,
    )(branch, w, slope)


def hidden_back_kernel(
    g_ref, w_ref, resid_ref, hat_ref, rstd_ref, gain_ref, wout_ref,
    grad_ref, out_ref, att_ref, sums_ref,
):
    for row in range(0, g_ref.shape[0], TILE):
        rows = slice(row, row + TILE)
        hidden_grad = resid_ref[rows, :] + contract(g_ref[rows, :], w_ref[...], 1, 1)
        hat = hat_ref[rows, :]
        grad = norm_back(hidden_grad, hat, rstd_ref[rows, :1], gain_ref[...])
        low = grad.astype(bf16)
        grad_ref[rows, :] = grad
        out_ref[rows, :] = low
        att_ref[rows, :] = contract(low, wout_ref[...], 1, 1).astype(bf16)
        sums = [column_sum(hidden_grad * hat), column_sum(hidden_grad), column_sum(low.astype(f32))]
        if row == 0:
            add_up(sums_ref, jnp.concatenate(sums, axis=0))
        else:
            sums_ref[...] += jnp.concatenate(sums, axis=0)


def hidden_back(inner, w, resid, hat, rstd, gain, w_out, wait=()):
    t, ff = inner.shape
    return call(
        hidden_back_kernel,
        "hidden_back",
        (t // TILE,),
        [
            row_spec(TILE, ff),
            whole_spec((D, ff)),
            row_spec(TILE, D),
            row_spec(TILE, D),
            row_spec(TILE, LANES),
            whole_spec((1, D)),
            whole_spec((D, D)),
        ],
        [row_spec(TILE, D)] * 3 + [whole_spec((3, D))],
        [like((t, D), f32), like((t, D), bf16), like((t, D), bf16), like((3, D), f32)],
        2 * t * D * ff + 2 * t * D * D,
        2 * t * ff + 24 * t * D,
        wait=wait,
    )(inner, w, resid, hat, rstd, gain, w_out)


def input_back_kernel(groups, *refs):
    g_refs, (w_ref, resid_ref, o_ref) = refs[:groups], refs[groups:]
    total = resid_ref[...]
    for part in range(3):
        for i, g_ref in enumerate(g_refs):
            width = g_ref.shape[2]
            at = part * D + i * width
            total = total + contract(g_ref[part], w_ref[:, at : at + width], 1, 1)
    o_ref[...] = total


def input_back(grads, w, resid, wait=()):
    t = resid.shape[0]
    return call(
        functools.partial(input_back_kernel, len(grads)),
        "input_back",
        (t // TILE,),
        [pl.BlockSpec((3, TILE, g.shape[2]), lambda i: (0, i, 0)) for g in grads]
        + [whole_spec((D, 3 * D)), row_spec(TILE, D)],
        row_spec(TILE, D),
        like((t, D), f32),
        6 * t * D * D,
        20 * t * D,
        wait=wait,
    )(*grads, w, resid)


def block_masks(n_devices, width):
    n = width * n_devices
    column = lax.broadcasted_iota(jnp.int32, (n_devices, n), 1)
    first = lax.broadcasted_iota(jnp.int32, (n_devices, n), 0) * width
    mine = (column >= first) & (column < first + width)
    at = lax.broadcasted_iota(jnp.int32, (1, n), 1) % width
    return mine, at


def unpack_kernel(n_devices, widths, p_ref, *o_refs):
    start = 0
    for width, o_ref in zip(widths, o_refs):
        mine, at = block_masks(n_devices, width)
        copies = (at == lax.broadcasted_iota(jnp.int32, (width, at.shape[1]), 0)).astype(bf16)
        spread = contract(p_ref[:, start : start + width], copies, 1, 0)
        o_ref[...] = column_sum(jnp.where(mine, spread, 0.0))
        start += width


def unpack(packed, widths, wait=()):
    n_devices = packed.shape[0]
    return call(
        functools.partial(unpack_kernel, n_devices, widths),
        "unpack",
        (1,),
        [whole_spec(packed.shape)],
        [whole_spec((1, w * n_devices)) for w in widths],
        [like((1, w * n_devices), f32) for w in widths],
        10**8,
        10**5,
        wait=wait,
    )(packed)


def pack_kernel(n_devices, widths, *refs):
    o_ref = refs[-1]
    o_ref[...] = jnp.zeros_like(o_ref)
    start = 0
    for width, ref in zip(widths, refs):
        mine, at = block_masks(n_devices, width)
        copies = (at == lax.broadcasted_iota(jnp.int32, (width, at.shape[1]), 0)).astype(bf16)
        rest = jnp.where(mine, ref[...], 0.0)
        total = jnp.zeros((n_devices, width), f32)
        for _ in range(3):
            term = rest.astype(bf16)
            total = total + contract(term, copies, 1, 1)
            rest = rest - term.astype(f32)
        o_ref[:, start : start + width] = total
        start += width


def pack(vectors, n_devices, wait=()):
    widths = [v.shape[1] // n_devices for v in vectors]
    total = sum(widths)
    total += -total % LANES
    return call(
        functools.partial(pack_kernel, n_devices, widths),
        "pack",
        (1,),
        [whole_spec(v.shape) for v in vectors],
        whole_spec((n_devices, total)),
        like((n_devices, total), f32),
        10**8,
        10**5,
        wait=wait,
    )(*vectors)


def pick_columns(table, offset, n_rows, n_z, a_ref, picked):
    t, k = a_ref.shape
    block = k // n_rows
    half = block // 2
    r = half // n_z
    core = table[2 * n_rows]
    side = core if offset == 0 else 1 - core
    if r % LANES:
        m = lax.broadcasted_iota(jnp.int32, (block, half), 1)
        source = (m // r) * (2 * r) + side * r + m % r
        choose = (lax.broadcasted_iota(jnp.int32, (block, half), 0) == source).astype(bf16)
    for piece in range(n_rows):
        first = table[offset + piece] * block
        if r % LANES:
            x = a_ref[:, pl.ds(pl.multiple_of(first, LANES), block)]
            picked[:, piece * half : (piece + 1) * half] = contract(x, choose, 1, 0).astype(bf16)
        else:
            for z in range(n_z):
                x = a_ref[:, pl.ds(pl.multiple_of(first + (2 * z + side) * r, LANES), r)]
                at = piece * half + z * r
                picked[:, at : at + r] = x


def weight_kernel(pairs, offset, n_rows, n_z, table, *refs):
    ins, refs = refs[: 2 * pairs], refs[2 * pairs :]
    refs, picked = refs[:-pairs], refs[-pairs:]

    @pl.when(pl.program_id(0) == 0)
    def _():
        for a_ref, p_ref in zip(ins[::2], picked):
            pick_columns(table, offset, n_rows, n_z, a_ref, p_ref)

    totals = []
    for p_ref, b_ref in zip(picked, ins[1::2]):
        b = b_ref[...]
        totals.append(contract(p_ref[...], b.reshape(b.shape[-2:]), 0, 0))
    total = totals[0] if pairs == 1 else jnp.concatenate(totals, axis=1)
    if len(refs) == 1:
        refs[0][...] = total.reshape(refs[0].shape).astype(refs[0].dtype)
    else:
        other, send_ref, keep_ref = refs
        total = total.reshape(other.shape) + other[...].astype(f32)
        half = keep_ref.shape[0]
        send_ref[...] = total[half:].astype(send_ref.dtype)
        keep_ref[...] = total[:half]


def weight_half(name, table, operands, n_rows, n_z, tile, other=None, other_type=bf16, wait=()):
    t, k = operands[0][0].shape
    r = k // (n_rows * n_z * 2)
    specs, arrays = [], []
    if len(operands) == 1:
        a, b = operands[0]
        per_part = b.shape[-1] // tile
        n = b.shape[-1] * (b.shape[0] if b.ndim == 3 else 1)
        if b.ndim == 3:
            b_spec = pl.BlockSpec((1, t, tile), lambda i, _: (i // per_part, 0, i % per_part))
        else:
            b_spec = col_spec(t, tile)
        specs, arrays = [whole_spec((t, k)), b_spec], [a, b]
    else:
        n = tile = sum(b.shape[1] for _, b in operands)
        for a, b in operands:
            specs += [whole_spec((t, k)), whole_spec(b.shape)]
            arrays += [a, b]

    def block(rows):
        return pl.BlockSpec((rows, n_z, r, tile), lambda i, _: (0, 0, 0, i))

    def shape(rows, dtype):
        return like((rows, n_z, r, n), dtype)

    own = other is not None
    return call(
        functools.partial(weight_kernel, len(operands), 0 if own else n_rows, n_rows, n_z),
        name,
        (n // tile,),
        specs + ([block(n_rows)] if own else []),
        [block(n_rows // 2)] * 2 if own else block(n_rows),
        [shape(n_rows // 2, bf16), shape(n_rows // 2, f32)] if own else shape(n_rows, other_type),
        t * k * n,
        2 * t * (k + n) + 3 * k * n,
        [pltpu.VMEM((t, k // 2), bf16) for _ in operands],
        table=table,
        wait=wait,
    )(table, *arrays, *([other] if own else []))


WINDOWS = (256, -(-(DMOST + 15) // 32) * 32)
NEG = -1e30


def contract(a, b, ca, cb):
    return lax.dot_general(a, b, (((ca,), (cb,)), ((), ())), preferred_element_type=f32)


def document_table(lengths):
    at = jnp.arange(DPR)
    starts = QPR * QLEN + jnp.sum(jnp.where(at[:, None] < at[None, :], lengths[:, None], 0), axis=0)
    need = starts % 16 + lengths
    ahead = (need[:, None] > need[None, :]) | ((need[:, None] == need[None, :]) & (at[:, None] < at[None, :]))
    rank = jnp.sum(ahead.astype(jnp.int32), axis=0)
    order = rank[None, :] == at[:, None]
    pick = lambda x: jnp.sum(jnp.where(order, x[None, :], 0), axis=1)
    wide = jnp.sum((need > WINDOWS[0]).astype(jnp.int32))
    return jnp.concatenate([pick(starts), pick(lengths), wide[None]]).astype(jnp.int32)


def for_documents(doc_ref, row_len, step):
    for wide in range(1, DPR):

        @pl.when(doc_ref[2 * DPR] == wide)
        def _():
            for d in range(DPR):
                window = WINDOWS[1] if d < wide else WINDOWS[0]
                start, size = doc_ref[d], doc_ref[DPR + d]
                base = pl.multiple_of(jnp.minimum((start // 16) * 16, row_len - window), 16)
                step(window, base, start - base, start - base + size)


def head_pair(x):
    lane = lax.broadcasted_iota(jnp.int32, x.shape, 1)
    zero = jnp.zeros_like(x)
    return jnp.concatenate(
        [jnp.where(lane < HEAD_DIM, x, zero), jnp.where(lane < HEAD_DIM, zero, x)], axis=0
    )


def pair_heads(x):
    n = x.shape[0] // 2
    lane = lax.broadcasted_iota(jnp.int32, (n, x.shape[1]), 1)
    return jnp.where(lane < HEAD_DIM, x[:n], x[n:])


def inside(n, low, high, axis):
    shape = (n, 1) if axis == 0 else (1, n)
    at = lax.broadcasted_iota(jnp.int32, shape, axis)
    return (at >= low) & (at < high)


def attend(q, k, v, low, high):
    s = contract(head_pair(q), k, 1, 1)
    s = s + jnp.where(inside(k.shape[0], low, high, 1), 0.0, NEG)
    p = jnp.exp(s - jnp.max(s, axis=1, keepdims=True))
    total = jnp.sum(p, axis=1, keepdims=True)
    return pair_heads(contract(p.astype(bf16), v, 1, 0) / total)


def attention_kernel(len_ref, q_ref, k_ref, v_ref, o_ref):
    def step(window, base, low, high):
        w = pl.ds(base, window)
        o = attend(q_ref[w, :], k_ref[w, :], v_ref[w, :], low, high)
        keep = inside(window, low, high, 0)
        o_ref[w, :] = jnp.where(keep, o, o_ref[w, :].astype(f32)).astype(bf16)

    for_documents(len_ref, q_ref.shape[0], step)
    o_ref[:QLEN, :] = attend(q_ref[:QLEN, :], k_ref[:128, :], v_ref[:128, :], 0, QLEN).astype(bf16)


def qkv_specs(t):
    per_part = D // LANES
    return [
        pl.BlockSpec((t, LANES), lambda i, _, p=p: (0, p * per_part + i)) for p in range(3)
    ]


def attention(lengths, qkv, wait=()):
    t = qkv.shape[0]
    return call(
        attention_kernel,
        "attention",
        (HEADS // 2,),
        qkv_specs(t),
        col_spec(t, LANES),
        like((t, D), bf16),
        2 * 10**10,
        8 * t * D,
        table=lengths,
        wait=wait,
    )(lengths, qkv, qkv, qkv)


def attend_back(q, k, v, g, low, high):
    n = q.shape[0]
    g = jnp.where(inside(n, low, high, 0), g, jnp.zeros_like(g))
    qq = head_pair(q)
    gg = head_pair(g)
    st = contract(k, qq, 1, 1)
    st = st + jnp.where(inside(k.shape[0], low, high, 0), 0.0, NEG)
    p = jnp.exp(st - jnp.max(st, axis=0, keepdims=True))
    p = p * (1.0 / jnp.sum(p, axis=0, keepdims=True))
    dp = contract(v, gg, 1, 1)
    delta = jnp.sum(p * dp, axis=0, keepdims=True)
    ds = (p * (dp - delta)).astype(bf16)
    dv = contract(p.astype(bf16), gg, 1, 0)
    dk = contract(ds, qq, 1, 0)
    dq = contract(ds, k, 0, 0) * (HEAD_DIM**-0.5)
    return pair_heads(dq), dk, dv


def attention_back_kernel(len_ref, q_ref, k_ref, v_ref, g_ref, cos_ref, sin_ref, o_ref, sum_ref, *sums):
    row_len = q_ref.shape[0]
    for ref in sums:
        ref[...] = jnp.zeros_like(ref)
    parts = attend_back(
        q_ref[:QLEN, :], k_ref[:128, :], v_ref[:128, :], g_ref[:QLEN, :], 0, QLEN
    )
    for ref, x in zip(sums, parts):
        ref[: x.shape[0], :] = x

    def step(window, base, low, high):
        w = pl.ds(base, window)
        parts = attend_back(q_ref[w, :], k_ref[w, :], v_ref[w, :], g_ref[w, :], low, high)
        for ref, x in zip(sums, parts):
            ref[w, :] += x

    for_documents(len_ref, row_len, step)
    cosine, sine = cos_ref[...], sin_ref[...]
    for part in range(3):
        x = sums[part][...]
        if part < 2:
            x = x * cosine - swap_halves(x) * sine
        x = x.astype(bf16)
        o_ref[part] = x
        sum_ref[part] = column_sum(x.astype(f32))


def attention_back(lengths, qkv, g, cosine, sine, group, groups, wait=()):
    t = qkv.shape[0]
    table = whole_spec((t, LANES))
    pairs = HEADS // 2 // groups
    first = group * pairs
    per_part = D // LANES
    specs = [
        pl.BlockSpec((t, LANES), lambda i, _, p=p: (0, p * per_part + first + i)) for p in range(3)
    ]
    return call(
        attention_back_kernel,
        "attention_back",
        (pairs,),
        specs + [pl.BlockSpec((t, LANES), lambda i, _: (0, first + i)), table, table],
        [
            pl.BlockSpec((3, t, LANES), lambda i, _: (0, 0, i)),
            pl.BlockSpec((3, 1, LANES), lambda i, _: (0, 0, i)),
        ],
        [like((3, t, D // groups), bf16), like((3, 1, D // groups), f32)],
        5 * 10**10 // groups,
        14 * t * D // groups,
        [pltpu.VMEM((t, LANES), f32)] * 3,
        table=lengths,
        wait=wait,
    )(lengths, qkv, qkv, qkv, g, cosine, sine)


SCORE_TILE = 256


def doc_inside(doc_ref, d):
    return doc_ref[...] == d


def score_exps(docs, queries, mask):
    picked = jnp.where(mask, docs, jnp.zeros_like(docs))
    return picked, jnp.exp(contract(picked, queries, 1, 1) * score_scale)


def split_dot(hot, x):
    high = x.astype(bf16)
    rest = (x - high.astype(f32)).astype(bf16)
    return contract(hot, high, 1, 0) + contract(hot, rest, 1, 0)


def score_kernel(
    doc_ref, query_ref, id_ref, hot_ref, count_ref, pos_ref, sum_ref, score_ref, stat_ref
):
    docs = doc_ref[...]
    n_queries = score_ref.shape[2]
    live = lax.broadcasted_iota(jnp.int32, (8, n_queries), 0) < DPR
    for head, (lanes, mask) in enumerate(head_lanes()):
        scores = jnp.zeros((8, n_queries), f32)
        for at in range(0, query_ref.shape[0], SCORE_TILE):
            _, e = score_exps(docs[:, lanes], query_ref[at : at + SCORE_TILE, lanes], mask)
            total = split_dot(hot_ref[...], e)
            sum_ref[head, :, at : at + SCORE_TILE] = total
            smooth = jnp.log(total) - count_ref[:, :1]
            query = lax.broadcasted_iota(jnp.int32, (SCORE_TILE, n_queries), 1)
            hot = (id_ref[at : at + SCORE_TILE, :] == query).astype(f32)
            scores += lax.dot_general(
                jnp.where(lax.broadcasted_iota(jnp.int32, smooth.shape, 0) < DPR, smooth, 0.0),
                hot,
                (((1,), (0,)), ((), ())),
                precision=highest,
                preferred_element_type=f32,
            )
        score_ref[head] = scores
        top = jnp.max(jnp.where(live, scores, NEG), axis=0, keepdims=True)
        den = column_sum(jnp.where(live, jnp.exp(scores - top), 0.0))
        pos = column_sum(jnp.where(live, scores * pos_ref[...], 0.0))
        stat_ref[head] = jnp.concatenate([top, den, pos], axis=0)


def score_grad_kernel(
    doc_ref, query_ref, id_ref, index_ref, sum_ref, score_ref, stat_ref, pos_ref, dq_ref, dd_ref
):
    docs = doc_ref[...]
    n_queries = score_ref.shape[2]
    dd_ref[...] = jnp.zeros_like(dd_ref)
    dq_ref[...] = jnp.zeros_like(dq_ref)
    index = index_ref[...]
    for head, (lanes, mask) in enumerate(head_lanes()):
        stats = stat_ref[head]
        grad = jnp.exp(score_ref[head] - stats[0:1]) / stats[1:2] - pos_ref[...]
        for at in range(0, query_ref.shape[0], SCORE_TILE):
            queries = query_ref[at : at + SCORE_TILE, lanes]
            picked, e = score_exps(docs[:, lanes], queries, mask)
            query = lax.broadcasted_iota(jnp.int32, (n_queries, SCORE_TILE), 0)
            hot = (id_ref[:, at : at + SCORE_TILE] == query).astype(f32)
            spread = lax.dot_general(
                grad, hot, (((1,), (0,)), ((), ())), precision=highest, preferred_element_type=f32
            )
            coef = score_scale * spread / sum_ref[head, :, at : at + SCORE_TILE]
            wide = jnp.zeros_like(e)
            for d in range(DPR):
                wide = jnp.where(index == d, coef[d : d + 1], wide)
            back = (e * wide).astype(bf16)
            dd_ref[:, lanes] += jnp.where(mask, contract(back, queries, 1, 0), 0.0)
            dq_ref[at : at + SCORE_TILE, lanes] += contract(back, picked, 0, 0)


def score_stats(docs, queries, ids, hot, counts, positive, wait=()):
    n, e = docs.shape
    n_tokens = queries.shape[0]
    n_queries = n_tokens // QLEN
    return call(
        score_kernel,
        "scores",
        (1,),
        [
            whole_spec((n, e)),
            whole_spec((n_tokens, e)),
            whole_spec((n_tokens, 1)),
            whole_spec((8, n)),
            whole_spec((8, LANES)),
            whole_spec((8, n_queries)),
        ],
        [
            whole_spec((3, 8, n_tokens)),
            whole_spec((3, 8, n_queries)),
            whole_spec((3, 3, n_queries)),
        ],
        [
            like((3, 8, n_tokens), f32),
            like((3, 8, n_queries), f32),
            like((3, 3, n_queries), f32),
        ],
        12 * n * n_tokens * e,
        10**6,
        wait=wait,
    )(docs, queries, ids, hot, counts, positive)


def score_grads(docs, queries, ids, index, sums, scores, stats, positive, wait=()):
    n, e = docs.shape
    n_tokens = queries.shape[0]
    n_queries = n_tokens // QLEN
    return call(
        score_grad_kernel,
        "score_grads",
        (1,),
        [
            whole_spec((n, e)),
            whole_spec((n_tokens, e)),
            whole_spec((1, n_tokens)),
            whole_spec((n, 1)),
            whole_spec((3, 8, n_tokens)),
            whole_spec((3, 8, n_queries)),
            whole_spec((3, 3, n_queries)),
            whole_spec((8, n_queries)),
        ],
        [whole_spec((n_tokens, e)), whole_spec((n, e))],
        [like((n_tokens, e), f32), like((n, e), f32)],
        24 * n * n_tokens * e,
        10**6,
        wait=wait,
    )(docs, queries, ids, index, sums, scores, stats, positive)


def layout(lengths, row_len, q_tokens):
    count = lengths.shape[0]
    before = jnp.arange(count)[:, None] <= jnp.arange(count)[None, :]
    ends = jnp.sum(jnp.where(before, lengths[:, None], 0), axis=0)
    offset = jnp.arange(row_len, dtype=jnp.int32) - q_tokens
    doc = jnp.sum((offset[:, None] >= ends[None, :]).astype(jnp.int32), axis=1)
    chosen = (doc[:, None] == jnp.arange(count, dtype=jnp.int32)[None, :]).astype(
        jnp.int32
    )
    begin = jnp.sum(chosen * (ends - lengths)[None, :], axis=1)
    is_query = offset < 0
    position = jnp.where(is_query, (offset + q_tokens) % QLEN, offset - begin)
    return position, doc


def combine_stats(one, two):
    top = jnp.maximum(one[:, 0], two[:, 0])
    den = one[:, 1] * jnp.exp(one[:, 0] - top) + two[:, 1] * jnp.exp(two[:, 0] - top)
    return jnp.stack([top, den, one[:, 2] + two[:, 2]], axis=1)


def reduce_stats(stats):
    n_rows, n_z, _, _ = sizes()
    moves = [[dict(swap_core=True)]]
    moves.append([dict(row_masks=(m, m)) for m in range(1, n_rows)])
    moves.append([dict(z_mask=m) for m in range(1, n_z)])
    for level in moves:
        parts = [exchange(stats, **move) for move in level]
        for part in parts:
            stats = combine_stats(stats, part)
    return stats


def on_device(
    tokens,
    lengths,
    positives,
    w_qkv,
    b_qkv,
    w_out,
    b_out,
    norm1_gain,
    norm1_bias,
    w_up,
    b_up,
    w_down,
    b_down,
    norm2_gain,
    norm2_bias,
    w_proj,
):
    n_rows, n_z, _, _ = sizes()
    n_devices = n_rows * n_z * 2
    row, z, core = place()
    device = (row * n_z + z) * 2 + core
    table = piece_table()
    row_len = tokens.shape[0]
    q_tokens = QPR * QLEN

    proj_width = -(-w_proj.shape[1] // LANES) * LANES
    w_out_proj = jnp.concatenate(
        [w_out, jnp.pad(w_proj, ((0, 0), (0, proj_width - w_proj.shape[1])))], axis=1
    )
    g_qkv, g_out, g_up, g_down = (Gather(w) for w in (w_qkv, w_out_proj, w_up, w_down))
    g_qkv.all_z(())
    g_qkv.all_rows((), ())
    first, last = g_qkv.own, g_qkv.pieces[-1]
    vectors = (b_qkv, b_out, norm1_gain, norm1_bias, b_up, b_down, norm2_gain, norm2_bias)
    widths = [v.shape[0] for v in vectors]
    packed = jnp.concatenate(vectors)
    packed = jnp.pad(packed, (0, -packed.shape[0] % LANES)).reshape(-1, LANES)
    packed = gather_small(packed, g_qkv.received + [first[0], last]).reshape(n_devices, -1)
    full_bqkv, full_bout, gain_one, bias_one, full_bup, full_bdown, gain_two, bias_two = unpack(
        packed, widths
    )
    g_up.all_z([[g_qkv.held], first], [first, [last]])
    g_out.all_z([first])
    w_qkv_all = g_qkv.whole(table)

    own_lengths = lax.dynamic_index_in_dim(lengths, device, 0, keepdims=False)
    position, doc_index = layout(own_lengths, row_len, q_tokens)
    documents = document_table(own_lengths)
    half = HEAD_DIM // 2
    frequency = 10000.0 ** (-jnp.arange(half, dtype=f32) / half)
    angles = position.astype(f32)[:, None] * frequency[None, :]
    cosine, sine = jnp.cos(angles), jnp.sin(angles)
    cosine = jnp.concatenate([cosine] * 4, axis=1)
    sine = jnp.concatenate([-sine, sine] * 2, axis=1)
    qkv, full_qkv = project_qkv(
        tokens, w_qkv_all, full_bqkv, cosine, sine, wait=[g_up.held]
    )
    g_out.own_rows([last], [qkv])
    g_up.own_rows([last], [qkv])
    doc_index = jnp.where(jnp.arange(row_len) < q_tokens, -1, doc_index)
    slots = jnp.arange(8, dtype=jnp.int32)
    hot = (slots[:, None] == doc_index[None, :]).astype(bf16)
    counts = jnp.broadcast_to(
        jnp.log(jnp.pad(own_lengths, (0, 8 - DPR), constant_values=1).astype(f32))[:, None],
        (8, LANES),
    )
    positive = (
        (positives[None, :] == device * DPR + slots[:, None]) & (slots < DPR)[:, None]
    ).astype(f32)
    query_ids = relative_order()[:, None] * QPR + jnp.arange(q_tokens, dtype=jnp.int32)[None, :] // QLEN
    query_ids = query_ids.reshape(-1, 1)
    query_row = query_ids.reshape(1, -1)
    doc_column = doc_index[:, None]
    early = [hot, counts, positive, query_ids, query_row, doc_column]
    attended = attention(documents, qkv, wait=[*g_up.pieces[1:], *early])
    g_out.other_rows([qkv], [attended])
    g_up.other_rows([qkv], [attended])
    w_out_all = g_out.whole(table, [[qkv], [attended]], [[attended]])
    g_down.all_z([[g_up.held], [qkv]], [[qkv], [attended]])
    hat1, rstd1, hidden_low, full_out = out_norm(
        attended, w_out_all.columns(0, D), full_bout, tokens, gain_one, bias_one, wait=[g_down.held]
    )

    w_up_all = g_up.whole(table, [[qkv], [attended]], [[attended]])
    part = up_gelu(hidden_low, w_up_all, full_bup)
    g_down.own_rows([attended], [part[0]])
    g_down.other_rows([part[0]])
    act, slope, full_up = up_gelu(hidden_low, w_up_all, full_bup, part, wait=g_down.own)
    w_down_all = g_down.whole(table, [[part[0]], [act]], [[act]])
    hat2, rstd2, result_low, raw, vecs, full_down, full_proj = down_norm(
        act,
        w_down_all,
        full_bdown,
        hat1,
        gain_one,
        bias_one,
        gain_two,
        bias_two,
        w_out_all.columns(D, proj_width),
    )
    full_qkv, full_out, full_up, full_down, full_proj = (
        w.reshape(-1, w.shape[-1]) for w in (full_qkv, full_out, full_up, full_down, full_proj)
    )

    query_all = gather_relative(vecs[:q_tokens]).reshape(n_devices * q_tokens, -1)
    sums, doc_scores, stats = score_stats(
        vecs, query_all, query_ids, hot, counts, positive
    )
    stats = reduce_stats(stats)
    query_count = n_z * 2 * QPR
    losses = lax.dynamic_slice_in_dim(
        stats[:, 0] + jnp.log(stats[:, 1]) - stats[:, 2], row * query_count, query_count, 1
    )
    query_grads, doc_grads = score_grads(
        vecs, query_all, query_row, doc_column, sums, doc_scores, stats, positive
    )
    doc_part = head_back(doc_grads, raw, full_proj, hat2, rstd2, gain_two)
    query_grad = scatter_relative(
        query_grads.reshape(2, n_rows, n_z, q_tokens, -1), bf16, [doc_part[2]]
    )
    resid_two_grad, branch_grad, raw_grad, sums2 = head_back(
        doc_grads, raw, full_proj, hat2, rstd2, gain_two, query_grad, doc_part[:3]
    )
    sums2 = sums2 + doc_part[3]

    def sib_half(name, operands, tile, dtype=bf16, wait=()):
        return weight_half(name + "_sib", table, operands, n_rows, n_z, tile, other_type=dtype, wait=wait)

    def own_half(name, operands, tile, sib, wide=False, wait=()):
        other = exchange(sib, swap_core=True)
        return Scatter(*weight_half(name, table, operands, n_rows, n_z, tile, other, wait=wait), wide)

    def attention_part(i, wait):
        return attention_back(documents, qkv, attended_grad, cosine, sine, i, 2, wait=wait)

    down_sib = sib_half("grad_down", [(act, branch_grad)], 512)
    inner_grad, grad_bup = act_back(branch_grad, full_down, slope, wait=[down_sib])
    down = own_half("grad_down", [(act, branch_grad)], 512, down_sib, True, wait=[grad_bup])
    up_sib = sib_half("grad_up", [(hidden_low, inner_grad)], 1024, f32, wait=[down.send])
    resid_one_grad, out_grad, attended_grad, sums1 = hidden_back(
        inner_grad, full_up, resid_two_grad, hat1, rstd1, gain_one, full_out, wait=[up_sib]
    )
    d2 = down.step(sums1)
    up = own_half("grad_up", [(hidden_low, inner_grad)], 1024, up_sib, wait=[sums1, d2])
    d3 = down.step(up.send)
    grad_a, sums_a = attention_part(0, [up.send, d3])
    sib_a = sib_half("grad_qkv", [(tokens, grad_a)], 512)
    d4 = down.step(sums_a)
    u2 = up.step(sums_a)
    out_sib = sib_half(
        "grad_out", [(attended, out_grad), (result_low, raw_grad)], None, wait=[sib_a]
    )
    grad_b, sums_b = attention_part(1, [out_sib, d4, u2])
    sib_b = sib_half("grad_qkv", [(tokens, grad_b)], 512)
    out = own_half(
        "grad_out",
        [(attended, out_grad), (result_low, raw_grad)],
        None,
        out_sib,
        True,
        wait=[sib_b],
    )
    u3 = up.step(sums_b)
    sum_down = down.finish(sums_b)
    qkv_a = own_half("grad_qkv", [(tokens, grad_a)], 512, sib_a, wait=[out.send, u3])
    u4 = up.step(qkv_a.send)
    o2 = out.step(qkv_a.send)
    qkv_b = own_half("grad_qkv", [(tokens, grad_b)], 512, sib_b, wait=[qkv_a.send, u4, o2])
    a2 = qkv_a.step(qkv_b.send)
    o3 = out.step(qkv_b.send)
    input_grad = input_back([grad_a, grad_b], full_qkv, resid_one_grad, wait=[qkv_b.send, a2, o3])
    b2 = qkv_b.step(input_grad)
    qkv_a.step(input_grad)
    o4 = out.step(b2)
    sum_up = up.finish(b2)
    grads = [sums_a[i] if j == 0 else sums_b[i] for i in range(3) for j in range(2)]
    grad_bqkv = jnp.concatenate(grads, axis=1)
    small = pack(
        [grad_bqkv, sums1[2:3], sums1[0:1], sums1[1:2], grad_bup, sums2[2:3], sums2[0:1], sums2[1:2]],
        n_devices,
        wait=[b2],
    )
    while qkv_b.stages[0][0] == "row":
        qkv_b.step(small)
    while qkv_a.stages[0][0] == "row":
        qkv_a.step()
    q3 = qkv_a.merge(qkv_b).send
    small = scatter_small(small.reshape(n_devices, -1, LANES), f32).reshape(-1)
    sum_out = out.finish(q3)
    sum_out, sum_proj = sum_out[:, :D], sum_out[:, D : D + w_proj.shape[1]]
    sum_qkv = qkv_a.finish()
    width = D // 2
    sum_qkv = jnp.concatenate(
        [sum_qkv[:, at * width : (at + 1) * width] for at in (0, 3, 1, 4, 2, 5)], axis=1
    )
    pieces = []
    at = 0
    for width in widths:
        pieces.append(small[at : at + width])
        at += width
    s_bqkv, s_bout, s_gain1, s_bias1, s_bup, s_bdown, s_gain2, s_bias2 = pieces
    return (
        losses,
        result_low,
        input_grad,
        sum_qkv,
        s_bqkv,
        sum_out,
        s_bout,
        s_gain1,
        s_bias1,
        sum_up,
        s_bup,
        sum_down,
        s_bdown,
        s_gain2,
        s_bias2,
        sum_proj,
    )


def solution(mesh):
    shard = P(AXES, None)
    vec = P(AXES)
    in_specs = (
        shard,
        P(),
        P(),
        shard,
        vec,
        shard,
        vec,
        vec,
        vec,
        shard,
        vec,
        shard,
        vec,
        vec,
        vec,
        shard,
    )
    out_specs = (P(None, "row"), shard) + (shard,) + in_specs[3:]
    return jax.shard_map(
        on_device, mesh=mesh, in_specs=in_specs, out_specs=out_specs, check_vma=False
    )
```

```python
import functools

import jax
import jax.numpy as jnp
from jax import lax
from jax.experimental import pallas as pl
from jax.experimental.pallas import tpu as pltpu
from jax.sharding import PartitionSpec as P

D = 1024
HEADS = 16
HEAD_DIM = 64
PROJ_A = 128
PROJ_B = 96
PROJ_C = 64
QLEN = 32
DPR = 4
QPR = 1
DMOST = 330

AXES = ("row", "col")
highest = lax.Precision.HIGHEST
eps_norm = 1e-05
eps_vec = 1e-06
score_scale = 16.0
f32 = jnp.float32
bf16 = jnp.bfloat16


def sizes():
    n_rows = lax.axis_size("row")
    n_z = lax.axis_size("col") // 2
    return n_rows, n_z, n_rows.bit_length() - 1, n_z.bit_length() - 1


def after(value, *before):
    return lax.optimization_barrier((value,) + before)[0] if before else value


def place():
    col = lax.axis_index("col")
    return lax.axis_index("row"), col // 2, col % 2


def exchange(value, row_masks=(0, 0), z_mask=0, swap_core=False):
    n_rows, n_z, _, _ = sizes()
    pairs = []
    for r in range(n_rows):
        for z in range(n_z):
            for c in range(2):
                here = (r * n_z + z) * 2 + c
                there = ((r ^ row_masks[c]) * n_z + (z ^ z_mask)) * 2 + (
                    1 - c if swap_core else c
                )
                pairs.append((here, there))
    return lax.ppermute(value, AXES, pairs)


def stage_bit(core, stage, row_bits):
    return (stage + core) % row_bits


def stage_masks(stage):
    _, _, row_bits, _ = sizes()
    return tuple(1 << stage_bit(c, stage, row_bits) for c in range(2))


def piece_mask(core, piece):
    _, _, row_bits, _ = sizes()
    return sum(
        1 << stage_bit(core, j, row_bits) for j in range(row_bits) if piece >> j & 1
    )


def ordered(bit, own, other, axis):
    return jnp.stack([jnp.where(bit == 0, own, other), jnp.where(bit == 0, other, own)], axis)


def transfer(value, start=(), use=(), **move):
    return after(exchange(after(value, *start), **move), *use)


class Gather:
    def __init__(self, shard):
        self.held, self.count, self.shard, self.received = shard, 0, shard, []

    def along_z(self, start=(), use=()):
        _, n_z, _, z_bits = sizes()
        _, z, _ = place()
        bit = z_bits - 1 - self.count
        other = transfer(self.held, start, use, z_mask=1 << bit)
        self.received.append(other)
        self.held = ordered(z >> bit & 1, self.held, other, self.count)
        self.count += 1
        if self.count == z_bits:
            self.pieces = [self.held.reshape((n_z,) + self.shard.shape)]

    def all_z(self, *bounds):
        _, _, _, z_bits = sizes()
        for i in range(z_bits):
            self.along_z(*bounds[min(i, len(bounds) - 1)])

    def own_rows(self, start=(), use=()):
        _, _, row_bits, _ = sizes()
        self.own = [
            transfer(self.pieces[0], start, use, row_masks=stage_masks(stage))
            for stage in range(row_bits)
        ]
        self.pieces = self.pieces + self.own

    def other_rows(self, start=(), use=()):
        _, _, row_bits, _ = sizes()
        pieces = [self.pieces[0], self.own[0]]
        for stage in range(1, row_bits):
            pieces = pieces + [self.own[stage]] + [
                transfer(p, start, use, row_masks=stage_masks(stage)) for p in pieces[1:]
            ]
        self.pieces = pieces

    def all_rows(self, own, other):
        self.own_rows(*own)
        self.other_rows(*other)

    def whole(self, table, early=(), late=()):
        last = len(self.pieces) - 1
        sibs = [
            transfer(p, *(late if i == last else early), swap_core=True)
            for i, p in enumerate(self.pieces)
        ]
        return Weight(table, self.pieces + sibs)


def piece_table():
    n_rows, _, _, _ = sizes()
    row, _, core = place()
    tables = [
        jnp.array([piece_mask(c, k) for k in range(n_rows)], jnp.int32) for c in range(2)
    ]
    own = row ^ jnp.where(core == 0, tables[0], tables[1])
    sib = row ^ jnp.where(core == 0, tables[1], tables[0])
    steps = jnp.arange(n_rows)

    def piece_of(rows):
        return jnp.sum(jnp.where(rows[None, :] == steps[:, None], steps[None, :], 0), axis=1)

    return jnp.concatenate([own, sib, core[None], piece_of(own), piece_of(sib)]).astype(jnp.int32)


class Weight:
    def __init__(self, table, pieces, start=0, size=None):
        self.table, self.pieces = table, pieces
        self.start, self.size = start, size or pieces[0].shape[2]

    def columns(self, start, size):
        return Weight(self.table, self.pieces, self.start + start, size)

    @property
    def shape(self):
        n_rows, n_z, _, _ = sizes()
        return (n_rows, n_z, 2, self.pieces[0].shape[1], self.size)

    def specs(self):
        return [pl.BlockSpec(memory_space=pl.ANY)] * len(self.pieces)

    def scratch(self):
        return [
            pltpu.VMEM(self.shape, self.pieces[0].dtype),
            pltpu.SemaphoreType.DMA((len(self.pieces) + 1,)),
        ]

    def out_shape(self):
        return jax.ShapeDtypeStruct(self.shape, self.pieces[0].dtype)

    def load(self, table, pieces, out_ref, w_ref, sems):
        n_rows = len(pieces) // 2
        core = table[2 * n_rows]
        out = pltpu.make_async_copy(w_ref, out_ref, sems.at[2 * n_rows])
        if self.size != pieces[0].shape[2]:
            pieces = [p.at[:, :, pl.ds(self.start, self.size)] for p in pieces]

        @pl.when(pl.program_id(0) == 0)
        def _():
            copies = [
                pltpu.make_async_copy(
                    piece,
                    w_ref.at[table[i], :, core if i < n_rows else 1 - core],
                    sems.at[i],
                )
                for i, piece in enumerate(pieces)
            ]
            for c in copies:
                c.start()
            for c in copies:
                c.wait()
            out.start()

        @pl.when(pl.program_id(0) == pl.num_programs(0) - 1)
        def _():
            out.wait()


def gather_small(shard, uses=()):
    n_rows, n_z, row_bits, z_bits = sizes()
    row, z, core = place()
    uses = list(uses)

    def arrive(**move):
        other = exchange(held, **move)
        return after(other, uses.pop(0)) if uses else other

    held = shard
    for count, bit in enumerate(reversed(range(z_bits))):
        held = ordered(z >> bit & 1, held, arrive(z_mask=1 << bit), count)
    for count, bit in enumerate(reversed(range(row_bits))):
        held = ordered(row >> bit & 1, held, arrive(row_masks=(1 << bit, 1 << bit)), count)
    held = ordered(core, held, arrive(swap_core=True), row_bits + z_bits)
    return held.reshape((n_rows * n_z * 2,) + shard.shape)


def scatter_small(blocks, dtype, starts=()):
    n_rows, n_z, row_bits, z_bits = sizes()
    row, z, core = place()
    held = blocks.reshape((2,) * (row_bits + z_bits + 1) + blocks.shape[1:])
    starts = list(starts)

    def halve(held, axis, bit, **move):
        send = lax.dynamic_index_in_dim(held, 1 - bit, axis, keepdims=False).astype(dtype)
        keep = lax.dynamic_index_in_dim(held, bit, axis, keepdims=False)
        start = starts.pop(0) if starts else ()
        return keep.astype(f32) + transfer(send, start, **move).astype(f32)

    held = halve(held, row_bits + z_bits, core, swap_core=True)
    for bit in range(row_bits):
        held = halve(held, row_bits - 1 - bit, row >> bit & 1, row_masks=(1 << bit, 1 << bit))
    for bit in range(z_bits):
        held = halve(held, z_bits - 1 - bit, z >> bit & 1, z_mask=1 << bit)
    return held


def gather_relative(block):
    n_rows, n_z, _, _ = sizes()
    held = jnp.stack([block] + [exchange(block, z_mask=m) for m in range(1, n_z)])
    held = jnp.stack([held] + [exchange(held, row_masks=(m, m)) for m in range(1, n_rows)])
    return jnp.stack([held, exchange(held, swap_core=True)])


def scatter_relative(blocks, dtype, use=()):
    n_rows, n_z, _, _ = sizes()

    def step(held, count, move, use=()):
        parts = [after(exchange(held[m].astype(dtype), **move(m)), *use) for m in range(1, count)]
        total = held[0]
        for part in parts:
            total = total + part.astype(f32)
        return total

    held = step(blocks, 2, lambda m: dict(swap_core=True), use)
    held = step(held, n_rows, lambda m: dict(row_masks=(m, m)))
    return step(held, n_z, lambda m: dict(z_mask=m))


def relative_order():
    n_rows, n_z, _, _ = sizes()
    row, z, core = place()
    at = jnp.arange(n_rows * n_z * 2)
    there_core = core ^ at // (n_rows * n_z)
    there_row = row ^ at // n_z % n_rows
    return ((there_row * n_z + (z ^ at % n_z)) * 2 + there_core).astype(jnp.int32)


class Scatter:
    def __init__(self, send, keep, wide=False):
        _, _, row_bits, z_bits = sizes()
        flat = lambda x: x.reshape((-1,) + x.shape[-2:])
        self.send, self.keep = flat(send), flat(keep)
        self.stages = [("row", j) for j in reversed(range(row_bits))]
        self.stages += [("z", b) for b in range(z_bits)]
        self.wide = self.stages[-1] if wide else None

    def receive(self):
        kind, at = self.stages.pop(0)
        move = dict(row_masks=stage_masks(at)) if kind == "row" else dict(z_mask=1 << at)
        return exchange(self.send, **move)

    def step(self, *use):
        _, z, _ = place()
        parts = (self.keep, after(self.receive(), *use))
        if not self.stages:
            return (parts[0] + parts[1].astype(f32))[0]
        kind, at = self.stages[0]
        half = self.keep.shape[0] // 2
        if kind == "row":
            pick = lambda x, other: x[half:] if other else x[:half]
        else:
            mine = z >> at & 1
            parts = tuple(x.reshape((half, 2) + x.shape[1:]) for x in parts)
            pick = lambda x, other: lax.dynamic_index_in_dim(
                x, 1 - mine if other else mine, 1, keepdims=False
            )
        total = lambda other: pick(parts[0], other) + pick(parts[1], other).astype(f32)
        self.send, self.keep = total(True), total(False)
        if self.stages[0] != self.wide:
            self.send = self.send.astype(bf16)
        return self.send

    def merge(self, other):
        self.send = jnp.concatenate([self.send, other.send], axis=-1)
        self.keep = jnp.concatenate([self.keep, other.keep], axis=-1)
        return self

    def finish(self, *use):
        while self.stages:
            out = self.step(*use)
        return out


def head_slices():
    return ((0, PROJ_A), (PROJ_A, PROJ_B), (PROJ_A + PROJ_B, PROJ_C))


LANES = 128


def whole_spec(shape):
    return pl.BlockSpec(
        shape, lambda *_: (0,) * len(shape), pipeline_mode=pl.Buffered(buffer_count=1)
    )


def row_spec(rows, width):
    return pl.BlockSpec((rows, width), lambda i, *_: (i, 0))


def col_spec(rows, width):
    return pl.BlockSpec((rows, width), lambda i, *_: (0, i))


def like(shape, dtype):
    return jax.ShapeDtypeStruct(shape, dtype)


def call(
    kernel, name, grid, in_specs, out_specs, out_shape, flops, moved, scratch=(), table=None, wait=(), aliases=None
):
    first = len(in_specs) + (0 if table is None else 1)
    in_specs = list(in_specs) + [pl.BlockSpec(memory_space=pl.ANY)] * len(wait)

    def body(*refs):
        kernel(*refs[:first], *refs[first + len(wait) :])

    run = pl.pallas_call(
        body,
        grid_spec=pltpu.PrefetchScalarGridSpec(
            num_scalar_prefetch=0 if table is None else 1,
            grid=grid,
            in_specs=in_specs,
            out_specs=out_specs,
            scratch_shapes=list(scratch),
        ),
        out_shape=out_shape,
        input_output_aliases=aliases or {},
        compiler_params=pltpu.CompilerParams(vmem_limit_bytes=56 << 20),
        cost_estimate=pl.CostEstimate(
            flops=int(flops), bytes_accessed=int(moved), transcendentals=0
        ),
        name=name,
    )
    return lambda *operands: run(*operands, *wait)


def swap_halves(x):
    lane = lax.broadcasted_iota(jnp.int32, x.shape, 1)
    half = HEAD_DIM // 2
    return jnp.where(
        lane % HEAD_DIM < half, pltpu.roll(x, LANES - half, 1), pltpu.roll(x, half, 1)
    )


QKV_TILE = 1024


def qkv_kernel(weight, table, x_ref, b_ref, cos_ref, sin_ref, *refs):
    pieces, (o_ref, w_out, w_ref, sems) = refs[:-4], refs[-4:]
    weight.load(table, pieces, w_out, w_ref, sems)
    tile = pl.program_id(0)
    per_part = D // QKV_TILE
    cols = pl.ds(pl.multiple_of(tile * QKV_TILE, LANES), QKV_TILE)
    w = w_ref[:, :, :, :, cols].reshape(x_ref.shape[1], QKV_TILE)
    bias = b_ref[...]

    @pl.when(tile < 2 * per_part)
    def _():
        scale = jnp.where(tile < per_part, HEAD_DIM**-0.5, 1.0)
        for row in range(0, x_ref.shape[0], TILE):
            rows = slice(row, row + TILE)
            acc = contract(x_ref[rows, :], w, 1, 0) + bias
            cosine = cos_ref[rows, :] * scale
            sine = sin_ref[rows, :] * scale
            for j in range(QKV_TILE // LANES):
                at = slice(j * LANES, (j + 1) * LANES)
                a = acc[:, at]
                o_ref[rows, at] = (a * cosine + swap_halves(a) * sine).astype(bf16)

    @pl.when(tile >= 2 * per_part)
    def _():
        for row in range(0, x_ref.shape[0], TILE):
            rows = slice(row, row + TILE)
            o_ref[rows, :] = (contract(x_ref[rows, :], w, 1, 0) + bias).astype(bf16)


def project_qkv(x, w, b, cosine, sine, wait=()):
    t = x.shape[0]
    any_out = pl.BlockSpec(memory_space=pl.ANY)
    return call(
        functools.partial(qkv_kernel, w),
        "project_qkv",
        (3 * D // QKV_TILE,),
        [
            whole_spec((t, D)),
            pl.BlockSpec((1, QKV_TILE), lambda i, _: (0, i)),
            whole_spec((t, LANES)),
            whole_spec((t, LANES)),
        ]
        + w.specs(),
        [col_spec(t, QKV_TILE), any_out],
        [like((t, 3 * D), bf16), w.out_shape()],
        6 * t * D * D,
        20 * t * D,
        w.scratch(),
        table=w.table,
        wait=wait,
    )(w.table, x, b, cosine, sine, *w.pieces)


TILE = 256


def normalized(v):
    mean = jnp.mean(v, axis=1, keepdims=True)
    centered = v - mean
    rstd = lax.rsqrt(jnp.mean(centered * centered, axis=1, keepdims=True) + eps_norm)
    return centered * rstd, rstd


def norm_back(g, hat, rstd, gain):
    y = g * gain
    return rstd * (
        y - jnp.mean(y, axis=1, keepdims=True) - hat * jnp.mean(y * hat, axis=1, keepdims=True)
    )


def add_up(ref, value):
    @pl.when(pl.program_id(0) == 0)
    def _():
        ref[...] = jnp.zeros_like(ref)

    ref[...] += value


def column_sum(x):
    return jnp.sum(x, axis=0, keepdims=True)


def out_norm_kernel(weight, table, a_ref, b_ref, x_ref, gain_ref, bias_ref, *refs):
    hat_ref, rstd_ref, low_ref, w_out, w_ref, sems = refs[-6:]
    weight.load(table, refs[:-6], w_out, w_ref, sems)
    w = w_ref[...].reshape(a_ref.shape[1], -1)
    v = x_ref[...].astype(f32) + contract(a_ref[...], w, 1, 0) + b_ref[...]
    hat, rstd = normalized(v)
    hat_ref[...] = hat
    rstd_ref[...] = jnp.broadcast_to(rstd, rstd_ref.shape)
    low_ref[...] = (hat * gain_ref[...] + bias_ref[...]).astype(bf16)


def out_norm(attended, w, b, x, gain, bias, wait=()):
    t = x.shape[0]
    vec = whole_spec((1, D))
    return call(
        functools.partial(out_norm_kernel, w),
        "out_norm",
        (t // TILE,),
        [row_spec(TILE, D), vec, row_spec(TILE, D), vec, vec] + w.specs(),
        [row_spec(TILE, D), row_spec(TILE, LANES), row_spec(TILE, D), pl.BlockSpec(memory_space=pl.ANY)],
        [like((t, D), f32), like((t, LANES), f32), like((t, D), bf16), w.out_shape()],
        2 * t * D * D,
        12 * t * D,
        w.scratch(),
        table=w.table,
        wait=wait,
    )(w.table, attended, b, x, gain, bias, *w.pieces)


UP_TILE = 1024
CHUNK = 32


def gelu_pair(x):
    phi = 0.5 + 0.5 * lax.erf(x * 0.5**0.5)
    return x * phi, phi + x * jnp.exp(x * x * -0.5) * (2.0 * jnp.pi) ** -0.5


def up_kernel(weight, table, h_ref, b_ref, *refs):
    act_ref, slope_ref, w_out, acc_ref, w_ref, sems = refs[-6:]
    out = w_out.at[:, :, :, :, pl.ds(weight.start, weight.size)]
    weight.load(table, refs[: len(weight.pieces)], out, w_ref, sems)
    cols = pl.ds(pl.multiple_of(pl.program_id(0) * UP_TILE, LANES), UP_TILE)
    acc_ref[...] = contract(h_ref[...], w_ref[:, :, :, :, cols].reshape(-1, UP_TILE), 1, 0)
    bias = b_ref[...]

    def step(i, _):
        rows = pl.ds(pl.multiple_of(i * CHUNK, CHUNK), CHUNK)
        act, slope = gelu_pair(acc_ref[rows, :] + bias)
        act_ref[rows, :] = act.astype(bf16)
        slope_ref[rows, :] = slope.astype(bf16)
        return 0

    lax.fori_loop(0, h_ref.shape[0] // CHUNK, step, 0)


def up_gelu(hidden, w, b, before=None, wait=()):
    t, ff = hidden.shape[0], w.size
    any_space = pl.BlockSpec(memory_space=pl.ANY)
    steps = ff // UP_TILE // 2
    first = 0 if before is None else steps
    before = [] if before is None else list(before)
    n_in = 3 + len(w.pieces)
    half = w.columns(first * UP_TILE, ff // 2)
    return call(
        functools.partial(up_kernel, half),
        "up_gelu",
        (steps,),
        [whole_spec((t, D)), pl.BlockSpec((1, UP_TILE), lambda i, _: (0, first + i))]
        + w.specs()
        + [any_space] * len(before),
        [pl.BlockSpec((t, UP_TILE), lambda i, _: (0, first + i))] * 2 + [any_space],
        [like((t, ff), bf16)] * 2 + [w.out_shape()],
        t * D * ff,
        2 * t * ff + D * ff,
        [pltpu.VMEM((t, UP_TILE), f32)] + half.scratch(),
        table=w.table,
        wait=wait,
        aliases={n_in + i: i for i in range(len(before))},
    )(w.table, hidden, b, *w.pieces, *before)


def head_masks(width):
    lane = lax.broadcasted_iota(jnp.int32, (1, width), 1)
    return [(lane >= start) & (lane < start + size) for start, size in head_slices()]


def head_lanes():
    for start, size in head_slices():
        low = start // LANES * LANES
        high = -(-(start + size) // LANES) * LANES
        lane = lax.broadcasted_iota(jnp.int32, (1, high - low), 1) + low
        yield slice(low, high), (lane >= start) & (lane < start + size)


def head_sums(x):
    out = jnp.zeros_like(x)
    for mask in head_masks(x.shape[1]):
        total = jnp.sum(jnp.where(mask, x, 0.0), axis=1, keepdims=True)
        out = jnp.where(mask, total, out)
    return out


def down_norm_kernel(
    weight, proj, table, a_ref, b_ref, hat1_ref, gain1_ref, bias1_ref, gain_ref, bias_ref, *refs
):
    n = len(weight.pieces)
    hat_ref, rstd_ref, low_ref, raw_ref, vec_ref = refs[-11:-6]
    w_out, p_out, w_ref, w_sems, p_ref, p_sems = refs[-6:]
    proj.load(table, refs[n : 2 * n], p_out, p_ref, p_sems)
    weight.load(table, refs[:n], w_out, w_ref, w_sems)
    w = w_ref[...].reshape(a_ref.shape[1], -1)
    p = p_ref[...].reshape(w.shape[1], -1)
    for row in range(0, a_ref.shape[0], TILE):
        rows = slice(row, row + TILE)
        hidden = hat1_ref[rows, :] * gain1_ref[...] + bias1_ref[...]
        hat, rstd = normalized(hidden + contract(a_ref[rows, :], w, 1, 0) + b_ref[...])
        hat_ref[rows, :] = hat
        rstd_ref[rows, :] = jnp.broadcast_to(rstd, (TILE, LANES))
        low = (hat * gain_ref[...] + bias_ref[...]).astype(bf16)
        low_ref[rows, :] = low
        raw = contract(low, p, 1, 0)
        raw_ref[rows, :] = raw
        vec_ref[rows, :] = (raw * lax.rsqrt(head_sums(raw * raw) + eps_vec)).astype(bf16)


def down_norm(act, w, b, hat1, gain1, bias1, gain, bias, proj, wait=()):
    t, ff = act.shape
    e = proj.size
    vec = whole_spec((1, D))
    any_space = pl.BlockSpec(memory_space=pl.ANY)
    return call(
        functools.partial(down_norm_kernel, w, proj),
        "down_norm",
        (t // TILE,),
        [row_spec(TILE, ff), vec, row_spec(TILE, D), vec, vec, vec, vec] + w.specs() + proj.specs(),
        [
            row_spec(TILE, D),
            row_spec(TILE, LANES),
            row_spec(TILE, D),
            row_spec(TILE, e),
            row_spec(TILE, e),
            any_space,
            any_space,
        ],
        [
            like((t, D), f32),
            like((t, LANES), f32),
            like((t, D), bf16),
            like((t, e), f32),
            like((t, e), bf16),
            w.out_shape(),
            proj.out_shape(),
        ],
        2 * t * D * ff,
        20 * t * D,
        w.scratch() + proj.scratch(),
        table=w.table,
        wait=wait,
    )(w.table, act, b, hat1, gain1, bias1, gain, bias, *w.pieces, *proj.pieces)


def head_back_kernel(
    has_query, g_ref, raw_ref, proj_ref, hat_ref, rstd_ref, gain_ref, *refs
):
    grad_ref, branch_ref, raw_out, sums_ref = refs[-4:]
    g, raw = g_ref[...], raw_ref[...]
    if has_query:
        q = refs[0][...]
        g = g + jnp.concatenate([q, jnp.zeros((g.shape[0] - q.shape[0], q.shape[1]), f32)], axis=0)
    scale = lax.rsqrt(head_sums(raw * raw) + eps_vec)
    y = raw * scale
    raw_grad = (scale * (g - y * head_sums(y * g))).astype(bf16)
    result_grad = contract(raw_grad, proj_ref[...], 1, 1)
    hat = hat_ref[...]
    grad = norm_back(result_grad, hat, rstd_ref[:, :1], gain_ref[...])
    branch = grad.astype(bf16)
    grad_ref[...] = grad
    branch_ref[...] = branch
    raw_out[...] = raw_grad
    add_up(
        sums_ref,
        jnp.concatenate(
            [
                column_sum(result_grad * hat),
                column_sum(result_grad),
                column_sum(branch.astype(f32)),
            ],
            axis=0,
        ),
    )


def head_back(g, raw, proj, hat, rstd, gain, query=None, before=(), wait=()):
    t, e = raw.shape
    first, steps = (1, t // TILE - 1) if query is None else (0, 1)
    extra = [] if query is None else [query]
    rows = lambda width: pl.BlockSpec((TILE, width), lambda i, *_: (first + i, 0))
    return call(
        functools.partial(head_back_kernel, query is not None),
        "head_back",
        (steps,),
        [
            rows(e),
            rows(e),
            whole_spec((D, e)),
            rows(D),
            rows(LANES),
            whole_spec((1, D)),
        ]
        + [whole_spec(x.shape) for x in extra]
        + [pl.BlockSpec(memory_space=pl.ANY)] * len(before),
        [rows(D), rows(D), rows(e), whole_spec((3, D))],
        [like((t, D), f32), like((t, D), bf16), like((t, e), bf16), like((3, D), f32)],
        2 * steps * TILE * D * e,
        16 * steps * TILE * D,
        wait=wait,
        aliases={6 + len(extra) + i: i for i in range(len(before))},
    )(g, raw, proj, hat, rstd, gain, *extra, *before)


def act_back_kernel(g_ref, w_ref, slope_ref, o_ref, sum_ref):
    total = jnp.zeros(sum_ref.shape, f32)
    for row in range(0, g_ref.shape[0], TILE):
        rows = slice(row, row + TILE)
        back = contract(g_ref[rows, :], w_ref[...], 1, 1) * slope_ref[rows, :].astype(f32)
        back = back.astype(bf16)
        o_ref[rows, :] = back
        total = total + column_sum(back.astype(f32))
    sum_ref[...] = total


def act_back(branch, w, slope, wait=()):
    t, ff = slope.shape
    return call(
        act_back_kernel,
        "act_back",
        (ff // UP_TILE,),
        [whole_spec((t, D)), row_spec(UP_TILE, D), col_spec(t, UP_TILE)],
        [col_spec(t, UP_TILE), col_spec(1, UP_TILE)],
        [like((t, ff), bf16), like((1, ff), f32)],
        2 * t * D * ff,
        4 * t * ff + 2 * D * ff,
        wait=wait,
    )(branch, w, slope)


def hidden_back_kernel(
    g_ref, w_ref, resid_ref, hat_ref, rstd_ref, gain_ref, wout_ref,
    grad_ref, out_ref, att_ref, sums_ref,
):
    for row in range(0, g_ref.shape[0], TILE):
        rows = slice(row, row + TILE)
        hidden_grad = resid_ref[rows, :] + contract(g_ref[rows, :], w_ref[...], 1, 1)
        hat = hat_ref[rows, :]
        grad = norm_back(hidden_grad, hat, rstd_ref[rows, :1], gain_ref[...])
        low = grad.astype(bf16)
        grad_ref[rows, :] = grad
        out_ref[rows, :] = low
        att_ref[rows, :] = contract(low, wout_ref[...], 1, 1).astype(bf16)
        sums = [column_sum(hidden_grad * hat), column_sum(hidden_grad), column_sum(low.astype(f32))]
        if row == 0:
            add_up(sums_ref, jnp.concatenate(sums, axis=0))
        else:
            sums_ref[...] += jnp.concatenate(sums, axis=0)


def hidden_back(inner, w, resid, hat, rstd, gain, w_out, wait=()):
    t, ff = inner.shape
    return call(
        hidden_back_kernel,
        "hidden_back",
        (t // TILE,),
        [
            row_spec(TILE, ff),
            whole_spec((D, ff)),
            row_spec(TILE, D),
            row_spec(TILE, D),
            row_spec(TILE, LANES),
            whole_spec((1, D)),
            whole_spec((D, D)),
        ],
        [row_spec(TILE, D)] * 3 + [whole_spec((3, D))],
        [like((t, D), f32), like((t, D), bf16), like((t, D), bf16), like((3, D), f32)],
        2 * t * D * ff + 2 * t * D * D,
        2 * t * ff + 24 * t * D,
        wait=wait,
    )(inner, w, resid, hat, rstd, gain, w_out)


def input_back_kernel(groups, *refs):
    g_refs, (w_ref, resid_ref, o_ref) = refs[:groups], refs[groups:]
    total = resid_ref[...]
    for part in range(3):
        for i, g_ref in enumerate(g_refs):
            width = g_ref.shape[2]
            at = part * D + i * width
            total = total + contract(g_ref[part], w_ref[:, at : at + width], 1, 1)
    o_ref[...] = total


def input_back(grads, w, resid, wait=()):
    t = resid.shape[0]
    return call(
        functools.partial(input_back_kernel, len(grads)),
        "input_back",
        (t // TILE,),
        [pl.BlockSpec((3, TILE, g.shape[2]), lambda i: (0, i, 0)) for g in grads]
        + [whole_spec((D, 3 * D)), row_spec(TILE, D)],
        row_spec(TILE, D),
        like((t, D), f32),
        6 * t * D * D,
        20 * t * D,
        wait=wait,
    )(*grads, w, resid)


def block_masks(n_devices, width):
    n = width * n_devices
    column = lax.broadcasted_iota(jnp.int32, (n_devices, n), 1)
    first = lax.broadcasted_iota(jnp.int32, (n_devices, n), 0) * width
    mine = (column >= first) & (column < first + width)
    at = lax.broadcasted_iota(jnp.int32, (1, n), 1) % width
    return mine, at


def unpack_kernel(n_devices, widths, p_ref, *o_refs):
    start = 0
    for width, o_ref in zip(widths, o_refs):
        mine, at = block_masks(n_devices, width)
        copies = (at == lax.broadcasted_iota(jnp.int32, (width, at.shape[1]), 0)).astype(bf16)
        spread = contract(p_ref[:, start : start + width], copies, 1, 0)
        o_ref[...] = column_sum(jnp.where(mine, spread, 0.0))
        start += width


def unpack(packed, widths, wait=()):
    n_devices = packed.shape[0]
    return call(
        functools.partial(unpack_kernel, n_devices, widths),
        "unpack",
        (1,),
        [whole_spec(packed.shape)],
        [whole_spec((1, w * n_devices)) for w in widths],
        [like((1, w * n_devices), f32) for w in widths],
        10**8,
        10**5,
        wait=wait,
    )(packed)


def pack_kernel(n_devices, widths, *refs):
    o_ref = refs[-1]
    o_ref[...] = jnp.zeros_like(o_ref)
    start = 0
    for width, ref in zip(widths, refs):
        mine, at = block_masks(n_devices, width)
        copies = (at == lax.broadcasted_iota(jnp.int32, (width, at.shape[1]), 0)).astype(bf16)
        rest = jnp.where(mine, ref[...], 0.0)
        total = jnp.zeros((n_devices, width), f32)
        for _ in range(3):
            term = rest.astype(bf16)
            total = total + contract(term, copies, 1, 1)
            rest = rest - term.astype(f32)
        o_ref[:, start : start + width] = total
        start += width


def pack(vectors, n_devices, wait=()):
    widths = [v.shape[1] // n_devices for v in vectors]
    total = sum(widths)
    total += -total % LANES
    return call(
        functools.partial(pack_kernel, n_devices, widths),
        "pack",
        (1,),
        [whole_spec(v.shape) for v in vectors],
        whole_spec((n_devices, total)),
        like((n_devices, total), f32),
        10**8,
        10**5,
        wait=wait,
    )(*vectors)


def halves_kernel(n_rows, n_z, table, own_in, sib_in, own_ref, sib_ref):
    core = table[2 * n_rows]
    for a_ref, o_ref, side in ((own_in, own_ref, core), (sib_in, sib_ref, 1 - core)):
        t, k = a_ref.shape
        x = a_ref[...].T.reshape(n_z, 2, k // (2 * n_z), t)
        o_ref[...] = jnp.where(side == 0, x[:, 0], x[:, 1]).reshape(o_ref.shape)


def halves(table, a, n_rows, n_z, wait=()):
    t, k = a.shape
    block = k // n_rows
    out = pl.BlockSpec((block // 2, t), lambda i, _: (i, 0))
    return call(
        functools.partial(halves_kernel, n_rows, n_z),
        "halves",
        (n_rows,),
        [
            pl.BlockSpec((t, block), lambda i, tab: (0, tab[i])),
            pl.BlockSpec((t, block), lambda i, tab: (0, tab[n_rows + i])),
        ],
        [out, out],
        [like((k // 2, t), bf16)] * 2,
        10**6,
        8 * t * k,
        table=table,
        wait=wait,
    )(table, a, a)


def pick_columns(table, offset, n_rows, n_z, a_ref, picked):
    t, k = a_ref.shape
    block = k // n_rows
    half = block // 2
    r = half // n_z
    core = table[2 * n_rows]
    side = core if offset == 0 else 1 - core
    if r % LANES:
        m = lax.broadcasted_iota(jnp.int32, (block, half), 1)
        source = (m // r) * (2 * r) + side * r + m % r
        choose = (lax.broadcasted_iota(jnp.int32, (block, half), 0) == source).astype(bf16)
    for piece in range(n_rows):
        first = table[offset + piece] * block
        if r % LANES:
            x = a_ref[:, pl.ds(pl.multiple_of(first, LANES), block)]
            picked[:, piece * half : (piece + 1) * half] = contract(x, choose, 1, 0).astype(bf16)
        else:
            for z in range(n_z):
                x = a_ref[:, pl.ds(pl.multiple_of(first + (2 * z + side) * r, LANES), r)]
                at = piece * half + z * r
                picked[:, at : at + r] = x


def weight_kernel(picks, offset, n_rows, n_z, table, *refs):
    pairs = len(picks)
    ins, refs = refs[: 2 * pairs], refs[2 * pairs :]
    count = sum(picks)
    refs, picked = refs[: len(refs) - count], list(refs[len(refs) - count :])

    if count:

        @pl.when(pl.program_id(0) == 0)
        def _():
            into = list(picked)
            for pick, a_ref in zip(picks, ins[::2]):
                if pick:
                    pick_columns(table, offset, n_rows, n_z, a_ref, into.pop(0))

    totals = []
    for pick, a_ref, b_ref in zip(picks, ins[::2], ins[1::2]):
        b = b_ref[...]
        b = b.reshape(b.shape[-2:])
        if pick:
            totals.append(contract(picked.pop(0)[...], b, 0, 0))
        else:
            totals.append(contract(a_ref[...], b, 1, 0))
    total = totals[0] if pairs == 1 else jnp.concatenate(totals, axis=1)
    if len(refs) == 1:
        refs[0][...] = total.reshape(refs[0].shape).astype(refs[0].dtype)
    else:
        other, send_ref, keep_ref = refs
        total = total.reshape(other.shape) + other[...].astype(f32)
        half = keep_ref.shape[0]
        send_ref[...] = total[half:].astype(send_ref.dtype)
        keep_ref[...] = total[:half]


def weight_half(name, table, operands, n_rows, n_z, tile, other=None, other_type=bf16, wait=()):
    own = other is not None
    picks = [not isinstance(a, tuple) for a, _ in operands]
    lefts = [a[0 if own else 1] if isinstance(a, tuple) else a for a, _ in operands]
    rights = [b for _, b in operands]
    t = rights[0].shape[-2]
    k = lefts[0].shape[1] if picks[0] else 2 * lefts[0].shape[0]
    r = k // (n_rows * n_z * 2)
    if len(operands) == 1:
        b = rights[0]
        per_part = b.shape[-1] // tile
        n = b.shape[-1] * (b.shape[0] if b.ndim == 3 else 1)
        if b.ndim == 3:
            b_specs = [pl.BlockSpec((1, t, tile), lambda i, _: (i // per_part, 0, i % per_part))]
        else:
            b_specs = [col_spec(t, tile)]
    else:
        n = tile = sum(b.shape[1] for b in rights)
        b_specs = [whole_spec(b.shape) for b in rights]
    specs, arrays = [], []
    for a, b, b_spec in zip(lefts, rights, b_specs):
        specs += [whole_spec(a.shape), b_spec]
        arrays += [a, b]

    def block(rows):
        return pl.BlockSpec((rows, n_z, r, tile), lambda i, _: (0, 0, 0, i))

    def shape(rows, dtype):
        return like((rows, n_z, r, n), dtype)

    return call(
        functools.partial(weight_kernel, picks, 0 if own else n_rows, n_rows, n_z),
        name,
        (n // tile,),
        specs + ([block(n_rows)] if own else []),
        [block(n_rows // 2)] * 2 if own else block(n_rows),
        [shape(n_rows // 2, bf16), shape(n_rows // 2, f32)] if own else shape(n_rows, other_type),
        t * k * n,
        2 * t * (k + n) + 3 * k * n,
        [pltpu.VMEM((t, k // 2), bf16) for pick in picks if pick],
        table=table,
        wait=wait,
    )(table, *arrays, *([other] if own else []))


WINDOWS = (256, -(-(DMOST + 15) // 32) * 32)
NEG = -1e30


def contract(a, b, ca, cb):
    return lax.dot_general(a, b, (((ca,), (cb,)), ((), ())), preferred_element_type=f32)


def document_table(lengths):
    at = jnp.arange(DPR)
    starts = QPR * QLEN + jnp.sum(jnp.where(at[:, None] < at[None, :], lengths[:, None], 0), axis=0)
    need = starts % 16 + lengths
    ahead = (need[:, None] > need[None, :]) | ((need[:, None] == need[None, :]) & (at[:, None] < at[None, :]))
    rank = jnp.sum(ahead.astype(jnp.int32), axis=0)
    order = rank[None, :] == at[:, None]
    pick = lambda x: jnp.sum(jnp.where(order, x[None, :], 0), axis=1)
    wide = jnp.sum((need > WINDOWS[0]).astype(jnp.int32))
    return jnp.concatenate([pick(starts), pick(lengths), wide[None]]).astype(jnp.int32)


def for_documents(doc_ref, row_len, step):
    for wide in range(1, DPR):

        @pl.when(doc_ref[2 * DPR] == wide)
        def _():
            for d in range(DPR):
                window = WINDOWS[1] if d < wide else WINDOWS[0]
                start, size = doc_ref[d], doc_ref[DPR + d]
                base = pl.multiple_of(jnp.minimum((start // 16) * 16, row_len - window), 16)
                step(window, base, start - base, start - base + size)


def head_pair(x):
    lane = lax.broadcasted_iota(jnp.int32, x.shape, 1)
    zero = jnp.zeros_like(x)
    return jnp.concatenate(
        [jnp.where(lane < HEAD_DIM, x, zero), jnp.where(lane < HEAD_DIM, zero, x)], axis=0
    )


def pair_heads(x):
    n = x.shape[0] // 2
    lane = lax.broadcasted_iota(jnp.int32, (n, x.shape[1]), 1)
    return jnp.where(lane < HEAD_DIM, x[:n], x[n:])


def inside(n, low, high, axis):
    shape = (n, 1) if axis == 0 else (1, n)
    at = lax.broadcasted_iota(jnp.int32, shape, axis)
    return (at >= low) & (at < high)


def attend(q, k, v, low, high):
    s = contract(head_pair(q), k, 1, 1)
    s = s + jnp.where(inside(k.shape[0], low, high, 1), 0.0, NEG)
    p = jnp.exp(s - jnp.max(s, axis=1, keepdims=True))
    total = jnp.sum(p, axis=1, keepdims=True)
    return pair_heads(contract(p.astype(bf16), v, 1, 0) / total)


def attention_kernel(len_ref, q_ref, k_ref, v_ref, o_ref):
    def step(window, base, low, high):
        w = pl.ds(base, window)
        o = attend(q_ref[w, :], k_ref[w, :], v_ref[w, :], low, high)
        keep = inside(window, low, high, 0)
        o_ref[w, :] = jnp.where(keep, o, o_ref[w, :].astype(f32)).astype(bf16)

    for_documents(len_ref, q_ref.shape[0], step)
    o_ref[:QLEN, :] = attend(q_ref[:QLEN, :], k_ref[:128, :], v_ref[:128, :], 0, QLEN).astype(bf16)


def qkv_specs(t):
    per_part = D // LANES
    return [
        pl.BlockSpec((t, LANES), lambda i, _, p=p: (0, p * per_part + i)) for p in range(3)
    ]


def attention(lengths, qkv, wait=()):
    t = qkv.shape[0]
    return call(
        attention_kernel,
        "attention",
        (HEADS // 2,),
        qkv_specs(t),
        col_spec(t, LANES),
        like((t, D), bf16),
        2 * 10**10,
        8 * t * D,
        table=lengths,
        wait=wait,
    )(lengths, qkv, qkv, qkv)


def attend_back(q, k, v, g, low, high):
    n = q.shape[0]
    g = jnp.where(inside(n, low, high, 0), g, jnp.zeros_like(g))
    qq = head_pair(q)
    gg = head_pair(g)
    st = contract(k, qq, 1, 1)
    st = st + jnp.where(inside(k.shape[0], low, high, 0), 0.0, NEG)
    p = jnp.exp(st - jnp.max(st, axis=0, keepdims=True))
    p = p * (1.0 / jnp.sum(p, axis=0, keepdims=True))
    dp = contract(v, gg, 1, 1)
    delta = jnp.sum(p * dp, axis=0, keepdims=True)
    ds = (p * (dp - delta)).astype(bf16)
    dv = contract(p.astype(bf16), gg, 1, 0)
    dk = contract(ds, qq, 1, 0)
    dq = contract(ds, k, 0, 0) * (HEAD_DIM**-0.5)
    return pair_heads(dq), dk, dv


def attention_back_kernel(len_ref, q_ref, k_ref, v_ref, g_ref, cos_ref, sin_ref, o_ref, sum_ref, *sums):
    row_len = q_ref.shape[0]
    for ref in sums:
        ref[...] = jnp.zeros_like(ref)
    parts = attend_back(
        q_ref[:QLEN, :], k_ref[:128, :], v_ref[:128, :], g_ref[:QLEN, :], 0, QLEN
    )
    for ref, x in zip(sums, parts):
        ref[: x.shape[0], :] = x

    def step(window, base, low, high):
        w = pl.ds(base, window)
        parts = attend_back(q_ref[w, :], k_ref[w, :], v_ref[w, :], g_ref[w, :], low, high)
        for ref, x in zip(sums, parts):
            ref[w, :] += x

    for_documents(len_ref, row_len, step)
    cosine, sine = cos_ref[...], sin_ref[...]
    for part in range(3):
        x = sums[part][...]
        if part < 2:
            x = x * cosine - swap_halves(x) * sine
        x = x.astype(bf16)
        o_ref[part] = x
        sum_ref[part] = column_sum(x.astype(f32))


def attention_back(lengths, qkv, g, cosine, sine, group, groups, wait=()):
    t = qkv.shape[0]
    table = whole_spec((t, LANES))
    pairs = HEADS // 2 // groups
    first = group * pairs
    per_part = D // LANES
    specs = [
        pl.BlockSpec((t, LANES), lambda i, _, p=p: (0, p * per_part + first + i)) for p in range(3)
    ]
    return call(
        attention_back_kernel,
        "attention_back",
        (pairs,),
        specs + [pl.BlockSpec((t, LANES), lambda i, _: (0, first + i)), table, table],
        [
            pl.BlockSpec((3, t, LANES), lambda i, _: (0, 0, i)),
            pl.BlockSpec((3, 1, LANES), lambda i, _: (0, 0, i)),
        ],
        [like((3, t, D // groups), bf16), like((3, 1, D // groups), f32)],
        5 * 10**10 // groups,
        14 * t * D // groups,
        [pltpu.VMEM((t, LANES), f32)] * 3,
        table=lengths,
        wait=wait,
    )(lengths, qkv, qkv, qkv, g, cosine, sine)


SCORE_TILE = 256


def doc_inside(doc_ref, d):
    return doc_ref[...] == d


def score_exps(docs, queries, mask):
    picked = jnp.where(mask, docs, jnp.zeros_like(docs))
    return picked, jnp.exp(contract(picked, queries, 1, 1) * score_scale)


def split_dot(hot, x):
    high = x.astype(bf16)
    rest = (x - high.astype(f32)).astype(bf16)
    return contract(hot, high, 1, 0) + contract(hot, rest, 1, 0)


def score_kernel(
    doc_ref, query_ref, id_ref, hot_ref, count_ref, pos_ref, sum_ref, score_ref, stat_ref
):
    docs = doc_ref[...]
    n_queries = score_ref.shape[2]
    live = lax.broadcasted_iota(jnp.int32, (8, n_queries), 0) < DPR
    for head, (lanes, mask) in enumerate(head_lanes()):
        scores = jnp.zeros((8, n_queries), f32)
        for at in range(0, query_ref.shape[0], SCORE_TILE):
            _, e = score_exps(docs[:, lanes], query_ref[at : at + SCORE_TILE, lanes], mask)
            total = split_dot(hot_ref[...], e)
            sum_ref[head, :, at : at + SCORE_TILE] = total
            smooth = jnp.log(total) - count_ref[:, :1]
            query = lax.broadcasted_iota(jnp.int32, (SCORE_TILE, n_queries), 1)
            hot = (id_ref[at : at + SCORE_TILE, :] == query).astype(f32)
            scores += lax.dot_general(
                jnp.where(lax.broadcasted_iota(jnp.int32, smooth.shape, 0) < DPR, smooth, 0.0),
                hot,
                (((1,), (0,)), ((), ())),
                precision=highest,
                preferred_element_type=f32,
            )
        score_ref[head] = scores
        top = jnp.max(jnp.where(live, scores, NEG), axis=0, keepdims=True)
        den = column_sum(jnp.where(live, jnp.exp(scores - top), 0.0))
        pos = column_sum(jnp.where(live, scores * pos_ref[...], 0.0))
        stat_ref[head] = jnp.concatenate([top, den, pos], axis=0)


def score_grad_kernel(
    doc_ref, query_ref, id_ref, index_ref, sum_ref, score_ref, stat_ref, pos_ref, dq_ref, dd_ref
):
    docs = doc_ref[...]
    n_queries = score_ref.shape[2]
    dd_ref[...] = jnp.zeros_like(dd_ref)
    dq_ref[...] = jnp.zeros_like(dq_ref)
    index = index_ref[...]
    for head, (lanes, mask) in enumerate(head_lanes()):
        stats = stat_ref[head]
        grad = jnp.exp(score_ref[head] - stats[0:1]) / stats[1:2] - pos_ref[...]
        for at in range(0, query_ref.shape[0], SCORE_TILE):
            queries = query_ref[at : at + SCORE_TILE, lanes]
            picked, e = score_exps(docs[:, lanes], queries, mask)
            query = lax.broadcasted_iota(jnp.int32, (n_queries, SCORE_TILE), 0)
            hot = (id_ref[:, at : at + SCORE_TILE] == query).astype(f32)
            spread = lax.dot_general(
                grad, hot, (((1,), (0,)), ((), ())), precision=highest, preferred_element_type=f32
            )
            coef = score_scale * spread / sum_ref[head, :, at : at + SCORE_TILE]
            wide = jnp.zeros_like(e)
            for d in range(DPR):
                wide = jnp.where(index == d, coef[d : d + 1], wide)
            back = (e * wide).astype(bf16)
            dd_ref[:, lanes] += jnp.where(mask, contract(back, queries, 1, 0), 0.0)
            dq_ref[at : at + SCORE_TILE, lanes] += contract(back, picked, 0, 0)


def score_stats(docs, queries, ids, hot, counts, positive, wait=()):
    n, e = docs.shape
    n_tokens = queries.shape[0]
    n_queries = n_tokens // QLEN
    return call(
        score_kernel,
        "scores",
        (1,),
        [
            whole_spec((n, e)),
            whole_spec((n_tokens, e)),
            whole_spec((n_tokens, 1)),
            whole_spec((8, n)),
            whole_spec((8, LANES)),
            whole_spec((8, n_queries)),
        ],
        [
            whole_spec((3, 8, n_tokens)),
            whole_spec((3, 8, n_queries)),
            whole_spec((3, 3, n_queries)),
        ],
        [
            like((3, 8, n_tokens), f32),
            like((3, 8, n_queries), f32),
            like((3, 3, n_queries), f32),
        ],
        12 * n * n_tokens * e,
        10**6,
        wait=wait,
    )(docs, queries, ids, hot, counts, positive)


def score_grads(docs, queries, ids, index, sums, scores, stats, positive, wait=()):
    n, e = docs.shape
    n_tokens = queries.shape[0]
    n_queries = n_tokens // QLEN
    return call(
        score_grad_kernel,
        "score_grads",
        (1,),
        [
            whole_spec((n, e)),
            whole_spec((n_tokens, e)),
            whole_spec((1, n_tokens)),
            whole_spec((n, 1)),
            whole_spec((3, 8, n_tokens)),
            whole_spec((3, 8, n_queries)),
            whole_spec((3, 3, n_queries)),
            whole_spec((8, n_queries)),
        ],
        [whole_spec((n_tokens, e)), whole_spec((n, e))],
        [like((n_tokens, e), f32), like((n, e), f32)],
        24 * n * n_tokens * e,
        10**6,
        wait=wait,
    )(docs, queries, ids, index, sums, scores, stats, positive)


def layout(lengths, row_len, q_tokens):
    count = lengths.shape[0]
    before = jnp.arange(count)[:, None] <= jnp.arange(count)[None, :]
    ends = jnp.sum(jnp.where(before, lengths[:, None], 0), axis=0)
    offset = jnp.arange(row_len, dtype=jnp.int32) - q_tokens
    doc = jnp.sum((offset[:, None] >= ends[None, :]).astype(jnp.int32), axis=1)
    chosen = (doc[:, None] == jnp.arange(count, dtype=jnp.int32)[None, :]).astype(
        jnp.int32
    )
    begin = jnp.sum(chosen * (ends - lengths)[None, :], axis=1)
    is_query = offset < 0
    position = jnp.where(is_query, (offset + q_tokens) % QLEN, offset - begin)
    return position, doc


def combine_stats(one, two):
    top = jnp.maximum(one[:, 0], two[:, 0])
    den = one[:, 1] * jnp.exp(one[:, 0] - top) + two[:, 1] * jnp.exp(two[:, 0] - top)
    return jnp.stack([top, den, one[:, 2] + two[:, 2]], axis=1)


def reduce_stats(stats):
    n_rows, n_z, _, _ = sizes()
    moves = [[dict(swap_core=True)]]
    moves.append([dict(row_masks=(m, m)) for m in range(1, n_rows)])
    moves.append([dict(z_mask=m) for m in range(1, n_z)])
    for level in moves:
        parts = [exchange(stats, **move) for move in level]
        for part in parts:
            stats = combine_stats(stats, part)
    return stats


def on_device(
    tokens,
    lengths,
    positives,
    w_qkv,
    b_qkv,
    w_out,
    b_out,
    norm1_gain,
    norm1_bias,
    w_up,
    b_up,
    w_down,
    b_down,
    norm2_gain,
    norm2_bias,
    w_proj,
):
    n_rows, n_z, _, _ = sizes()
    n_devices = n_rows * n_z * 2
    row, z, core = place()
    device = (row * n_z + z) * 2 + core
    table = piece_table()
    row_len = tokens.shape[0]
    q_tokens = QPR * QLEN

    own_lengths = lax.dynamic_index_in_dim(lengths, device, 0, keepdims=False)
    position, doc_index = layout(own_lengths, row_len, q_tokens)
    documents = document_table(own_lengths)
    half = HEAD_DIM // 2
    frequency = 10000.0 ** (-jnp.arange(half, dtype=f32) / half)
    angles = position.astype(f32)[:, None] * frequency[None, :]
    cosine, sine = jnp.cos(angles), jnp.sin(angles)
    cosine = jnp.concatenate([cosine] * 4, axis=1)
    sine = jnp.concatenate([-sine, sine] * 2, axis=1)
    doc_index = jnp.where(jnp.arange(row_len) < q_tokens, -1, doc_index)
    slots = jnp.arange(8, dtype=jnp.int32)
    hot = (slots[:, None] == doc_index[None, :]).astype(bf16)
    counts = jnp.broadcast_to(
        jnp.log(jnp.pad(own_lengths, (0, 8 - DPR), constant_values=1).astype(f32))[:, None],
        (8, LANES),
    )
    positive = (
        (positives[None, :] == device * DPR + slots[:, None]) & (slots < DPR)[:, None]
    ).astype(f32)
    query_ids = relative_order()[:, None] * QPR + jnp.arange(q_tokens, dtype=jnp.int32)[None, :] // QLEN
    query_ids = query_ids.reshape(-1, 1)
    query_row = query_ids.reshape(1, -1)
    doc_column = doc_index[:, None]
    early = [hot, counts, positive, query_ids, query_row, doc_column]
    proj_width = -(-w_proj.shape[1] // LANES) * LANES
    w_first = jnp.concatenate(
        [w_qkv, w_out, jnp.pad(w_proj, ((0, 0), (0, proj_width - w_proj.shape[1])))], axis=1
    )
    g_qkv, g_up, g_down = (Gather(w) for w in (w_first, w_up, w_down))
    g_qkv.all_z(())
    tokens_half = tuple(halves(table, tokens, n_rows, n_z, wait=[g_qkv.held, *early]))
    g_qkv.all_rows([(), [tokens_half[0]]], ())
    first, last = g_qkv.own, g_qkv.pieces[-1]
    vectors = (b_qkv, b_out, norm1_gain, norm1_bias, b_up, b_down, norm2_gain, norm2_bias)
    widths = [v.shape[0] for v in vectors]
    packed = jnp.concatenate(vectors)
    packed = jnp.pad(packed, (0, -packed.shape[0] % LANES)).reshape(-1, LANES)
    packed = gather_small(packed, g_qkv.received + [first[0], last]).reshape(n_devices, -1)
    full_bqkv, full_bout, gain_one, bias_one, full_bup, full_bdown, gain_two, bias_two = unpack(
        packed, widths
    )
    g_up.all_z([[g_qkv.held]], [[], [last]])
    first_all = g_qkv.whole(table)

    qkv, full_qkv = project_qkv(
        tokens, first_all.columns(0, 3 * D), full_bqkv, cosine, sine, wait=[tokens_half[0]]
    )
    g_up.own_rows([last], [qkv])
    attended = attention(documents, qkv, wait=g_up.own)
    g_up.other_rows([qkv], [attended])
    g_down.all_z([[g_up.held], [qkv]], [[qkv], [attended]])
    hat1, rstd1, hidden_low, full_out = out_norm(
        attended, first_all.columns(3 * D, D), full_bout, tokens, gain_one, bias_one, wait=[*g_up.pieces, g_down.held]
    )

    w_up_all = g_up.whole(table, [[attended]], [[attended]])
    part = up_gelu(hidden_low, w_up_all, full_bup)
    g_down.own_rows([attended], [part[0]])
    g_down.other_rows([part[0]])
    act, slope, full_up = up_gelu(hidden_low, w_up_all, full_bup, part, wait=g_down.own)
    w_down_all = g_down.whole(table, [[part[0]], [act]], [[act]])
    hat2, rstd2, result_low, raw, vecs, full_down, full_proj = down_norm(
        act,
        w_down_all,
        full_bdown,
        hat1,
        gain_one,
        bias_one,
        gain_two,
        bias_two,
        first_all.columns(4 * D, proj_width),
    )
    full_qkv, full_out, full_up, full_down, full_proj = (
        w.reshape(-1, w.shape[-1]) for w in (full_qkv, full_out, full_up, full_down, full_proj)
    )

    query_all = gather_relative(vecs[:q_tokens]).reshape(n_devices * q_tokens, -1)
    sums, doc_scores, stats = score_stats(
        vecs, query_all, query_ids, hot, counts, positive
    )
    stats = reduce_stats(stats)
    query_count = n_z * 2 * QPR
    losses = lax.dynamic_slice_in_dim(
        stats[:, 0] + jnp.log(stats[:, 1]) - stats[:, 2], row * query_count, query_count, 1
    )
    query_grads, doc_grads = score_grads(
        vecs, query_all, query_row, doc_column, sums, doc_scores, stats, positive
    )
    doc_part = head_back(doc_grads, raw, full_proj, hat2, rstd2, gain_two)
    query_grad = scatter_relative(
        query_grads.reshape(2, n_rows, n_z, q_tokens, -1), bf16, [doc_part[2]]
    )
    resid_two_grad, branch_grad, raw_grad, sums2 = head_back(
        doc_grads, raw, full_proj, hat2, rstd2, gain_two, query_grad, doc_part[:3]
    )
    sums2 = sums2 + doc_part[3]

    def sib_half(name, operands, tile, dtype=bf16, wait=()):
        return weight_half(name + "_sib", table, operands, n_rows, n_z, tile, other_type=dtype, wait=wait)

    def own_half(name, operands, tile, sib, wide=False, wait=()):
        other = exchange(sib, swap_core=True)
        return Scatter(*weight_half(name, table, operands, n_rows, n_z, tile, other, wait=wait), wide)

    def attention_part(i, wait):
        return attention_back(documents, qkv, attended_grad, cosine, sine, i, 2, wait=wait)

    down_sib = sib_half("grad_down", [(act, branch_grad)], 512)
    inner_grad, grad_bup = act_back(branch_grad, full_down, slope, wait=[down_sib])
    down = own_half("grad_down", [(act, branch_grad)], 512, down_sib, True, wait=[grad_bup])
    up_sib = sib_half("grad_up", [(hidden_low, inner_grad)], 1024, f32, wait=[down.send])
    resid_one_grad, out_grad, attended_grad, sums1 = hidden_back(
        inner_grad, full_up, resid_two_grad, hat1, rstd1, gain_one, full_out, wait=[up_sib]
    )
    d2 = down.step(sums1)
    up = own_half("grad_up", [(hidden_low, inner_grad)], 1024, up_sib, wait=[sums1, d2])
    d3 = down.step(up.send)
    out_pairs = [(attended, out_grad), (result_low, raw_grad)]
    out_sib = sib_half("grad_out", out_pairs, None, wait=[up.send])
    grad_a, sums_a = attention_part(0, [out_sib, d3])
    d4 = down.step(sums_a)
    u2 = up.step(sums_a)
    sib_a = sib_half("grad_qkv", [(tokens_half, grad_a)], 512)
    out = own_half("grad_out", out_pairs, None, out_sib, True, wait=[sib_a])
    grad_b, sums_b = attention_part(1, [out.send, d4, u2])
    sib_b = sib_half("grad_qkv", [(tokens_half, grad_b)], 512)
    o2 = out.step(sums_b)
    u3 = up.step(sums_b)
    sum_down = down.finish(sums_b)
    qkv_a = own_half("grad_qkv", [(tokens_half, grad_a)], 512, sib_a, wait=[sib_b, o2, u3])
    o3 = out.step(qkv_a.send)
    u4 = up.step(qkv_a.send)
    qkv_b = own_half("grad_qkv", [(tokens_half, grad_b)], 512, sib_b, wait=[qkv_a.send, o3, u4])
    a2 = qkv_a.step(qkv_b.send)
    o4 = out.step(qkv_b.send)
    input_grad = input_back([grad_a, grad_b], full_qkv, resid_one_grad, wait=[qkv_b.send, a2, o4])
    b2 = qkv_b.step(input_grad)
    qkv_a.step(input_grad)
    grads = [sums_a[i] if j == 0 else sums_b[i] for i in range(3) for j in range(2)]
    grad_bqkv = jnp.concatenate(grads, axis=1)
    small = pack(
        [grad_bqkv, sums1[2:3], sums1[0:1], sums1[1:2], grad_bup, sums2[2:3], sums2[0:1], sums2[1:2]],
        n_devices,
        wait=[b2],
    )
    while qkv_b.stages[0][0] == "row":
        qkv_b.step(small)
    while qkv_a.stages[0][0] == "row":
        qkv_a.step()
    q3 = qkv_a.merge(qkv_b).send
    sum_up = up.finish(q3)
    sum_out = out.finish(q3)
    sum_out, sum_proj = sum_out[:, :D], sum_out[:, D : D + w_proj.shape[1]]
    q4 = qkv_a.step()
    small = scatter_small(
        small.reshape(n_devices, -1, LANES), f32, [[q3], [q3], [q3], [q4], [q4]]
    ).reshape(-1)
    sum_qkv = qkv_a.finish()
    width = D // 2
    sum_qkv = jnp.concatenate(
        [sum_qkv[:, at * width : (at + 1) * width] for at in (0, 3, 1, 4, 2, 5)], axis=1
    )
    pieces = []
    at = 0
    for width in widths:
        pieces.append(small[at : at + width])
        at += width
    s_bqkv, s_bout, s_gain1, s_bias1, s_bup, s_bdown, s_gain2, s_bias2 = pieces
    return (
        losses,
        result_low,
        input_grad,
        sum_qkv,
        s_bqkv,
        sum_out,
        s_bout,
        s_gain1,
        s_bias1,
        sum_up,
        s_bup,
        sum_down,
        s_bdown,
        s_gain2,
        s_bias2,
        sum_proj,
    )


def solution(mesh):
    shard = P(AXES, None)
    vec = P(AXES)
    in_specs = (
        shard,
        P(),
        P(),
        shard,
        vec,
        shard,
        vec,
        vec,
        vec,
        shard,
        vec,
        shard,
        vec,
        vec,
        vec,
        shard,
    )
    out_specs = (P(None, "row"), shard) + (shard,) + in_specs[3:]
    return jax.shard_map(
        on_device, mesh=mesh, in_specs=in_specs, out_specs=out_specs, check_vma=False
    )
```

```python
import functools

import jax
import jax.numpy as jnp
from jax import lax
from jax.experimental import pallas as pl
from jax.experimental.pallas import tpu as pltpu
from jax.sharding import PartitionSpec as P

D = 1024
HEADS = 16
HEAD_DIM = 64
PROJ_A = 128
PROJ_B = 96
PROJ_C = 64
QLEN = 32
DPR = 4
QPR = 1
DMOST = 330

AXES = ("row", "col")
highest = lax.Precision.HIGHEST
eps_norm = 1e-05
eps_vec = 1e-06
score_scale = 16.0
f32 = jnp.float32
bf16 = jnp.bfloat16


def sizes():
    n_rows = lax.axis_size("row")
    n_z = lax.axis_size("col") // 2
    return n_rows, n_z, n_rows.bit_length() - 1, n_z.bit_length() - 1


def after(value, *before):
    return lax.optimization_barrier((value,) + before)[0] if before else value


def place():
    col = lax.axis_index("col")
    return lax.axis_index("row"), col // 2, col % 2


def exchange(value, row_masks=(0, 0), z_mask=0, swap_core=False):
    n_rows, n_z, _, _ = sizes()
    pairs = []
    for r in range(n_rows):
        for z in range(n_z):
            for c in range(2):
                here = (r * n_z + z) * 2 + c
                there = ((r ^ row_masks[c]) * n_z + (z ^ z_mask)) * 2 + (
                    1 - c if swap_core else c
                )
                pairs.append((here, there))
    return lax.ppermute(value, AXES, pairs)


def stage_bit(core, stage, row_bits):
    return (stage + core) % row_bits


def stage_masks(stage):
    _, _, row_bits, _ = sizes()
    return tuple(1 << stage_bit(c, stage, row_bits) for c in range(2))


def piece_mask(core, piece):
    _, _, row_bits, _ = sizes()
    return sum(
        1 << stage_bit(core, j, row_bits) for j in range(row_bits) if piece >> j & 1
    )


def ordered(bit, own, other, axis):
    return jnp.stack([jnp.where(bit == 0, own, other), jnp.where(bit == 0, other, own)], axis)


def transfer(value, start=(), use=(), **move):
    return after(exchange(after(value, *start), **move), *use)


class Gather:
    def __init__(self, shard):
        self.held, self.count, self.shard, self.received = shard, 0, shard, []

    def along_z(self, start=(), use=()):
        _, n_z, _, z_bits = sizes()
        _, z, _ = place()
        bit = z_bits - 1 - self.count
        other = transfer(self.held, start, use, z_mask=1 << bit)
        self.received.append(other)
        self.held = ordered(z >> bit & 1, self.held, other, self.count)
        self.count += 1
        if self.count == z_bits:
            self.pieces = [self.held.reshape((n_z,) + self.shard.shape)]

    def all_z(self, *bounds):
        _, _, _, z_bits = sizes()
        for i in range(z_bits):
            self.along_z(*bounds[min(i, len(bounds) - 1)])

    def own_rows(self, start=(), use=()):
        _, _, row_bits, _ = sizes()
        self.own = [
            transfer(self.pieces[0], start, use, row_masks=stage_masks(stage))
            for stage in range(row_bits)
        ]
        self.pieces = self.pieces + self.own

    def other_rows(self, start=(), use=()):
        _, _, row_bits, _ = sizes()
        pieces = [self.pieces[0], self.own[0]]
        for stage in range(1, row_bits):
            pieces = pieces + [self.own[stage]] + [
                transfer(p, start, use, row_masks=stage_masks(stage)) for p in pieces[1:]
            ]
        self.pieces = pieces

    def all_rows(self, own, other):
        self.own_rows(*own)
        self.other_rows(*other)

    def whole(self, table, early=(), late=()):
        last = len(self.pieces) - 1
        sibs = [
            transfer(p, *(late if i == last else early), swap_core=True)
            for i, p in enumerate(self.pieces)
        ]
        return Weight(table, self.pieces + sibs)


def piece_table():
    n_rows, _, _, _ = sizes()
    row, _, core = place()
    tables = [
        jnp.array([piece_mask(c, k) for k in range(n_rows)], jnp.int32) for c in range(2)
    ]
    own = row ^ jnp.where(core == 0, tables[0], tables[1])
    sib = row ^ jnp.where(core == 0, tables[1], tables[0])
    steps = jnp.arange(n_rows)

    def piece_of(rows):
        return jnp.sum(jnp.where(rows[None, :] == steps[:, None], steps[None, :], 0), axis=1)

    return jnp.concatenate([own, sib, core[None], piece_of(own), piece_of(sib)]).astype(jnp.int32)


class Weight:
    def __init__(self, table, pieces, start=0, size=None):
        self.table, self.pieces = table, pieces
        self.start, self.size = start, size or pieces[0].shape[2]

    def columns(self, start, size):
        return Weight(self.table, self.pieces, self.start + start, size)

    @property
    def shape(self):
        n_rows, n_z, _, _ = sizes()
        return (n_rows, n_z, 2, self.pieces[0].shape[1], self.size)

    def specs(self):
        return [pl.BlockSpec(memory_space=pl.ANY)] * len(self.pieces)

    def scratch(self):
        return [
            pltpu.VMEM(self.shape, self.pieces[0].dtype),
            pltpu.SemaphoreType.DMA((len(self.pieces) + 1,)),
        ]

    def out_shape(self):
        return jax.ShapeDtypeStruct(self.shape, self.pieces[0].dtype)

    def load(self, table, pieces, out_ref, w_ref, sems):
        n_rows = len(pieces) // 2
        core = table[2 * n_rows]
        out = pltpu.make_async_copy(w_ref, out_ref, sems.at[2 * n_rows])
        if self.size != pieces[0].shape[2]:
            pieces = [p.at[:, :, pl.ds(self.start, self.size)] for p in pieces]

        @pl.when(pl.program_id(0) == 0)
        def _():
            copies = [
                pltpu.make_async_copy(
                    piece,
                    w_ref.at[table[i], :, core if i < n_rows else 1 - core],
                    sems.at[i],
                )
                for i, piece in enumerate(pieces)
            ]
            for c in copies:
                c.start()
            for c in copies:
                c.wait()
            out.start()

        @pl.when(pl.program_id(0) == pl.num_programs(0) - 1)
        def _():
            out.wait()


def gather_small(shard, uses=()):
    n_rows, n_z, row_bits, z_bits = sizes()
    row, z, core = place()
    uses = list(uses)

    def arrive(**move):
        other = exchange(held, **move)
        return after(other, uses.pop(0)) if uses else other

    held = shard
    for count, bit in enumerate(reversed(range(z_bits))):
        held = ordered(z >> bit & 1, held, arrive(z_mask=1 << bit), count)
    for count, bit in enumerate(reversed(range(row_bits))):
        held = ordered(row >> bit & 1, held, arrive(row_masks=(1 << bit, 1 << bit)), count)
    held = ordered(core, held, arrive(swap_core=True), row_bits + z_bits)
    return held.reshape((n_rows * n_z * 2,) + shard.shape)


def scatter_small(blocks, dtype, starts=()):
    n_rows, n_z, row_bits, z_bits = sizes()
    row, z, core = place()
    held = blocks.reshape((2,) * (row_bits + z_bits + 1) + blocks.shape[1:])
    starts = list(starts)

    def halve(held, axis, bit, **move):
        send = lax.dynamic_index_in_dim(held, 1 - bit, axis, keepdims=False).astype(dtype)
        keep = lax.dynamic_index_in_dim(held, bit, axis, keepdims=False)
        start = starts.pop(0) if starts else ()
        return keep.astype(f32) + transfer(send, start, **move).astype(f32)

    held = halve(held, row_bits + z_bits, core, swap_core=True)
    for bit in range(row_bits):
        held = halve(held, row_bits - 1 - bit, row >> bit & 1, row_masks=(1 << bit, 1 << bit))
    for bit in range(z_bits):
        held = halve(held, z_bits - 1 - bit, z >> bit & 1, z_mask=1 << bit)
    return held


def gather_relative(block):
    n_rows, n_z, _, _ = sizes()
    held = jnp.stack([block] + [exchange(block, z_mask=m) for m in range(1, n_z)])
    held = jnp.stack([held] + [exchange(held, row_masks=(m, m)) for m in range(1, n_rows)])
    return jnp.stack([held, exchange(held, swap_core=True)])


def scatter_relative(blocks, dtype, use=()):
    n_rows, n_z, _, _ = sizes()

    def step(held, count, move, use=()):
        parts = [after(exchange(held[m].astype(dtype), **move(m)), *use) for m in range(1, count)]
        total = held[0]
        for part in parts:
            total = total + part.astype(f32)
        return total

    held = step(blocks, 2, lambda m: dict(swap_core=True), use)
    held = step(held, n_rows, lambda m: dict(row_masks=(m, m)))
    return step(held, n_z, lambda m: dict(z_mask=m))


def relative_order():
    n_rows, n_z, _, _ = sizes()
    row, z, core = place()
    at = jnp.arange(n_rows * n_z * 2)
    there_core = core ^ at // (n_rows * n_z)
    there_row = row ^ at // n_z % n_rows
    return ((there_row * n_z + (z ^ at % n_z)) * 2 + there_core).astype(jnp.int32)


class Scatter:
    def __init__(self, send, keep, wide=False):
        _, _, row_bits, z_bits = sizes()
        flat = lambda x: x.reshape((-1,) + x.shape[-2:])
        self.send, self.keep = flat(send), flat(keep)
        self.stages = [("row", j) for j in reversed(range(row_bits))]
        self.stages += [("z", b) for b in range(z_bits)]
        self.wide = self.stages[-1] if wide else None

    def receive(self):
        kind, at = self.stages.pop(0)
        move = dict(row_masks=stage_masks(at)) if kind == "row" else dict(z_mask=1 << at)
        return exchange(self.send, **move)

    def step(self, *use):
        _, z, _ = place()
        parts = (self.keep, after(self.receive(), *use))
        if not self.stages:
            return (parts[0] + parts[1].astype(f32))[0]
        kind, at = self.stages[0]
        half = self.keep.shape[0] // 2
        if kind == "row":
            pick = lambda x, other: x[half:] if other else x[:half]
        else:
            mine = z >> at & 1
            parts = tuple(x.reshape((half, 2) + x.shape[1:]) for x in parts)
            pick = lambda x, other: lax.dynamic_index_in_dim(
                x, 1 - mine if other else mine, 1, keepdims=False
            )
        total = lambda other: pick(parts[0], other) + pick(parts[1], other).astype(f32)
        self.send, self.keep = total(True), total(False)
        if self.stages[0] != self.wide:
            self.send = self.send.astype(bf16)
        return self.send

    def merge(self, other):
        self.send = jnp.concatenate([self.send, other.send], axis=-1)
        self.keep = jnp.concatenate([self.keep, other.keep], axis=-1)
        return self

    def finish(self, *use):
        while self.stages:
            out = self.step(*use)
        return out


def head_slices():
    return ((0, PROJ_A), (PROJ_A, PROJ_B), (PROJ_A + PROJ_B, PROJ_C))


LANES = 128


def whole_spec(shape):
    return pl.BlockSpec(
        shape, lambda *_: (0,) * len(shape), pipeline_mode=pl.Buffered(buffer_count=1)
    )


def row_spec(rows, width):
    return pl.BlockSpec((rows, width), lambda i, *_: (i, 0))


def col_spec(rows, width):
    return pl.BlockSpec((rows, width), lambda i, *_: (0, i))


def like(shape, dtype):
    return jax.ShapeDtypeStruct(shape, dtype)


def call(
    kernel, name, grid, in_specs, out_specs, out_shape, flops, moved, scratch=(), table=None, wait=(), aliases=None
):
    first = len(in_specs) + (0 if table is None else 1)
    in_specs = list(in_specs) + [pl.BlockSpec(memory_space=pl.ANY)] * len(wait)

    def body(*refs):
        kernel(*refs[:first], *refs[first + len(wait) :])

    run = pl.pallas_call(
        body,
        grid_spec=pltpu.PrefetchScalarGridSpec(
            num_scalar_prefetch=0 if table is None else 1,
            grid=grid,
            in_specs=in_specs,
            out_specs=out_specs,
            scratch_shapes=list(scratch),
        ),
        out_shape=out_shape,
        input_output_aliases=aliases or {},
        compiler_params=pltpu.CompilerParams(vmem_limit_bytes=56 << 20),
        cost_estimate=pl.CostEstimate(
            flops=int(flops), bytes_accessed=int(moved), transcendentals=0
        ),
        name=name,
    )
    return lambda *operands: run(*operands, *wait)


def swap_halves(x):
    lane = lax.broadcasted_iota(jnp.int32, x.shape, 1)
    half = HEAD_DIM // 2
    return jnp.where(
        lane % HEAD_DIM < half, pltpu.roll(x, LANES - half, 1), pltpu.roll(x, half, 1)
    )


QKV_TILE = 1024


def qkv_kernel(weight, table, x_ref, b_ref, cos_ref, sin_ref, *refs):
    pieces, (o_ref, w_out, w_ref, sems) = refs[:-4], refs[-4:]
    weight.load(table, pieces, w_out, w_ref, sems)
    tile = pl.program_id(0)
    per_part = D // QKV_TILE
    cols = pl.ds(pl.multiple_of(tile * QKV_TILE, LANES), QKV_TILE)
    w = w_ref[:, :, :, :, cols].reshape(x_ref.shape[1], QKV_TILE)
    bias = b_ref[...]

    @pl.when(tile < 2 * per_part)
    def _():
        scale = jnp.where(tile < per_part, HEAD_DIM**-0.5, 1.0)
        for row in range(0, x_ref.shape[0], TILE):
            rows = slice(row, row + TILE)
            acc = contract(x_ref[rows, :], w, 1, 0) + bias
            cosine = cos_ref[rows, :] * scale
            sine = sin_ref[rows, :] * scale
            for j in range(QKV_TILE // LANES):
                at = slice(j * LANES, (j + 1) * LANES)
                a = acc[:, at]
                o_ref[rows, at] = (a * cosine + swap_halves(a) * sine).astype(bf16)

    @pl.when(tile >= 2 * per_part)
    def _():
        for row in range(0, x_ref.shape[0], TILE):
            rows = slice(row, row + TILE)
            o_ref[rows, :] = (contract(x_ref[rows, :], w, 1, 0) + bias).astype(bf16)


def project_qkv(x, w, b, cosine, sine, wait=()):
    t = x.shape[0]
    any_out = pl.BlockSpec(memory_space=pl.ANY)
    return call(
        functools.partial(qkv_kernel, w),
        "project_qkv",
        (3 * D // QKV_TILE,),
        [
            whole_spec((t, D)),
            pl.BlockSpec((1, QKV_TILE), lambda i, _: (0, i)),
            whole_spec((t, LANES)),
            whole_spec((t, LANES)),
        ]
        + w.specs(),
        [col_spec(t, QKV_TILE), any_out],
        [like((t, 3 * D), bf16), w.out_shape()],
        6 * t * D * D,
        20 * t * D,
        w.scratch(),
        table=w.table,
        wait=wait,
    )(w.table, x, b, cosine, sine, *w.pieces)


TILE = 256


def normalized(v):
    mean = jnp.mean(v, axis=1, keepdims=True)
    centered = v - mean
    rstd = lax.rsqrt(jnp.mean(centered * centered, axis=1, keepdims=True) + eps_norm)
    return centered * rstd, rstd


def norm_back(g, hat, rstd, gain):
    y = g * gain
    return rstd * (
        y - jnp.mean(y, axis=1, keepdims=True) - hat * jnp.mean(y * hat, axis=1, keepdims=True)
    )


def add_up(ref, value):
    @pl.when(pl.program_id(0) == 0)
    def _():
        ref[...] = jnp.zeros_like(ref)

    ref[...] += value


def column_sum(x):
    return jnp.sum(x, axis=0, keepdims=True)


def out_norm_kernel(weight, table, a_ref, b_ref, x_ref, gain_ref, bias_ref, *refs):
    hat_ref, rstd_ref, low_ref, w_out, w_ref, sems = refs[-6:]
    weight.load(table, refs[:-6], w_out, w_ref, sems)
    w = w_ref[...].reshape(a_ref.shape[1], -1)
    v = x_ref[...].astype(f32) + contract(a_ref[...], w, 1, 0) + b_ref[...]
    hat, rstd = normalized(v)
    hat_ref[...] = hat
    rstd_ref[...] = jnp.broadcast_to(rstd, rstd_ref.shape)
    low_ref[...] = (hat * gain_ref[...] + bias_ref[...]).astype(bf16)


def out_norm(attended, w, b, x, gain, bias, wait=()):
    t = x.shape[0]
    vec = whole_spec((1, D))
    return call(
        functools.partial(out_norm_kernel, w),
        "out_norm",
        (t // TILE,),
        [row_spec(TILE, D), vec, row_spec(TILE, D), vec, vec] + w.specs(),
        [row_spec(TILE, D), row_spec(TILE, LANES), row_spec(TILE, D), pl.BlockSpec(memory_space=pl.ANY)],
        [like((t, D), f32), like((t, LANES), f32), like((t, D), bf16), w.out_shape()],
        2 * t * D * D,
        12 * t * D,
        w.scratch(),
        table=w.table,
        wait=wait,
    )(w.table, attended, b, x, gain, bias, *w.pieces)


UP_TILE = 1024
CHUNK = 32


def gelu_pair(x):
    phi = 0.5 + 0.5 * lax.erf(x * 0.5**0.5)
    return x * phi, phi + x * jnp.exp(x * x * -0.5) * (2.0 * jnp.pi) ** -0.5


def up_kernel(weight, table, h_ref, b_ref, *refs):
    act_ref, slope_ref, w_out, acc_ref, w_ref, sems = refs[-6:]
    out = w_out.at[:, :, :, :, pl.ds(weight.start, weight.size)]
    weight.load(table, refs[: len(weight.pieces)], out, w_ref, sems)
    cols = pl.ds(pl.multiple_of(pl.program_id(0) * UP_TILE, LANES), UP_TILE)
    acc_ref[...] = contract(h_ref[...], w_ref[:, :, :, :, cols].reshape(-1, UP_TILE), 1, 0)
    bias = b_ref[...]

    def step(i, _):
        rows = pl.ds(pl.multiple_of(i * CHUNK, CHUNK), CHUNK)
        act, slope = gelu_pair(acc_ref[rows, :] + bias)
        act_ref[rows, :] = act.astype(bf16)
        slope_ref[rows, :] = slope.astype(bf16)
        return 0

    lax.fori_loop(0, h_ref.shape[0] // CHUNK, step, 0)


def up_gelu(hidden, w, b, before=None, wait=()):
    t, ff = hidden.shape[0], w.size
    any_space = pl.BlockSpec(memory_space=pl.ANY)
    steps = ff // UP_TILE // 2
    first = 0 if before is None else steps
    before = [] if before is None else list(before)
    n_in = 3 + len(w.pieces)
    half = w.columns(first * UP_TILE, ff // 2)
    return call(
        functools.partial(up_kernel, half),
        "up_gelu",
        (steps,),
        [whole_spec((t, D)), pl.BlockSpec((1, UP_TILE), lambda i, _: (0, first + i))]
        + w.specs()
        + [any_space] * len(before),
        [pl.BlockSpec((t, UP_TILE), lambda i, _: (0, first + i))] * 2 + [any_space],
        [like((t, ff), bf16)] * 2 + [w.out_shape()],
        t * D * ff,
        2 * t * ff + D * ff,
        [pltpu.VMEM((t, UP_TILE), f32)] + half.scratch(),
        table=w.table,
        wait=wait,
        aliases={n_in + i: i for i in range(len(before))},
    )(w.table, hidden, b, *w.pieces, *before)


def head_masks(width):
    lane = lax.broadcasted_iota(jnp.int32, (1, width), 1)
    return [(lane >= start) & (lane < start + size) for start, size in head_slices()]


def head_lanes():
    for start, size in head_slices():
        low = start // LANES * LANES
        high = -(-(start + size) // LANES) * LANES
        lane = lax.broadcasted_iota(jnp.int32, (1, high - low), 1) + low
        yield slice(low, high), (lane >= start) & (lane < start + size)


def head_sums(x):
    out = jnp.zeros_like(x)
    for mask in head_masks(x.shape[1]):
        total = jnp.sum(jnp.where(mask, x, 0.0), axis=1, keepdims=True)
        out = jnp.where(mask, total, out)
    return out


def down_norm_kernel(
    weight, proj, table, a_ref, b_ref, hat1_ref, gain1_ref, bias1_ref, gain_ref, bias_ref, *refs
):
    n = len(weight.pieces)
    hat_ref, rstd_ref, low_ref, raw_ref, vec_ref = refs[-11:-6]
    w_out, p_out, w_ref, w_sems, p_ref, p_sems = refs[-6:]
    proj.load(table, refs[n : 2 * n], p_out, p_ref, p_sems)
    weight.load(table, refs[:n], w_out, w_ref, w_sems)
    w = w_ref[...].reshape(a_ref.shape[1], -1)
    p = p_ref[...].reshape(w.shape[1], -1)
    for row in range(0, a_ref.shape[0], TILE):
        rows = slice(row, row + TILE)
        hidden = hat1_ref[rows, :] * gain1_ref[...] + bias1_ref[...]
        hat, rstd = normalized(hidden + contract(a_ref[rows, :], w, 1, 0) + b_ref[...])
        hat_ref[rows, :] = hat
        rstd_ref[rows, :] = jnp.broadcast_to(rstd, (TILE, LANES))
        low = (hat * gain_ref[...] + bias_ref[...]).astype(bf16)
        low_ref[rows, :] = low
        raw = contract(low, p, 1, 0)
        raw_ref[rows, :] = raw
        vec_ref[rows, :] = (raw * lax.rsqrt(head_sums(raw * raw) + eps_vec)).astype(bf16)


def down_norm(act, w, b, hat1, gain1, bias1, gain, bias, proj, wait=()):
    t, ff = act.shape
    e = proj.size
    vec = whole_spec((1, D))
    any_space = pl.BlockSpec(memory_space=pl.ANY)
    return call(
        functools.partial(down_norm_kernel, w, proj),
        "down_norm",
        (t // TILE,),
        [row_spec(TILE, ff), vec, row_spec(TILE, D), vec, vec, vec, vec] + w.specs() + proj.specs(),
        [
            row_spec(TILE, D),
            row_spec(TILE, LANES),
            row_spec(TILE, D),
            row_spec(TILE, e),
            row_spec(TILE, e),
            any_space,
            any_space,
        ],
        [
            like((t, D), f32),
            like((t, LANES), f32),
            like((t, D), bf16),
            like((t, e), f32),
            like((t, e), bf16),
            w.out_shape(),
            proj.out_shape(),
        ],
        2 * t * D * ff,
        20 * t * D,
        w.scratch() + proj.scratch(),
        table=w.table,
        wait=wait,
    )(w.table, act, b, hat1, gain1, bias1, gain, bias, *w.pieces, *proj.pieces)


def head_back_kernel(
    has_query, g_ref, raw_ref, proj_ref, hat_ref, rstd_ref, gain_ref, *refs
):
    grad_ref, branch_ref, raw_out, sums_ref = refs[-4:]
    g, raw = g_ref[...], raw_ref[...]
    if has_query:
        q = refs[0][...]
        g = g + jnp.concatenate([q, jnp.zeros((g.shape[0] - q.shape[0], q.shape[1]), f32)], axis=0)
    scale = lax.rsqrt(head_sums(raw * raw) + eps_vec)
    y = raw * scale
    raw_grad = (scale * (g - y * head_sums(y * g))).astype(bf16)
    result_grad = contract(raw_grad, proj_ref[...], 1, 1)
    hat = hat_ref[...]
    grad = norm_back(result_grad, hat, rstd_ref[:, :1], gain_ref[...])
    branch = grad.astype(bf16)
    grad_ref[...] = grad
    branch_ref[...] = branch
    raw_out[...] = raw_grad
    add_up(
        sums_ref,
        jnp.concatenate(
            [
                column_sum(result_grad * hat),
                column_sum(result_grad),
                column_sum(branch.astype(f32)),
            ],
            axis=0,
        ),
    )


def head_back(g, raw, proj, hat, rstd, gain, query=None, before=(), wait=()):
    t, e = raw.shape
    first, steps = (1, t // TILE - 1) if query is None else (0, 1)
    extra = [] if query is None else [query]
    rows = lambda width: pl.BlockSpec((TILE, width), lambda i, *_: (first + i, 0))
    return call(
        functools.partial(head_back_kernel, query is not None),
        "head_back",
        (steps,),
        [
            rows(e),
            rows(e),
            whole_spec((D, e)),
            rows(D),
            rows(LANES),
            whole_spec((1, D)),
        ]
        + [whole_spec(x.shape) for x in extra]
        + [pl.BlockSpec(memory_space=pl.ANY)] * len(before),
        [rows(D), rows(D), rows(e), whole_spec((3, D))],
        [like((t, D), f32), like((t, D), bf16), like((t, e), bf16), like((3, D), f32)],
        2 * steps * TILE * D * e,
        16 * steps * TILE * D,
        wait=wait,
        aliases={6 + len(extra) + i: i for i in range(len(before))},
    )(g, raw, proj, hat, rstd, gain, *extra, *before)


def act_back_kernel(g_ref, w_ref, slope_ref, o_ref, sum_ref):
    back = (contract(g_ref[...], w_ref[...], 1, 1) * slope_ref[...].astype(f32)).astype(bf16)
    o_ref[...] = back
    sum_ref[...] = column_sum(back.astype(f32))


def act_back(branch, w, slope, wait=()):
    t, ff = slope.shape
    return call(
        act_back_kernel,
        "act_back",
        (ff // UP_TILE,),
        [whole_spec((t, D)), row_spec(UP_TILE, D), col_spec(t, UP_TILE)],
        [col_spec(t, UP_TILE), col_spec(1, UP_TILE)],
        [like((t, ff), bf16), like((1, ff), f32)],
        2 * t * D * ff,
        4 * t * ff + 2 * D * ff,
        wait=wait,
    )(branch, w, slope)


def hidden_back_kernel(
    g_ref, w_ref, resid_ref, hat_ref, rstd_ref, gain_ref, wout_ref,
    grad_ref, out_ref, att_ref, sums_ref,
):
    for row in range(0, g_ref.shape[0], TILE):
        rows = slice(row, row + TILE)
        hidden_grad = resid_ref[rows, :] + contract(g_ref[rows, :], w_ref[...], 1, 1)
        hat = hat_ref[rows, :]
        grad = norm_back(hidden_grad, hat, rstd_ref[rows, :1], gain_ref[...])
        low = grad.astype(bf16)
        grad_ref[rows, :] = grad
        out_ref[rows, :] = low
        att_ref[rows, :] = contract(low, wout_ref[...], 1, 1).astype(bf16)
        sums = [column_sum(hidden_grad * hat), column_sum(hidden_grad), column_sum(low.astype(f32))]
        if row == 0:
            add_up(sums_ref, jnp.concatenate(sums, axis=0))
        else:
            sums_ref[...] += jnp.concatenate(sums, axis=0)


def hidden_back(inner, w, resid, hat, rstd, gain, w_out, wait=()):
    t, ff = inner.shape
    return call(
        hidden_back_kernel,
        "hidden_back",
        (t // TILE,),
        [
            row_spec(TILE, ff),
            whole_spec((D, ff)),
            row_spec(TILE, D),
            row_spec(TILE, D),
            row_spec(TILE, LANES),
            whole_spec((1, D)),
            whole_spec((D, D)),
        ],
        [row_spec(TILE, D)] * 3 + [whole_spec((3, D))],
        [like((t, D), f32), like((t, D), bf16), like((t, D), bf16), like((3, D), f32)],
        2 * t * D * ff + 2 * t * D * D,
        2 * t * ff + 24 * t * D,
        wait=wait,
    )(inner, w, resid, hat, rstd, gain, w_out)


def input_back_kernel(groups, *refs):
    g_refs, (w_ref, resid_ref, o_ref) = refs[:groups], refs[groups:]
    total = resid_ref[...]
    for part in range(3):
        for i, g_ref in enumerate(g_refs):
            width = g_ref.shape[2]
            at = part * D + i * width
            total = total + contract(g_ref[part], w_ref[:, at : at + width], 1, 1)
    o_ref[...] = total


def input_back(grads, w, resid, wait=()):
    t = resid.shape[0]
    return call(
        functools.partial(input_back_kernel, len(grads)),
        "input_back",
        (t // TILE,),
        [pl.BlockSpec((3, TILE, g.shape[2]), lambda i: (0, i, 0)) for g in grads]
        + [whole_spec((D, 3 * D)), row_spec(TILE, D)],
        row_spec(TILE, D),
        like((t, D), f32),
        6 * t * D * D,
        20 * t * D,
        wait=wait,
    )(*grads, w, resid)


def block_masks(n_devices, width):
    n = width * n_devices
    column = lax.broadcasted_iota(jnp.int32, (n_devices, n), 1)
    first = lax.broadcasted_iota(jnp.int32, (n_devices, n), 0) * width
    mine = (column >= first) & (column < first + width)
    at = lax.broadcasted_iota(jnp.int32, (1, n), 1) % width
    return mine, at


def unpack_kernel(n_devices, widths, p_ref, *o_refs):
    start = 0
    for width, o_ref in zip(widths, o_refs):
        mine, at = block_masks(n_devices, width)
        copies = (at == lax.broadcasted_iota(jnp.int32, (width, at.shape[1]), 0)).astype(bf16)
        spread = contract(p_ref[:, start : start + width], copies, 1, 0)
        o_ref[...] = column_sum(jnp.where(mine, spread, 0.0))
        start += width


def unpack(packed, widths, wait=()):
    n_devices = packed.shape[0]
    return call(
        functools.partial(unpack_kernel, n_devices, widths),
        "unpack",
        (1,),
        [whole_spec(packed.shape)],
        [whole_spec((1, w * n_devices)) for w in widths],
        [like((1, w * n_devices), f32) for w in widths],
        10**8,
        10**5,
        wait=wait,
    )(packed)


def pack_kernel(n_devices, widths, *refs):
    o_ref = refs[-1]
    o_ref[...] = jnp.zeros_like(o_ref)
    start = 0
    for width, ref in zip(widths, refs):
        mine, at = block_masks(n_devices, width)
        copies = (at == lax.broadcasted_iota(jnp.int32, (width, at.shape[1]), 0)).astype(bf16)
        rest = jnp.where(mine, ref[...], 0.0)
        total = jnp.zeros((n_devices, width), f32)
        for _ in range(3):
            term = rest.astype(bf16)
            total = total + contract(term, copies, 1, 1)
            rest = rest - term.astype(f32)
        o_ref[:, start : start + width] = total
        start += width


def pack(vectors, n_devices, wait=()):
    widths = [v.shape[1] // n_devices for v in vectors]
    total = sum(widths)
    total += -total % LANES
    return call(
        functools.partial(pack_kernel, n_devices, widths),
        "pack",
        (1,),
        [whole_spec(v.shape) for v in vectors],
        whole_spec((n_devices, total)),
        like((n_devices, total), f32),
        10**8,
        10**5,
        wait=wait,
    )(*vectors)


def halves_kernel(n_rows, n_z, table, own_in, sib_in, own_ref, sib_ref):
    core = table[2 * n_rows]
    for a_ref, o_ref, side in ((own_in, own_ref, core), (sib_in, sib_ref, 1 - core)):
        t, k = a_ref.shape
        x = a_ref[...].T.reshape(n_z, 2, k // (2 * n_z), t)
        o_ref[...] = jnp.where(side == 0, x[:, 0], x[:, 1]).reshape(o_ref.shape)


def halves(table, a, n_rows, n_z, wait=()):
    t, k = a.shape
    block = k // n_rows
    out = pl.BlockSpec((block // 2, t), lambda i, _: (i, 0))
    return call(
        functools.partial(halves_kernel, n_rows, n_z),
        "halves",
        (n_rows,),
        [
            pl.BlockSpec((t, block), lambda i, tab: (0, tab[i])),
            pl.BlockSpec((t, block), lambda i, tab: (0, tab[n_rows + i])),
        ],
        [out, out],
        [like((k // 2, t), bf16)] * 2,
        10**6,
        8 * t * k,
        table=table,
        wait=wait,
    )(table, a, a)


def pick_columns(table, offset, n_rows, n_z, a_ref, picked):
    t, k = a_ref.shape
    block = k // n_rows
    half = block // 2
    r = half // n_z
    core = table[2 * n_rows]
    side = core if offset == 0 else 1 - core
    if r % LANES:
        m = lax.broadcasted_iota(jnp.int32, (block, half), 1)
        source = (m // r) * (2 * r) + side * r + m % r
        choose = (lax.broadcasted_iota(jnp.int32, (block, half), 0) == source).astype(bf16)
    for piece in range(n_rows):
        first = table[offset + piece] * block
        if r % LANES:
            x = a_ref[:, pl.ds(pl.multiple_of(first, LANES), block)]
            picked[:, piece * half : (piece + 1) * half] = contract(x, choose, 1, 0).astype(bf16)
        else:
            for z in range(n_z):
                x = a_ref[:, pl.ds(pl.multiple_of(first + (2 * z + side) * r, LANES), r)]
                at = piece * half + z * r
                picked[:, at : at + r] = x


def weight_kernel(picks, offset, n_rows, n_z, table, *refs):
    pairs = len(picks)
    ins, refs = refs[: 2 * pairs], refs[2 * pairs :]
    count = sum(picks)
    refs, picked = refs[: len(refs) - count], list(refs[len(refs) - count :])

    if count:

        @pl.when(pl.program_id(0) == 0)
        def _():
            into = list(picked)
            for pick, a_ref in zip(picks, ins[::2]):
                if pick:
                    pick_columns(table, offset, n_rows, n_z, a_ref, into.pop(0))

    totals = []
    for pick, a_ref, b_ref in zip(picks, ins[::2], ins[1::2]):
        b = b_ref[...]
        b = b.reshape(b.shape[-2:])
        if pick:
            totals.append(contract(picked.pop(0)[...], b, 0, 0))
        else:
            totals.append(contract(a_ref[...], b, 1, 0))
    total = totals[0] if pairs == 1 else jnp.concatenate(totals, axis=1)
    if len(refs) == 1:
        refs[0][...] = total.reshape(refs[0].shape).astype(refs[0].dtype)
    else:
        other, send_ref, keep_ref = refs
        total = total.reshape(other.shape) + other[...].astype(f32)
        half = keep_ref.shape[0]
        send_ref[...] = total[half:].astype(send_ref.dtype)
        keep_ref[...] = total[:half]


def weight_half(name, table, operands, n_rows, n_z, tile, other=None, other_type=bf16, wait=()):
    own = other is not None
    picks = [not isinstance(a, tuple) for a, _ in operands]
    lefts = [a[0 if own else 1] if isinstance(a, tuple) else a for a, _ in operands]
    rights = [b for _, b in operands]
    t = rights[0].shape[-2]
    k = lefts[0].shape[1] if picks[0] else 2 * lefts[0].shape[0]
    r = k // (n_rows * n_z * 2)
    if len(operands) == 1:
        b = rights[0]
        per_part = b.shape[-1] // tile
        n = b.shape[-1] * (b.shape[0] if b.ndim == 3 else 1)
        if b.ndim == 3:
            b_specs = [pl.BlockSpec((1, t, tile), lambda i, _: (i // per_part, 0, i % per_part))]
        else:
            b_specs = [col_spec(t, tile)]
    else:
        n = tile = sum(b.shape[1] for b in rights)
        b_specs = [whole_spec(b.shape) for b in rights]
    specs, arrays = [], []
    for a, b, b_spec in zip(lefts, rights, b_specs):
        specs += [whole_spec(a.shape), b_spec]
        arrays += [a, b]

    def block(rows):
        return pl.BlockSpec((rows, n_z, r, tile), lambda i, _: (0, 0, 0, i))

    def shape(rows, dtype):
        return like((rows, n_z, r, n), dtype)

    return call(
        functools.partial(weight_kernel, picks, 0 if own else n_rows, n_rows, n_z),
        name,
        (n // tile,),
        specs + ([block(n_rows)] if own else []),
        [block(n_rows // 2)] * 2 if own else block(n_rows),
        [shape(n_rows // 2, bf16), shape(n_rows // 2, f32)] if own else shape(n_rows, other_type),
        t * k * n,
        2 * t * (k + n) + 3 * k * n,
        [pltpu.VMEM((t, k // 2), bf16) for pick in picks if pick],
        table=table,
        wait=wait,
    )(table, *arrays, *([other] if own else []))


def piece_kernel(offset, n_rows, n_z, table, a_ref, b_ref, *refs):
    r = a_ref.shape[1] // (2 * n_z)
    core = table[2 * n_rows]
    side = core if offset == 0 else 1 - core
    blocks = [a_ref[:, pl.ds(pl.multiple_of((2 * z + side) * r, LANES), r)] for z in range(n_z)]
    total = contract(jnp.concatenate(blocks, axis=1), b_ref[...], 0, 0)
    if len(refs) == 1:
        refs[0][...] = total.reshape(refs[0].shape).astype(refs[0].dtype)
        return
    other, send_ref, keep_ref = refs
    total = total.reshape(other.shape) + other[...].astype(f32)
    kept = pl.program_id(0) < n_rows // 2

    @pl.when(kept)
    def _():
        keep_ref[...] = total

    @pl.when(jnp.logical_not(kept))
    def _():
        send_ref[...] = total.astype(send_ref.dtype)


def weight_pieces(name, table, a, b, n_rows, n_z, other=None, wait=()):
    (t, k), n = a.shape, b.shape[1]
    r = k // (n_rows * n_z * 2)
    half = n_rows // 2
    own = other is not None
    offset = 0 if own else n_rows
    block = (1, n_z, r, n)
    each = pl.BlockSpec(block, lambda i, _: (i, 0, 0, 0))
    outs = [
        pl.BlockSpec(block, lambda i, _: (jnp.maximum(i - half, 0), 0, 0, 0)),
        pl.BlockSpec(block, lambda i, _: (jnp.minimum(i, half - 1), 0, 0, 0)),
    ]
    return call(
        functools.partial(piece_kernel, offset, n_rows, n_z),
        name,
        (n_rows,),
        [
            pl.BlockSpec((t, k // n_rows), lambda i, tab: (0, tab[offset + i])),
            whole_spec(b.shape),
        ]
        + ([each] if own else []),
        outs if own else each,
        [like((half, n_z, r, n), bf16), like((half, n_z, r, n), f32)]
        if own
        else like((n_rows, n_z, r, n), bf16),
        t * k * n,
        2 * t * (k + n) + 3 * k * n,
        table=table,
        wait=wait,
    )(table, a, b, *([other] if own else []))


WINDOWS = (256, -(-(DMOST + 15) // 32) * 32)
NEG = -1e30


def contract(a, b, ca, cb):
    return lax.dot_general(a, b, (((ca,), (cb,)), ((), ())), preferred_element_type=f32)


def document_table(lengths):
    at = jnp.arange(DPR)
    starts = QPR * QLEN + jnp.sum(jnp.where(at[:, None] < at[None, :], lengths[:, None], 0), axis=0)
    need = starts % 16 + lengths
    ahead = (need[:, None] > need[None, :]) | ((need[:, None] == need[None, :]) & (at[:, None] < at[None, :]))
    rank = jnp.sum(ahead.astype(jnp.int32), axis=0)
    order = rank[None, :] == at[:, None]
    pick = lambda x: jnp.sum(jnp.where(order, x[None, :], 0), axis=1)
    wide = jnp.sum((need > WINDOWS[0]).astype(jnp.int32))
    return jnp.concatenate([pick(starts), pick(lengths), wide[None]]).astype(jnp.int32)


def for_documents(doc_ref, row_len, step):
    for wide in range(1, DPR):

        @pl.when(doc_ref[2 * DPR] == wide)
        def _():
            for d in range(DPR):
                window = WINDOWS[1] if d < wide else WINDOWS[0]
                start, size = doc_ref[d], doc_ref[DPR + d]
                base = pl.multiple_of(jnp.minimum((start // 16) * 16, row_len - window), 16)
                step(window, base, start - base, start - base + size)


def head_pair(x):
    lane = lax.broadcasted_iota(jnp.int32, x.shape, 1)
    zero = jnp.zeros_like(x)
    return jnp.concatenate(
        [jnp.where(lane < HEAD_DIM, x, zero), jnp.where(lane < HEAD_DIM, zero, x)], axis=0
    )


def pair_heads(x):
    n = x.shape[0] // 2
    lane = lax.broadcasted_iota(jnp.int32, (n, x.shape[1]), 1)
    return jnp.where(lane < HEAD_DIM, x[:n], x[n:])


def inside(n, low, high, axis):
    shape = (n, 1) if axis == 0 else (1, n)
    at = lax.broadcasted_iota(jnp.int32, shape, axis)
    return (at >= low) & (at < high)


def attend(q, k, v, low, high):
    s = contract(head_pair(q), k, 1, 1)
    s = s + jnp.where(inside(k.shape[0], low, high, 1), 0.0, NEG)
    p = jnp.exp(s - jnp.max(s, axis=1, keepdims=True))
    total = jnp.sum(p, axis=1, keepdims=True)
    return pair_heads(contract(p.astype(bf16), v, 1, 0) / total)


def attention_kernel(len_ref, q_ref, k_ref, v_ref, o_ref):
    def step(window, base, low, high):
        w = pl.ds(base, window)
        o = attend(q_ref[w, :], k_ref[w, :], v_ref[w, :], low, high)
        keep = inside(window, low, high, 0)
        o_ref[w, :] = jnp.where(keep, o, o_ref[w, :].astype(f32)).astype(bf16)

    for_documents(len_ref, q_ref.shape[0], step)
    o_ref[:QLEN, :] = attend(q_ref[:QLEN, :], k_ref[:128, :], v_ref[:128, :], 0, QLEN).astype(bf16)


def qkv_specs(t):
    per_part = D // LANES
    return [
        pl.BlockSpec((t, LANES), lambda i, _, p=p: (0, p * per_part + i)) for p in range(3)
    ]


def attention(lengths, qkv, wait=()):
    t = qkv.shape[0]
    return call(
        attention_kernel,
        "attention",
        (HEADS // 2,),
        qkv_specs(t),
        col_spec(t, LANES),
        like((t, D), bf16),
        2 * 10**10,
        8 * t * D,
        table=lengths,
        wait=wait,
    )(lengths, qkv, qkv, qkv)


def attend_back(q, k, v, g, low, high):
    n = q.shape[0]
    g = jnp.where(inside(n, low, high, 0), g, jnp.zeros_like(g))
    qq = head_pair(q)
    gg = head_pair(g)
    st = contract(k, qq, 1, 1)
    st = st + jnp.where(inside(k.shape[0], low, high, 0), 0.0, NEG)
    p = jnp.exp(st - jnp.max(st, axis=0, keepdims=True))
    p = p * (1.0 / jnp.sum(p, axis=0, keepdims=True))
    dp = contract(v, gg, 1, 1)
    delta = jnp.sum(p * dp, axis=0, keepdims=True)
    ds = (p * (dp - delta)).astype(bf16)
    dv = contract(p.astype(bf16), gg, 1, 0)
    dk = contract(ds, qq, 1, 0)
    dq = contract(ds, k, 0, 0) * (HEAD_DIM**-0.5)
    return pair_heads(dq), dk, dv


def attention_back_kernel(len_ref, q_ref, k_ref, v_ref, g_ref, cos_ref, sin_ref, o_ref, sum_ref, *sums):
    row_len = q_ref.shape[0]
    for ref in sums:
        ref[...] = jnp.zeros_like(ref)
    parts = attend_back(
        q_ref[:QLEN, :], k_ref[:128, :], v_ref[:128, :], g_ref[:QLEN, :], 0, QLEN
    )
    for ref, x in zip(sums, parts):
        ref[: x.shape[0], :] = x

    def step(window, base, low, high):
        w = pl.ds(base, window)
        parts = attend_back(q_ref[w, :], k_ref[w, :], v_ref[w, :], g_ref[w, :], low, high)
        for ref, x in zip(sums, parts):
            ref[w, :] += x

    for_documents(len_ref, row_len, step)
    cosine, sine = cos_ref[...], sin_ref[...]
    for part in range(3):
        x = sums[part][...]
        if part < 2:
            x = x * cosine - swap_halves(x) * sine
        x = x.astype(bf16)
        o_ref[part] = x
        sum_ref[part] = column_sum(x.astype(f32))


def attention_back(lengths, qkv, g, cosine, sine, group, groups, wait=()):
    t = qkv.shape[0]
    table = whole_spec((t, LANES))
    pairs = HEADS // 2 // groups
    first = group * pairs
    per_part = D // LANES
    specs = [
        pl.BlockSpec((t, LANES), lambda i, _, p=p: (0, p * per_part + first + i)) for p in range(3)
    ]
    return call(
        attention_back_kernel,
        "attention_back",
        (pairs,),
        specs + [pl.BlockSpec((t, LANES), lambda i, _: (0, first + i)), table, table],
        [
            pl.BlockSpec((3, t, LANES), lambda i, _: (0, 0, i)),
            pl.BlockSpec((3, 1, LANES), lambda i, _: (0, 0, i)),
        ],
        [like((3, t, D // groups), bf16), like((3, 1, D // groups), f32)],
        5 * 10**10 // groups,
        14 * t * D // groups,
        [pltpu.VMEM((t, LANES), f32)] * 3,
        table=lengths,
        wait=wait,
    )(lengths, qkv, qkv, qkv, g, cosine, sine)


SCORE_TILE = 256


def doc_inside(doc_ref, d):
    return doc_ref[...] == d


def score_exps(docs, queries, mask):
    picked = jnp.where(mask, docs, jnp.zeros_like(docs))
    return picked, jnp.exp(contract(picked, queries, 1, 1) * score_scale)


def split_dot(hot, x):
    high = x.astype(bf16)
    rest = (x - high.astype(f32)).astype(bf16)
    return contract(hot, high, 1, 0) + contract(hot, rest, 1, 0)


def score_kernel(
    doc_ref, query_ref, id_ref, hot_ref, count_ref, pos_ref, sum_ref, score_ref, stat_ref
):
    docs = doc_ref[...]
    n_queries = score_ref.shape[2]
    live = lax.broadcasted_iota(jnp.int32, (8, n_queries), 0) < DPR
    for head, (lanes, mask) in enumerate(head_lanes()):
        scores = jnp.zeros((8, n_queries), f32)
        for at in range(0, query_ref.shape[0], SCORE_TILE):
            _, e = score_exps(docs[:, lanes], query_ref[at : at + SCORE_TILE, lanes], mask)
            total = split_dot(hot_ref[...], e)
            sum_ref[head, :, at : at + SCORE_TILE] = total
            smooth = jnp.log(total) - count_ref[:, :1]
            query = lax.broadcasted_iota(jnp.int32, (SCORE_TILE, n_queries), 1)
            hot = (id_ref[at : at + SCORE_TILE, :] == query).astype(f32)
            scores += lax.dot_general(
                jnp.where(lax.broadcasted_iota(jnp.int32, smooth.shape, 0) < DPR, smooth, 0.0),
                hot,
                (((1,), (0,)), ((), ())),
                precision=highest,
                preferred_element_type=f32,
            )
        score_ref[head] = scores
        top = jnp.max(jnp.where(live, scores, NEG), axis=0, keepdims=True)
        den = column_sum(jnp.where(live, jnp.exp(scores - top), 0.0))
        pos = column_sum(jnp.where(live, scores * pos_ref[...], 0.0))
        stat_ref[head] = jnp.concatenate([top, den, pos], axis=0)


def score_grad_kernel(
    doc_ref, query_ref, id_ref, index_ref, sum_ref, score_ref, stat_ref, pos_ref, dq_ref, dd_ref
):
    docs = doc_ref[...]
    n_queries = score_ref.shape[2]
    dd_ref[...] = jnp.zeros_like(dd_ref)
    dq_ref[...] = jnp.zeros_like(dq_ref)
    index = index_ref[...]
    for head, (lanes, mask) in enumerate(head_lanes()):
        stats = stat_ref[head]
        grad = jnp.exp(score_ref[head] - stats[0:1]) / stats[1:2] - pos_ref[...]
        for at in range(0, query_ref.shape[0], SCORE_TILE):
            queries = query_ref[at : at + SCORE_TILE, lanes]
            picked, e = score_exps(docs[:, lanes], queries, mask)
            query = lax.broadcasted_iota(jnp.int32, (n_queries, SCORE_TILE), 0)
            hot = (id_ref[:, at : at + SCORE_TILE] == query).astype(f32)
            spread = lax.dot_general(
                grad, hot, (((1,), (0,)), ((), ())), precision=highest, preferred_element_type=f32
            )
            coef = score_scale * spread / sum_ref[head, :, at : at + SCORE_TILE]
            wide = jnp.zeros_like(e)
            for d in range(DPR):
                wide = jnp.where(index == d, coef[d : d + 1], wide)
            back = (e * wide).astype(bf16)
            dd_ref[:, lanes] += jnp.where(mask, contract(back, queries, 1, 0), 0.0)
            dq_ref[at : at + SCORE_TILE, lanes] += contract(back, picked, 0, 0)


def score_stats(docs, queries, ids, hot, counts, positive, wait=()):
    n, e = docs.shape
    n_tokens = queries.shape[0]
    n_queries = n_tokens // QLEN
    return call(
        score_kernel,
        "scores",
        (1,),
        [
            whole_spec((n, e)),
            whole_spec((n_tokens, e)),
            whole_spec((n_tokens, 1)),
            whole_spec((8, n)),
            whole_spec((8, LANES)),
            whole_spec((8, n_queries)),
        ],
        [
            whole_spec((3, 8, n_tokens)),
            whole_spec((3, 8, n_queries)),
            whole_spec((3, 3, n_queries)),
        ],
        [
            like((3, 8, n_tokens), f32),
            like((3, 8, n_queries), f32),
            like((3, 3, n_queries), f32),
        ],
        12 * n * n_tokens * e,
        10**6,
        wait=wait,
    )(docs, queries, ids, hot, counts, positive)


def score_grads(docs, queries, ids, index, sums, scores, stats, positive, wait=()):
    n, e = docs.shape
    n_tokens = queries.shape[0]
    n_queries = n_tokens // QLEN
    return call(
        score_grad_kernel,
        "score_grads",
        (1,),
        [
            whole_spec((n, e)),
            whole_spec((n_tokens, e)),
            whole_spec((1, n_tokens)),
            whole_spec((n, 1)),
            whole_spec((3, 8, n_tokens)),
            whole_spec((3, 8, n_queries)),
            whole_spec((3, 3, n_queries)),
            whole_spec((8, n_queries)),
        ],
        [whole_spec((n_tokens, e)), whole_spec((n, e))],
        [like((n_tokens, e), f32), like((n, e), f32)],
        24 * n * n_tokens * e,
        10**6,
        wait=wait,
    )(docs, queries, ids, index, sums, scores, stats, positive)


def layout(lengths, row_len, q_tokens):
    count = lengths.shape[0]
    before = jnp.arange(count)[:, None] <= jnp.arange(count)[None, :]
    ends = jnp.sum(jnp.where(before, lengths[:, None], 0), axis=0)
    offset = jnp.arange(row_len, dtype=jnp.int32) - q_tokens
    doc = jnp.sum((offset[:, None] >= ends[None, :]).astype(jnp.int32), axis=1)
    chosen = (doc[:, None] == jnp.arange(count, dtype=jnp.int32)[None, :]).astype(
        jnp.int32
    )
    begin = jnp.sum(chosen * (ends - lengths)[None, :], axis=1)
    is_query = offset < 0
    position = jnp.where(is_query, (offset + q_tokens) % QLEN, offset - begin)
    return position, doc


def combine_stats(one, two):
    top = jnp.maximum(one[:, 0], two[:, 0])
    den = one[:, 1] * jnp.exp(one[:, 0] - top) + two[:, 1] * jnp.exp(two[:, 0] - top)
    return jnp.stack([top, den, one[:, 2] + two[:, 2]], axis=1)


def reduce_stats(stats):
    n_rows, n_z, _, _ = sizes()
    moves = [[dict(swap_core=True)]]
    moves.append([dict(row_masks=(m, m)) for m in range(1, n_rows)])
    moves.append([dict(z_mask=m) for m in range(1, n_z)])
    for level in moves:
        parts = [exchange(stats, **move) for move in level]
        for part in parts:
            stats = combine_stats(stats, part)
    return stats


def on_device(
    tokens,
    lengths,
    positives,
    w_qkv,
    b_qkv,
    w_out,
    b_out,
    norm1_gain,
    norm1_bias,
    w_up,
    b_up,
    w_down,
    b_down,
    norm2_gain,
    norm2_bias,
    w_proj,
):
    n_rows, n_z, _, _ = sizes()
    n_devices = n_rows * n_z * 2
    row, z, core = place()
    device = (row * n_z + z) * 2 + core
    table = piece_table()
    row_len = tokens.shape[0]
    q_tokens = QPR * QLEN

    own_lengths = lax.dynamic_index_in_dim(lengths, device, 0, keepdims=False)
    position, doc_index = layout(own_lengths, row_len, q_tokens)
    documents = document_table(own_lengths)
    half = HEAD_DIM // 2
    frequency = 10000.0 ** (-jnp.arange(half, dtype=f32) / half)
    angles = position.astype(f32)[:, None] * frequency[None, :]
    cosine, sine = jnp.cos(angles), jnp.sin(angles)
    cosine = jnp.concatenate([cosine] * 4, axis=1)
    sine = jnp.concatenate([-sine, sine] * 2, axis=1)
    doc_index = jnp.where(jnp.arange(row_len) < q_tokens, -1, doc_index)
    slots = jnp.arange(8, dtype=jnp.int32)
    hot = (slots[:, None] == doc_index[None, :]).astype(bf16)
    counts = jnp.broadcast_to(
        jnp.log(jnp.pad(own_lengths, (0, 8 - DPR), constant_values=1).astype(f32))[:, None],
        (8, LANES),
    )
    positive = (
        (positives[None, :] == device * DPR + slots[:, None]) & (slots < DPR)[:, None]
    ).astype(f32)
    query_ids = relative_order()[:, None] * QPR + jnp.arange(q_tokens, dtype=jnp.int32)[None, :] // QLEN
    query_ids = query_ids.reshape(-1, 1)
    query_row = query_ids.reshape(1, -1)
    doc_column = doc_index[:, None]
    early = [hot, counts, positive, query_ids, query_row, doc_column]
    proj_width = -(-w_proj.shape[1] // LANES) * LANES
    w_first = jnp.concatenate(
        [w_qkv, w_out, jnp.pad(w_proj, ((0, 0), (0, proj_width - w_proj.shape[1])))], axis=1
    )
    g_qkv, g_up, g_down = (Gather(w) for w in (w_first, w_up, w_down))
    g_qkv.all_z((), ((), early))
    tokens_half = tuple(halves(table, tokens, n_rows, n_z, wait=[g_qkv.held]))
    g_qkv.all_rows([(), [tokens_half[0]]], ())
    first, last = g_qkv.own, g_qkv.pieces[-1]
    vectors = (b_qkv, b_out, norm1_gain, norm1_bias, b_up, b_down, norm2_gain, norm2_bias)
    widths = [v.shape[0] for v in vectors]
    packed = jnp.concatenate(vectors)
    packed = jnp.pad(packed, (0, -packed.shape[0] % LANES)).reshape(-1, LANES)
    packed = gather_small(packed, g_qkv.received + [first[0], last]).reshape(n_devices, -1)
    full_bqkv, full_bout, gain_one, bias_one, full_bup, full_bdown, gain_two, bias_two = unpack(
        packed, widths
    )
    g_up.all_z([[g_qkv.held]], [[], [last]])
    first_all = g_qkv.whole(table)

    qkv, full_qkv = project_qkv(
        tokens, first_all.columns(0, 3 * D), full_bqkv, cosine, sine, wait=[tokens_half[0]]
    )
    g_up.own_rows([last], [qkv])
    attended = attention(documents, qkv, wait=g_up.own)
    g_up.other_rows([qkv], [attended])
    g_down.all_z([[g_up.held], [qkv]], [[qkv], [attended]])
    hat1, rstd1, hidden_low, full_out = out_norm(
        attended, first_all.columns(3 * D, D), full_bout, tokens, gain_one, bias_one, wait=[*g_up.pieces, g_down.held]
    )

    w_up_all = g_up.whole(table, [[attended]], [[attended]])
    part = up_gelu(hidden_low, w_up_all, full_bup)
    g_down.own_rows([attended], [part[0]])
    g_down.other_rows([part[0]])
    act, slope, full_up = up_gelu(hidden_low, w_up_all, full_bup, part, wait=g_down.own)
    w_down_all = g_down.whole(table, [[part[0]], [act]], [[act]])
    hat2, rstd2, result_low, raw, vecs, full_down, full_proj = down_norm(
        act,
        w_down_all,
        full_bdown,
        hat1,
        gain_one,
        bias_one,
        gain_two,
        bias_two,
        first_all.columns(4 * D, proj_width),
    )
    full_qkv, full_out, full_up, full_down, full_proj = (
        w.reshape(-1, w.shape[-1]) for w in (full_qkv, full_out, full_up, full_down, full_proj)
    )

    query_all = gather_relative(vecs[:q_tokens]).reshape(n_devices * q_tokens, -1)
    sums, doc_scores, stats = score_stats(
        vecs, query_all, query_ids, hot, counts, positive
    )
    stats = reduce_stats(stats)
    query_count = n_z * 2 * QPR
    losses = lax.dynamic_slice_in_dim(
        stats[:, 0] + jnp.log(stats[:, 1]) - stats[:, 2], row * query_count, query_count, 1
    )
    query_grads, doc_grads = score_grads(
        vecs, query_all, query_row, doc_column, sums, doc_scores, stats, positive
    )
    doc_part = head_back(doc_grads, raw, full_proj, hat2, rstd2, gain_two)
    query_grad = scatter_relative(
        query_grads.reshape(2, n_rows, n_z, q_tokens, -1), bf16, [doc_part[2]]
    )
    resid_two_grad, branch_grad, raw_grad, sums2 = head_back(
        doc_grads, raw, full_proj, hat2, rstd2, gain_two, query_grad, doc_part[:3]
    )
    sums2 = sums2 + doc_part[3]

    def sib_half(name, operands, tile, dtype=bf16, wait=()):
        return weight_half(name + "_sib", table, operands, n_rows, n_z, tile, other_type=dtype, wait=wait)

    def own_half(name, operands, tile, sib, wide=False, wait=()):
        other = exchange(sib, swap_core=True)
        return Scatter(*weight_half(name, table, operands, n_rows, n_z, tile, other, wait=wait), wide)

    def attention_part(i, wait):
        return attention_back(documents, qkv, attended_grad, cosine, sine, i, 2, wait=wait)

    whole_lanes = act.shape[1] // n_devices % LANES == 0
    if whole_lanes:
        down_sib = weight_pieces("grad_down_sib", table, act, branch_grad, n_rows, n_z)
    else:
        down_sib = sib_half("grad_down", [(act, branch_grad)], 512)
    inner_grad, grad_bup = act_back(branch_grad, full_down, slope, wait=[down_sib])
    if whole_lanes:
        other = exchange(down_sib, swap_core=True)
        parts = weight_pieces(
            "grad_down", table, act, branch_grad, n_rows, n_z, other, wait=[grad_bup]
        )
        down = Scatter(*parts, True)
    else:
        down = own_half("grad_down", [(act, branch_grad)], 512, down_sib, True, wait=[grad_bup])
    up_sib = sib_half("grad_up", [(hidden_low, inner_grad)], 1024, f32, wait=[down.send])
    resid_one_grad, out_grad, attended_grad, sums1 = hidden_back(
        inner_grad, full_up, resid_two_grad, hat1, rstd1, gain_one, full_out, wait=[up_sib]
    )
    d2 = down.step(sums1)
    up = own_half("grad_up", [(hidden_low, inner_grad)], 1024, up_sib, wait=[sums1, d2])
    d3 = down.step(up.send)
    out_pairs = [(attended, out_grad), (result_low, raw_grad)]
    out_sib = sib_half("grad_out", out_pairs, None, wait=[up.send])
    grad_a, sums_a = attention_part(0, [out_sib, d3])
    d4 = down.step(sums_a)
    u2 = up.step(sums_a)
    sib_a = sib_half("grad_qkv", [(tokens_half, grad_a)], 512, wait=[d4, u2])
    out = own_half("grad_out", out_pairs, None, out_sib, True, wait=[sib_a])
    grad_b, sums_b = attention_part(1, [out.send, d4, u2])
    o2 = out.step(sums_b)
    u3 = up.step(sums_b)
    sum_down = down.finish(sums_b)
    sib_b = sib_half("grad_qkv", [(tokens_half, grad_b)], 512, wait=[sum_down])
    qkv_a = own_half("grad_qkv", [(tokens_half, grad_a)], 512, sib_a, wait=[sib_b, o2, u3])
    o3 = out.step(qkv_a.send)
    u4 = up.step(qkv_a.send)
    qkv_b = own_half("grad_qkv", [(tokens_half, grad_b)], 512, sib_b, wait=[qkv_a.send, o3, u4])
    a2 = qkv_a.step(qkv_b.send)
    o4 = out.step(qkv_b.send)
    input_grad = input_back([grad_a, grad_b], full_qkv, resid_one_grad, wait=[qkv_b.send, a2, o4])
    sum_up = up.finish(input_grad)
    sum_out = out.finish(input_grad)
    b2 = qkv_b.step(input_grad)
    qkv_a.step(input_grad)
    grads = [sums_a[i] if j == 0 else sums_b[i] for i in range(3) for j in range(2)]
    grad_bqkv = jnp.concatenate(grads, axis=1)
    small = pack(
        [grad_bqkv, sums1[2:3], sums1[0:1], sums1[1:2], grad_bup, sums2[2:3], sums2[0:1], sums2[1:2]],
        n_devices,
        wait=[b2, sum_up, sum_out],
    )
    while qkv_b.stages[0][0] == "row":
        qkv_b.step(small)
    while qkv_a.stages[0][0] == "row":
        qkv_a.step()
    q3 = qkv_a.merge(qkv_b).send
    sum_out, sum_proj = sum_out[:, :D], sum_out[:, D : D + w_proj.shape[1]]
    q4 = qkv_a.step()
    small = scatter_small(
        small.reshape(n_devices, -1, LANES), f32, [[], [q3], [q3], [q4], [q4]]
    ).reshape(-1)
    sum_qkv = qkv_a.finish()
    width = D // 2
    sum_qkv = jnp.concatenate(
        [sum_qkv[:, at * width : (at + 1) * width] for at in (0, 3, 1, 4, 2, 5)], axis=1
    )
    pieces = []
    at = 0
    for width in widths:
        pieces.append(small[at : at + width])
        at += width
    s_bqkv, s_bout, s_gain1, s_bias1, s_bup, s_bdown, s_gain2, s_bias2 = pieces
    return (
        losses,
        result_low,
        input_grad,
        sum_qkv,
        s_bqkv,
        sum_out,
        s_bout,
        s_gain1,
        s_bias1,
        sum_up,
        s_bup,
        sum_down,
        s_bdown,
        s_gain2,
        s_bias2,
        sum_proj,
    )


def solution(mesh):
    shard = P(AXES, None)
    vec = P(AXES)
    in_specs = (
        shard,
        P(),
        P(),
        shard,
        vec,
        shard,
        vec,
        vec,
        vec,
        shard,
        vec,
        shard,
        vec,
        vec,
        vec,
        shard,
    )
    out_specs = (P(None, "row"), shard) + (shard,) + in_specs[3:]
    return jax.shard_map(
        on_device, mesh=mesh, in_specs=in_specs, out_specs=out_specs, check_vma=False
    )
```

```python
import functools

import jax
import jax.numpy as jnp
from jax import lax
from jax.experimental import pallas as pl
from jax.experimental.pallas import tpu as pltpu
from jax.sharding import PartitionSpec as P

D = 1024
HEADS = 16
HEAD_DIM = 64
PROJ_A = 128
PROJ_B = 96
PROJ_C = 64
QLEN = 32
DPR = 4
QPR = 1
DMOST = 330

AXES = ("row", "col")
highest = lax.Precision.HIGHEST
eps_norm = 1e-05
eps_vec = 1e-06
score_scale = 16.0
f32 = jnp.float32
bf16 = jnp.bfloat16


def sizes():
    n_rows = lax.axis_size("row")
    n_z = lax.axis_size("col") // 2
    return n_rows, n_z, n_rows.bit_length() - 1, n_z.bit_length() - 1


def after(value, *before):
    return lax.optimization_barrier((value,) + before)[0] if before else value


def place():
    col = lax.axis_index("col")
    return lax.axis_index("row"), col // 2, col % 2


def exchange(value, row_masks=(0, 0), z_mask=0, swap_core=False):
    n_rows, n_z, _, _ = sizes()
    pairs = []
    for r in range(n_rows):
        for z in range(n_z):
            for c in range(2):
                here = (r * n_z + z) * 2 + c
                there = ((r ^ row_masks[c]) * n_z + (z ^ z_mask)) * 2 + (
                    1 - c if swap_core else c
                )
                pairs.append((here, there))
    return lax.ppermute(value, AXES, pairs)


def stage_bit(core, stage, row_bits):
    return (stage + core) % row_bits


def stage_masks(stage):
    _, _, row_bits, _ = sizes()
    return tuple(1 << stage_bit(c, stage, row_bits) for c in range(2))


def piece_mask(core, piece):
    _, _, row_bits, _ = sizes()
    return sum(
        1 << stage_bit(core, j, row_bits) for j in range(row_bits) if piece >> j & 1
    )


def ordered(bit, own, other, axis):
    return jnp.stack([jnp.where(bit == 0, own, other), jnp.where(bit == 0, other, own)], axis)


def transfer(value, start=(), use=(), **move):
    return after(exchange(after(value, *start), **move), *use)


class Gather:
    def __init__(self, shard):
        self.held, self.count, self.shard, self.received = shard, 0, shard, []

    def along_z(self, start=(), use=()):
        _, n_z, _, z_bits = sizes()
        _, z, _ = place()
        bit = z_bits - 1 - self.count
        other = transfer(self.held, start, use, z_mask=1 << bit)
        self.received.append(other)
        self.held = ordered(z >> bit & 1, self.held, other, self.count)
        self.count += 1
        if self.count == z_bits:
            self.pieces = [self.held.reshape((n_z,) + self.shard.shape)]

    def all_z(self, *bounds):
        _, _, _, z_bits = sizes()
        for i in range(z_bits):
            self.along_z(*bounds[min(i, len(bounds) - 1)])

    def own_rows(self, start=(), use=()):
        _, _, row_bits, _ = sizes()
        self.own = [
            transfer(self.pieces[0], start, use, row_masks=stage_masks(stage))
            for stage in range(row_bits)
        ]
        self.pieces = self.pieces + self.own

    def other_rows(self, start=(), use=()):
        _, _, row_bits, _ = sizes()
        pieces = [self.pieces[0], self.own[0]]
        for stage in range(1, row_bits):
            pieces = pieces + [self.own[stage]] + [
                transfer(p, start, use, row_masks=stage_masks(stage)) for p in pieces[1:]
            ]
        self.pieces = pieces

    def all_rows(self, own, other):
        self.own_rows(*own)
        self.other_rows(*other)

    def whole(self, table, early=(), late=()):
        last = len(self.pieces) - 1
        sibs = [
            transfer(p, *(late if i == last else early), swap_core=True)
            for i, p in enumerate(self.pieces)
        ]
        return Weight(table, self.pieces + sibs)


def piece_table():
    n_rows, _, _, _ = sizes()
    row, _, core = place()
    tables = [
        jnp.array([piece_mask(c, k) for k in range(n_rows)], jnp.int32) for c in range(2)
    ]
    own = row ^ jnp.where(core == 0, tables[0], tables[1])
    sib = row ^ jnp.where(core == 0, tables[1], tables[0])
    steps = jnp.arange(n_rows)

    def piece_of(rows):
        return jnp.sum(jnp.where(rows[None, :] == steps[:, None], steps[None, :], 0), axis=1)

    return jnp.concatenate([own, sib, core[None], piece_of(own), piece_of(sib)]).astype(jnp.int32)


class Weight:
    def __init__(self, table, pieces, start=0, size=None):
        self.table, self.pieces = table, pieces
        self.start, self.size = start, size or pieces[0].shape[2]

    def columns(self, start, size):
        return Weight(self.table, self.pieces, self.start + start, size)

    @property
    def shape(self):
        n_rows, n_z, _, _ = sizes()
        return (n_rows, n_z, 2, self.pieces[0].shape[1], self.size)

    def specs(self):
        return [pl.BlockSpec(memory_space=pl.ANY)] * len(self.pieces)

    def scratch(self):
        return [
            pltpu.VMEM(self.shape, self.pieces[0].dtype),
            pltpu.SemaphoreType.DMA((len(self.pieces) + 1,)),
        ]

    def out_shape(self):
        return jax.ShapeDtypeStruct(self.shape, self.pieces[0].dtype)

    def load(self, table, pieces, out_ref, w_ref, sems):
        n_rows = len(pieces) // 2
        core = table[2 * n_rows]
        out = pltpu.make_async_copy(w_ref, out_ref, sems.at[2 * n_rows])
        if self.size != pieces[0].shape[2]:
            pieces = [p.at[:, :, pl.ds(self.start, self.size)] for p in pieces]

        @pl.when(pl.program_id(0) == 0)
        def _():
            copies = [
                pltpu.make_async_copy(
                    piece,
                    w_ref.at[table[i], :, core if i < n_rows else 1 - core],
                    sems.at[i],
                )
                for i, piece in enumerate(pieces)
            ]
            for c in copies:
                c.start()
            for c in copies:
                c.wait()
            out.start()

        @pl.when(pl.program_id(0) == pl.num_programs(0) - 1)
        def _():
            out.wait()


def gather_small(shard, uses=()):
    n_rows, n_z, row_bits, z_bits = sizes()
    row, z, core = place()
    uses = list(uses)

    def arrive(**move):
        other = exchange(held, **move)
        return after(other, uses.pop(0)) if uses else other

    held = shard
    for count, bit in enumerate(reversed(range(z_bits))):
        held = ordered(z >> bit & 1, held, arrive(z_mask=1 << bit), count)
    for count, bit in enumerate(reversed(range(row_bits))):
        held = ordered(row >> bit & 1, held, arrive(row_masks=(1 << bit, 1 << bit)), count)
    held = ordered(core, held, arrive(swap_core=True), row_bits + z_bits)
    return held.reshape((n_rows * n_z * 2,) + shard.shape)


def scatter_small(blocks, dtype, starts=()):
    n_rows, n_z, row_bits, z_bits = sizes()
    row, z, core = place()
    held = blocks.reshape((2,) * (row_bits + z_bits + 1) + blocks.shape[1:])
    starts = list(starts)

    def halve(held, axis, bit, **move):
        send = lax.dynamic_index_in_dim(held, 1 - bit, axis, keepdims=False).astype(dtype)
        keep = lax.dynamic_index_in_dim(held, bit, axis, keepdims=False)
        start = starts.pop(0) if starts else ()
        return keep.astype(f32) + transfer(send, start, **move).astype(f32)

    held = halve(held, row_bits + z_bits, core, swap_core=True)
    for bit in range(row_bits):
        held = halve(held, row_bits - 1 - bit, row >> bit & 1, row_masks=(1 << bit, 1 << bit))
    for bit in range(z_bits):
        held = halve(held, z_bits - 1 - bit, z >> bit & 1, z_mask=1 << bit)
    return held


def gather_relative(block):
    n_rows, n_z, _, _ = sizes()
    held = jnp.stack([block] + [exchange(block, z_mask=m) for m in range(1, n_z)])
    held = jnp.stack([held] + [exchange(held, row_masks=(m, m)) for m in range(1, n_rows)])
    return jnp.stack([held, exchange(held, swap_core=True)])


def scatter_relative(keep, send, use=()):
    n_rows, n_z, _, _ = sizes()
    held = keep + after(exchange(send, swap_core=True), *use).astype(f32)

    def step(held, count, move):
        parts = [exchange(held[m].astype(send.dtype), **move(m)) for m in range(1, count)]
        total = held[0]
        for part in parts:
            total = total + part.astype(f32)
        return total

    held = step(held, n_rows, lambda m: dict(row_masks=(m, m)))
    return step(held, n_z, lambda m: dict(z_mask=m))


def relative_order():
    n_rows, n_z, _, _ = sizes()
    row, z, core = place()
    at = jnp.arange(n_rows * n_z * 2)
    there_core = core ^ at // (n_rows * n_z)
    there_row = row ^ at // n_z % n_rows
    return ((there_row * n_z + (z ^ at % n_z)) * 2 + there_core).astype(jnp.int32)


class Scatter:
    def __init__(self, send, keep, wide=False):
        _, _, row_bits, z_bits = sizes()
        flat = lambda x: x.reshape((-1,) + x.shape[-2:])
        self.send, self.keep = flat(send), flat(keep)
        self.stages = [("row", j) for j in reversed(range(row_bits))]
        self.stages += [("z", b) for b in range(z_bits)]
        self.wide = self.stages[-1] if wide else None

    def receive(self):
        kind, at = self.stages.pop(0)
        move = dict(row_masks=stage_masks(at)) if kind == "row" else dict(z_mask=1 << at)
        return exchange(self.send, **move)

    def step(self, *use):
        _, z, _ = place()
        parts = (self.keep, after(self.receive(), *use))
        if not self.stages:
            return (parts[0] + parts[1].astype(f32))[0]
        kind, at = self.stages[0]
        half = self.keep.shape[0] // 2
        if kind == "row":
            pick = lambda x, other: x[half:] if other else x[:half]
        else:
            mine = z >> at & 1
            parts = tuple(x.reshape((half, 2) + x.shape[1:]) for x in parts)
            pick = lambda x, other: lax.dynamic_index_in_dim(
                x, 1 - mine if other else mine, 1, keepdims=False
            )
        total = lambda other: pick(parts[0], other) + pick(parts[1], other).astype(f32)
        self.send, self.keep = total(True), total(False)
        if self.stages[0] != self.wide:
            self.send = self.send.astype(bf16)
        return self.send

    def merge(self, other):
        self.send = jnp.concatenate([self.send, other.send], axis=-1)
        self.keep = jnp.concatenate([self.keep, other.keep], axis=-1)
        return self

    def finish(self, *use):
        while self.stages:
            out = self.step(*use)
        return out


def head_slices():
    return ((0, PROJ_A), (PROJ_A, PROJ_B), (PROJ_A + PROJ_B, PROJ_C))


LANES = 128


def whole_spec(shape):
    return pl.BlockSpec(
        shape, lambda *_: (0,) * len(shape), pipeline_mode=pl.Buffered(buffer_count=1)
    )


def row_spec(rows, width):
    return pl.BlockSpec((rows, width), lambda i, *_: (i, 0))


def col_spec(rows, width):
    return pl.BlockSpec((rows, width), lambda i, *_: (0, i))


def like(shape, dtype):
    return jax.ShapeDtypeStruct(shape, dtype)


def call(
    kernel, name, grid, in_specs, out_specs, out_shape, flops, moved, scratch=(), table=None, wait=(), aliases=None
):
    first = len(in_specs) + (0 if table is None else 1)
    in_specs = list(in_specs) + [pl.BlockSpec(memory_space=pl.ANY)] * len(wait)

    def body(*refs):
        kernel(*refs[:first], *refs[first + len(wait) :])

    run = pl.pallas_call(
        body,
        grid_spec=pltpu.PrefetchScalarGridSpec(
            num_scalar_prefetch=0 if table is None else 1,
            grid=grid,
            in_specs=in_specs,
            out_specs=out_specs,
            scratch_shapes=list(scratch),
        ),
        out_shape=out_shape,
        input_output_aliases=aliases or {},
        compiler_params=pltpu.CompilerParams(vmem_limit_bytes=56 << 20),
        cost_estimate=pl.CostEstimate(
            flops=int(flops), bytes_accessed=int(moved), transcendentals=0
        ),
        name=name,
    )
    return lambda *operands: run(*operands, *wait)


def swap_halves(x):
    lane = lax.broadcasted_iota(jnp.int32, x.shape, 1)
    half = HEAD_DIM // 2
    return jnp.where(
        lane % HEAD_DIM < half, pltpu.roll(x, LANES - half, 1), pltpu.roll(x, half, 1)
    )


QKV_TILE = 1024


def qkv_kernel(weight, table, x_ref, b_ref, cos_ref, sin_ref, *refs):
    pieces, (o_ref, w_out, w_ref, sems) = refs[:-4], refs[-4:]
    weight.load(table, pieces, w_out, w_ref, sems)
    tile = pl.program_id(0)
    per_part = D // QKV_TILE
    cols = pl.ds(pl.multiple_of(tile * QKV_TILE, LANES), QKV_TILE)
    w = w_ref[:, :, :, :, cols].reshape(x_ref.shape[1], QKV_TILE)
    bias = b_ref[...]

    @pl.when(tile < 2 * per_part)
    def _():
        scale = jnp.where(tile < per_part, HEAD_DIM**-0.5, 1.0)
        for row in range(0, x_ref.shape[0], TILE):
            rows = slice(row, row + TILE)
            acc = contract(x_ref[rows, :], w, 1, 0) + bias
            cosine = cos_ref[rows, :] * scale
            sine = sin_ref[rows, :] * scale
            for j in range(QKV_TILE // LANES):
                at = slice(j * LANES, (j + 1) * LANES)
                a = acc[:, at]
                o_ref[rows, at] = (a * cosine + swap_halves(a) * sine).astype(bf16)

    @pl.when(tile >= 2 * per_part)
    def _():
        for row in range(0, x_ref.shape[0], TILE):
            rows = slice(row, row + TILE)
            o_ref[rows, :] = (contract(x_ref[rows, :], w, 1, 0) + bias).astype(bf16)


def project_qkv(x, w, b, cosine, sine, wait=()):
    t = x.shape[0]
    any_out = pl.BlockSpec(memory_space=pl.ANY)
    return call(
        functools.partial(qkv_kernel, w),
        "project_qkv",
        (3 * D // QKV_TILE,),
        [
            whole_spec((t, D)),
            pl.BlockSpec((1, QKV_TILE), lambda i, _: (0, i)),
            whole_spec((t, LANES)),
            whole_spec((t, LANES)),
        ]
        + w.specs(),
        [col_spec(t, QKV_TILE), any_out],
        [like((t, 3 * D), bf16), w.out_shape()],
        6 * t * D * D,
        20 * t * D,
        w.scratch(),
        table=w.table,
        wait=wait,
    )(w.table, x, b, cosine, sine, *w.pieces)


TILE = 256


def normalized(v):
    mean = jnp.mean(v, axis=1, keepdims=True)
    centered = v - mean
    rstd = lax.rsqrt(jnp.mean(centered * centered, axis=1, keepdims=True) + eps_norm)
    return centered * rstd, rstd


def norm_back(g, hat, rstd, gain):
    y = g * gain
    return rstd * (
        y - jnp.mean(y, axis=1, keepdims=True) - hat * jnp.mean(y * hat, axis=1, keepdims=True)
    )


def add_up(ref, value):
    @pl.when(pl.program_id(0) == 0)
    def _():
        ref[...] = jnp.zeros_like(ref)

    ref[...] += value


def column_sum(x):
    return jnp.sum(x, axis=0, keepdims=True)


def out_norm_kernel(weight, table, a_ref, b_ref, x_ref, gain_ref, bias_ref, *refs):
    hat_ref, rstd_ref, low_ref, w_out, w_ref, sems = refs[-6:]
    weight.load(table, refs[:-6], w_out, w_ref, sems)
    w = w_ref[...].reshape(a_ref.shape[1], -1)
    v = x_ref[...].astype(f32) + contract(a_ref[...], w, 1, 0) + b_ref[...]
    hat, rstd = normalized(v)
    hat_ref[...] = hat
    rstd_ref[...] = jnp.broadcast_to(rstd, rstd_ref.shape)
    low_ref[...] = (hat * gain_ref[...] + bias_ref[...]).astype(bf16)


def out_norm(attended, w, b, x, gain, bias, wait=()):
    t = x.shape[0]
    vec = whole_spec((1, D))
    return call(
        functools.partial(out_norm_kernel, w),
        "out_norm",
        (t // TILE,),
        [row_spec(TILE, D), vec, row_spec(TILE, D), vec, vec] + w.specs(),
        [row_spec(TILE, D), row_spec(TILE, LANES), row_spec(TILE, D), pl.BlockSpec(memory_space=pl.ANY)],
        [like((t, D), f32), like((t, LANES), f32), like((t, D), bf16), w.out_shape()],
        2 * t * D * D,
        12 * t * D,
        w.scratch(),
        table=w.table,
        wait=wait,
    )(w.table, attended, b, x, gain, bias, *w.pieces)


UP_TILE = 1024
CHUNK = 32


def gelu_pair(x):
    phi = 0.5 + 0.5 * lax.erf(x * 0.5**0.5)
    return x * phi, phi + x * jnp.exp(x * x * -0.5) * (2.0 * jnp.pi) ** -0.5


def up_kernel(weight, table, h_ref, b_ref, *refs):
    act_ref, slope_ref, w_out, acc_ref, w_ref, sems = refs[-6:]
    out = w_out.at[:, :, :, :, pl.ds(weight.start, weight.size)]
    weight.load(table, refs[: len(weight.pieces)], out, w_ref, sems)
    cols = pl.ds(pl.multiple_of(pl.program_id(0) * UP_TILE, LANES), UP_TILE)
    acc_ref[...] = contract(h_ref[...], w_ref[:, :, :, :, cols].reshape(-1, UP_TILE), 1, 0)
    bias = b_ref[...]

    def step(i, _):
        rows = pl.ds(pl.multiple_of(i * CHUNK, CHUNK), CHUNK)
        act, slope = gelu_pair(acc_ref[rows, :] + bias)
        act_ref[rows, :] = act.astype(bf16)
        slope_ref[rows, :] = slope.astype(bf16)
        return 0

    lax.fori_loop(0, h_ref.shape[0] // CHUNK, step, 0)


def up_gelu(hidden, w, b, before=None, wait=()):
    t, ff = hidden.shape[0], w.size
    any_space = pl.BlockSpec(memory_space=pl.ANY)
    steps = ff // UP_TILE // 2
    first = 0 if before is None else steps
    before = [] if before is None else list(before)
    n_in = 3 + len(w.pieces)
    half = w.columns(first * UP_TILE, ff // 2)
    return call(
        functools.partial(up_kernel, half),
        "up_gelu",
        (steps,),
        [whole_spec((t, D)), pl.BlockSpec((1, UP_TILE), lambda i, _: (0, first + i))]
        + w.specs()
        + [any_space] * len(before),
        [pl.BlockSpec((t, UP_TILE), lambda i, _: (0, first + i))] * 2 + [any_space],
        [like((t, ff), bf16)] * 2 + [w.out_shape()],
        t * D * ff,
        2 * t * ff + D * ff,
        [pltpu.VMEM((t, UP_TILE), f32)] + half.scratch(),
        table=w.table,
        wait=wait,
        aliases={n_in + i: i for i in range(len(before))},
    )(w.table, hidden, b, *w.pieces, *before)


def head_masks(width):
    lane = lax.broadcasted_iota(jnp.int32, (1, width), 1)
    return [(lane >= start) & (lane < start + size) for start, size in head_slices()]


def head_lanes():
    for start, size in head_slices():
        low = start // LANES * LANES
        high = -(-(start + size) // LANES) * LANES
        lane = lax.broadcasted_iota(jnp.int32, (1, high - low), 1) + low
        yield slice(low, high), (lane >= start) & (lane < start + size)


def head_sums(x):
    out = jnp.zeros_like(x)
    for mask in head_masks(x.shape[1]):
        total = jnp.sum(jnp.where(mask, x, 0.0), axis=1, keepdims=True)
        out = jnp.where(mask, total, out)
    return out


def down_norm_kernel(
    weight, proj, table, a_ref, b_ref, hat1_ref, gain1_ref, bias1_ref, gain_ref, bias_ref, *refs
):
    n = len(weight.pieces)
    hat_ref, rstd_ref, low_ref, raw_ref, vec_ref = refs[-11:-6]
    w_out, p_out, w_ref, w_sems, p_ref, p_sems = refs[-6:]
    proj.load(table, refs[n : 2 * n], p_out, p_ref, p_sems)
    weight.load(table, refs[:n], w_out, w_ref, w_sems)
    w = w_ref[...].reshape(a_ref.shape[1], -1)
    p = p_ref[...].reshape(w.shape[1], -1)
    for row in range(0, a_ref.shape[0], TILE):
        rows = slice(row, row + TILE)
        hidden = hat1_ref[rows, :] * gain1_ref[...] + bias1_ref[...]
        hat, rstd = normalized(hidden + contract(a_ref[rows, :], w, 1, 0) + b_ref[...])
        hat_ref[rows, :] = hat
        rstd_ref[rows, :] = jnp.broadcast_to(rstd, (TILE, LANES))
        low = (hat * gain_ref[...] + bias_ref[...]).astype(bf16)
        low_ref[rows, :] = low
        raw = contract(low, p, 1, 0)
        raw_ref[rows, :] = raw
        vec_ref[rows, :] = (raw * lax.rsqrt(head_sums(raw * raw) + eps_vec)).astype(bf16)


def down_norm(act, w, b, hat1, gain1, bias1, gain, bias, proj, wait=()):
    t, ff = act.shape
    e = proj.size
    vec = whole_spec((1, D))
    any_space = pl.BlockSpec(memory_space=pl.ANY)
    return call(
        functools.partial(down_norm_kernel, w, proj),
        "down_norm",
        (t // TILE,),
        [row_spec(TILE, ff), vec, row_spec(TILE, D), vec, vec, vec, vec] + w.specs() + proj.specs(),
        [
            row_spec(TILE, D),
            row_spec(TILE, LANES),
            row_spec(TILE, D),
            row_spec(TILE, e),
            row_spec(TILE, e),
            any_space,
            any_space,
        ],
        [
            like((t, D), f32),
            like((t, LANES), f32),
            like((t, D), bf16),
            like((t, e), f32),
            like((t, e), bf16),
            w.out_shape(),
            proj.out_shape(),
        ],
        2 * t * D * ff,
        20 * t * D,
        w.scratch() + proj.scratch(),
        table=w.table,
        wait=wait,
    )(w.table, act, b, hat1, gain1, bias1, gain, bias, *w.pieces, *proj.pieces)


def head_back_kernel(
    has_query, g_ref, raw_ref, proj_ref, hat_ref, rstd_ref, gain_ref, *refs
):
    grad_ref, branch_ref, raw_out, sums_ref = refs[-4:]
    g, raw = g_ref[...], raw_ref[...]
    if has_query:
        q = refs[0][...]
        g = g + jnp.concatenate([q, jnp.zeros((g.shape[0] - q.shape[0], q.shape[1]), f32)], axis=0)
    scale = lax.rsqrt(head_sums(raw * raw) + eps_vec)
    y = raw * scale
    raw_grad = (scale * (g - y * head_sums(y * g))).astype(bf16)
    result_grad = contract(raw_grad, proj_ref[...], 1, 1)
    hat = hat_ref[...]
    grad = norm_back(result_grad, hat, rstd_ref[:, :1], gain_ref[...])
    branch = grad.astype(bf16)
    grad_ref[...] = grad
    branch_ref[...] = branch
    raw_out[...] = raw_grad
    add_up(
        sums_ref,
        jnp.concatenate(
            [
                column_sum(result_grad * hat),
                column_sum(result_grad),
                column_sum(branch.astype(f32)),
            ],
            axis=0,
        ),
    )


def head_back(g, raw, proj, hat, rstd, gain, query=None, before=(), wait=()):
    t, e = raw.shape
    first, steps = (1, t // TILE - 1) if query is None else (0, 1)
    extra = [] if query is None else [query]
    rows = lambda width: pl.BlockSpec((TILE, width), lambda i, *_: (first + i, 0))
    return call(
        functools.partial(head_back_kernel, query is not None),
        "head_back",
        (steps,),
        [
            rows(e),
            rows(e),
            whole_spec((D, e)),
            rows(D),
            rows(LANES),
            whole_spec((1, D)),
        ]
        + [whole_spec(x.shape) for x in extra]
        + [pl.BlockSpec(memory_space=pl.ANY)] * len(before),
        [rows(D), rows(D), rows(e), whole_spec((3, D))],
        [like((t, D), f32), like((t, D), bf16), like((t, e), bf16), like((3, D), f32)],
        2 * steps * TILE * D * e,
        16 * steps * TILE * D,
        wait=wait,
        aliases={6 + len(extra) + i: i for i in range(len(before))},
    )(g, raw, proj, hat, rstd, gain, *extra, *before)


def act_back_kernel(g_ref, w_ref, slope_ref, o_ref, sum_ref):
    back = (contract(g_ref[...], w_ref[...], 1, 1) * slope_ref[...].astype(f32)).astype(bf16)
    o_ref[...] = back
    sum_ref[...] = column_sum(back.astype(f32))


def act_back(branch, w, slope, wait=()):
    t, ff = slope.shape
    return call(
        act_back_kernel,
        "act_back",
        (ff // UP_TILE,),
        [whole_spec((t, D)), row_spec(UP_TILE, D), col_spec(t, UP_TILE)],
        [col_spec(t, UP_TILE), col_spec(1, UP_TILE)],
        [like((t, ff), bf16), like((1, ff), f32)],
        2 * t * D * ff,
        4 * t * ff + 2 * D * ff,
        wait=wait,
    )(branch, w, slope)


def hidden_back_kernel(
    g_ref, w_ref, resid_ref, hat_ref, rstd_ref, gain_ref, wout_ref,
    grad_ref, out_ref, att_ref, sums_ref,
):
    for row in range(0, g_ref.shape[0], TILE):
        rows = slice(row, row + TILE)
        hidden_grad = resid_ref[rows, :] + contract(g_ref[rows, :], w_ref[...], 1, 1)
        hat = hat_ref[rows, :]
        grad = norm_back(hidden_grad, hat, rstd_ref[rows, :1], gain_ref[...])
        low = grad.astype(bf16)
        grad_ref[rows, :] = grad
        out_ref[rows, :] = low
        att_ref[rows, :] = contract(low, wout_ref[...], 1, 1).astype(bf16)
        sums = [column_sum(hidden_grad * hat), column_sum(hidden_grad), column_sum(low.astype(f32))]
        if row == 0:
            add_up(sums_ref, jnp.concatenate(sums, axis=0))
        else:
            sums_ref[...] += jnp.concatenate(sums, axis=0)


def hidden_back(inner, w, resid, hat, rstd, gain, w_out, wait=()):
    t, ff = inner.shape
    return call(
        hidden_back_kernel,
        "hidden_back",
        (t // TILE,),
        [
            row_spec(TILE, ff),
            whole_spec((D, ff)),
            row_spec(TILE, D),
            row_spec(TILE, D),
            row_spec(TILE, LANES),
            whole_spec((1, D)),
            whole_spec((D, D)),
        ],
        [row_spec(TILE, D)] * 3 + [whole_spec((3, D))],
        [like((t, D), f32), like((t, D), bf16), like((t, D), bf16), like((3, D), f32)],
        2 * t * D * ff + 2 * t * D * D,
        2 * t * ff + 24 * t * D,
        wait=wait,
    )(inner, w, resid, hat, rstd, gain, w_out)


def input_back_kernel(groups, *refs):
    g_refs, (w_ref, resid_ref, o_ref) = refs[:groups], refs[groups:]
    total = resid_ref[...]
    for part in range(3):
        for i, g_ref in enumerate(g_refs):
            width = g_ref.shape[2]
            at = part * D + i * width
            total = total + contract(g_ref[part], w_ref[:, at : at + width], 1, 1)
    o_ref[...] = total


def input_back(grads, w, resid, wait=()):
    t = resid.shape[0]
    return call(
        functools.partial(input_back_kernel, len(grads)),
        "input_back",
        (t // TILE,),
        [pl.BlockSpec((3, TILE, g.shape[2]), lambda i: (0, i, 0)) for g in grads]
        + [whole_spec((D, 3 * D)), row_spec(TILE, D)],
        row_spec(TILE, D),
        like((t, D), f32),
        6 * t * D * D,
        20 * t * D,
        wait=wait,
    )(*grads, w, resid)


def block_masks(n_devices, width):
    n = width * n_devices
    column = lax.broadcasted_iota(jnp.int32, (n_devices, n), 1)
    first = lax.broadcasted_iota(jnp.int32, (n_devices, n), 0) * width
    mine = (column >= first) & (column < first + width)
    at = lax.broadcasted_iota(jnp.int32, (1, n), 1) % width
    return mine, at


def unpack_kernel(n_devices, widths, p_ref, *o_refs):
    start = 0
    for width, o_ref in zip(widths, o_refs):
        mine, at = block_masks(n_devices, width)
        copies = (at == lax.broadcasted_iota(jnp.int32, (width, at.shape[1]), 0)).astype(bf16)
        spread = contract(p_ref[:, start : start + width], copies, 1, 0)
        o_ref[...] = column_sum(jnp.where(mine, spread, 0.0))
        start += width


def unpack(packed, widths, wait=()):
    n_devices = packed.shape[0]
    return call(
        functools.partial(unpack_kernel, n_devices, widths),
        "unpack",
        (1,),
        [whole_spec(packed.shape)],
        [whole_spec((1, w * n_devices)) for w in widths],
        [like((1, w * n_devices), f32) for w in widths],
        10**8,
        10**5,
        wait=wait,
    )(packed)


def pack_kernel(n_devices, widths, *refs):
    o_ref = refs[-1]
    o_ref[...] = jnp.zeros_like(o_ref)
    start = 0
    for width, ref in zip(widths, refs):
        mine, at = block_masks(n_devices, width)
        copies = (at == lax.broadcasted_iota(jnp.int32, (width, at.shape[1]), 0)).astype(bf16)
        rest = jnp.where(mine, ref[...], 0.0)
        total = jnp.zeros((n_devices, width), f32)
        for _ in range(3):
            term = rest.astype(bf16)
            total = total + contract(term, copies, 1, 1)
            rest = rest - term.astype(f32)
        o_ref[:, start : start + width] = total
        start += width


def pack(vectors, n_devices, wait=()):
    widths = [v.shape[1] // n_devices for v in vectors]
    total = sum(widths)
    total += -total % LANES
    return call(
        functools.partial(pack_kernel, n_devices, widths),
        "pack",
        (1,),
        [whole_spec(v.shape) for v in vectors],
        whole_spec((n_devices, total)),
        like((n_devices, total), f32),
        10**8,
        10**5,
        wait=wait,
    )(*vectors)


def halves_kernel(n_rows, n_z, table, own_in, sib_in, own_ref, sib_ref):
    core = table[2 * n_rows]
    for a_ref, o_ref, side in ((own_in, own_ref, core), (sib_in, sib_ref, 1 - core)):
        t, k = a_ref.shape
        x = a_ref[...].T.reshape(n_z, 2, k // (2 * n_z), t)
        o_ref[...] = jnp.where(side == 0, x[:, 0], x[:, 1]).reshape(o_ref.shape)


def halves(table, a, n_rows, n_z, wait=()):
    t, k = a.shape
    block = k // n_rows
    out = pl.BlockSpec((block // 2, t), lambda i, _: (i, 0))
    return call(
        functools.partial(halves_kernel, n_rows, n_z),
        "halves",
        (n_rows,),
        [
            pl.BlockSpec((t, block), lambda i, tab: (0, tab[i])),
            pl.BlockSpec((t, block), lambda i, tab: (0, tab[n_rows + i])),
        ],
        [out, out],
        [like((k // 2, t), bf16)] * 2,
        10**6,
        8 * t * k,
        table=table,
        wait=wait,
    )(table, a, a)


def pick_columns(table, offset, n_rows, n_z, a_ref, picked):
    t, k = a_ref.shape
    block = k // n_rows
    half = block // 2
    r = half // n_z
    core = table[2 * n_rows]
    side = core if offset == 0 else 1 - core
    if r % LANES:
        m = lax.broadcasted_iota(jnp.int32, (block, half), 1)
        source = (m // r) * (2 * r) + side * r + m % r
        choose = (lax.broadcasted_iota(jnp.int32, (block, half), 0) == source).astype(bf16)
    for piece in range(n_rows):
        first = table[offset + piece] * block
        if r % LANES:
            x = a_ref[:, pl.ds(pl.multiple_of(first, LANES), block)]
            picked[:, piece * half : (piece + 1) * half] = contract(x, choose, 1, 0).astype(bf16)
        else:
            for z in range(n_z):
                x = a_ref[:, pl.ds(pl.multiple_of(first + (2 * z + side) * r, LANES), r)]
                at = piece * half + z * r
                picked[:, at : at + r] = x


def weight_kernel(picks, offset, n_rows, n_z, table, *refs):
    pairs = len(picks)
    ins, refs = refs[: 2 * pairs], refs[2 * pairs :]
    count = sum(picks)
    refs, picked = refs[: len(refs) - count], list(refs[len(refs) - count :])

    if count:

        @pl.when(pl.program_id(0) == 0)
        def _():
            into = list(picked)
            for pick, a_ref in zip(picks, ins[::2]):
                if pick:
                    pick_columns(table, offset, n_rows, n_z, a_ref, into.pop(0))

    totals = []
    for pick, a_ref, b_ref in zip(picks, ins[::2], ins[1::2]):
        b = b_ref[...]
        b = b.reshape(b.shape[-2:])
        if pick:
            totals.append(contract(picked.pop(0)[...], b, 0, 0))
        else:
            totals.append(contract(a_ref[...], b, 1, 0))
    total = totals[0] if pairs == 1 else jnp.concatenate(totals, axis=1)
    if len(refs) == 1:
        refs[0][...] = total.reshape(refs[0].shape).astype(refs[0].dtype)
    else:
        other, send_ref, keep_ref = refs
        total = total.reshape(other.shape) + other[...].astype(f32)
        half = keep_ref.shape[0]
        send_ref[...] = total[half:].astype(send_ref.dtype)
        keep_ref[...] = total[:half]


def weight_half(name, table, operands, n_rows, n_z, tile, other=None, other_type=bf16, wait=()):
    own = other is not None
    picks = [not isinstance(a, tuple) for a, _ in operands]
    lefts = [a[0 if own else 1] if isinstance(a, tuple) else a for a, _ in operands]
    rights = [b for _, b in operands]
    t = rights[0].shape[-2]
    k = lefts[0].shape[1] if picks[0] else 2 * lefts[0].shape[0]
    r = k // (n_rows * n_z * 2)
    if len(operands) == 1:
        b = rights[0]
        per_part = b.shape[-1] // tile
        n = b.shape[-1] * (b.shape[0] if b.ndim == 3 else 1)
        if b.ndim == 3:
            b_specs = [pl.BlockSpec((1, t, tile), lambda i, _: (i // per_part, 0, i % per_part))]
        else:
            b_specs = [col_spec(t, tile)]
    else:
        n = tile = sum(b.shape[1] for b in rights)
        b_specs = [whole_spec(b.shape) for b in rights]
    specs, arrays = [], []
    for a, b, b_spec in zip(lefts, rights, b_specs):
        specs += [whole_spec(a.shape), b_spec]
        arrays += [a, b]

    def block(rows):
        return pl.BlockSpec((rows, n_z, r, tile), lambda i, _: (0, 0, 0, i))

    def shape(rows, dtype):
        return like((rows, n_z, r, n), dtype)

    return call(
        functools.partial(weight_kernel, picks, 0 if own else n_rows, n_rows, n_z),
        name,
        (n // tile,),
        specs + ([block(n_rows)] if own else []),
        [block(n_rows // 2)] * 2 if own else block(n_rows),
        [shape(n_rows // 2, bf16), shape(n_rows // 2, f32)] if own else shape(n_rows, other_type),
        t * k * n,
        2 * t * (k + n) + 3 * k * n,
        [pltpu.VMEM((t, k // 2), bf16) for pick in picks if pick],
        table=table,
        wait=wait,
    )(table, *arrays, *([other] if own else []))


def piece_kernel(offset, n_rows, n_z, table, a_ref, b_ref, *refs):
    r = a_ref.shape[1] // (2 * n_z)
    core = table[2 * n_rows]
    side = core if offset == 0 else 1 - core
    blocks = [a_ref[:, pl.ds(pl.multiple_of((2 * z + side) * r, LANES), r)] for z in range(n_z)]
    total = contract(jnp.concatenate(blocks, axis=1), b_ref[...], 0, 0)
    if len(refs) == 1:
        refs[0][...] = total.reshape(refs[0].shape).astype(refs[0].dtype)
        return
    other, send_ref, keep_ref = refs
    total = total.reshape(other.shape) + other[...].astype(f32)
    kept = pl.program_id(0) < n_rows // 2

    @pl.when(kept)
    def _():
        keep_ref[...] = total

    @pl.when(jnp.logical_not(kept))
    def _():
        send_ref[...] = total.astype(send_ref.dtype)


def weight_pieces(name, table, a, b, n_rows, n_z, other=None, wait=()):
    (t, k), n = a.shape, b.shape[1]
    r = k // (n_rows * n_z * 2)
    half = n_rows // 2
    own = other is not None
    offset = 0 if own else n_rows
    block = (1, n_z, r, n)
    each = pl.BlockSpec(block, lambda i, _: (i, 0, 0, 0))
    outs = [
        pl.BlockSpec(block, lambda i, _: (jnp.maximum(i - half, 0), 0, 0, 0)),
        pl.BlockSpec(block, lambda i, _: (jnp.minimum(i, half - 1), 0, 0, 0)),
    ]
    return call(
        functools.partial(piece_kernel, offset, n_rows, n_z),
        name,
        (n_rows,),
        [
            pl.BlockSpec((t, k // n_rows), lambda i, tab: (0, tab[offset + i])),
            whole_spec(b.shape),
        ]
        + ([each] if own else []),
        outs if own else each,
        [like((half, n_z, r, n), bf16), like((half, n_z, r, n), f32)]
        if own
        else like((n_rows, n_z, r, n), bf16),
        t * k * n,
        2 * t * (k + n) + 3 * k * n,
        table=table,
        wait=wait,
    )(table, a, b, *([other] if own else []))


WINDOWS = (256, -(-(DMOST + 15) // 32) * 32)
NEG = -1e30


def contract(a, b, ca, cb):
    return lax.dot_general(a, b, (((ca,), (cb,)), ((), ())), preferred_element_type=f32)


def document_table(lengths):
    at = jnp.arange(DPR)
    starts = QPR * QLEN + jnp.sum(jnp.where(at[:, None] < at[None, :], lengths[:, None], 0), axis=0)
    need = starts % 16 + lengths
    ahead = (need[:, None] > need[None, :]) | ((need[:, None] == need[None, :]) & (at[:, None] < at[None, :]))
    rank = jnp.sum(ahead.astype(jnp.int32), axis=0)
    order = rank[None, :] == at[:, None]
    pick = lambda x: jnp.sum(jnp.where(order, x[None, :], 0), axis=1)
    wide = jnp.sum((need > WINDOWS[0]).astype(jnp.int32))
    return jnp.concatenate([pick(starts), pick(lengths), wide[None]]).astype(jnp.int32)


def for_documents(doc_ref, row_len, step):
    for wide in range(1, DPR):

        @pl.when(doc_ref[2 * DPR] == wide)
        def _():
            for d in range(DPR):
                window = WINDOWS[1] if d < wide else WINDOWS[0]
                start, size = doc_ref[d], doc_ref[DPR + d]
                base = pl.multiple_of(jnp.minimum((start // 16) * 16, row_len - window), 16)
                step(window, base, start - base, start - base + size)


def head_pair(x):
    lane = lax.broadcasted_iota(jnp.int32, x.shape, 1)
    zero = jnp.zeros_like(x)
    return jnp.concatenate(
        [jnp.where(lane < HEAD_DIM, x, zero), jnp.where(lane < HEAD_DIM, zero, x)], axis=0
    )


def pair_heads(x):
    n = x.shape[0] // 2
    lane = lax.broadcasted_iota(jnp.int32, (n, x.shape[1]), 1)
    return jnp.where(lane < HEAD_DIM, x[:n], x[n:])


def inside(n, low, high, axis):
    shape = (n, 1) if axis == 0 else (1, n)
    at = lax.broadcasted_iota(jnp.int32, shape, axis)
    return (at >= low) & (at < high)


def attend(q, k, v, low, high):
    s = contract(head_pair(q), k, 1, 1)
    s = s + jnp.where(inside(k.shape[0], low, high, 1), 0.0, NEG)
    p = jnp.exp(s - jnp.max(s, axis=1, keepdims=True))
    total = jnp.sum(p, axis=1, keepdims=True)
    return pair_heads(contract(p.astype(bf16), v, 1, 0) / total)


def attention_kernel(len_ref, q_ref, k_ref, v_ref, o_ref):
    def step(window, base, low, high):
        w = pl.ds(base, window)
        o = attend(q_ref[w, :], k_ref[w, :], v_ref[w, :], low, high)
        keep = inside(window, low, high, 0)
        o_ref[w, :] = jnp.where(keep, o, o_ref[w, :].astype(f32)).astype(bf16)

    for_documents(len_ref, q_ref.shape[0], step)
    o_ref[:QLEN, :] = attend(q_ref[:QLEN, :], k_ref[:128, :], v_ref[:128, :], 0, QLEN).astype(bf16)


def qkv_specs(t):
    per_part = D // LANES
    return [
        pl.BlockSpec((t, LANES), lambda i, _, p=p: (0, p * per_part + i)) for p in range(3)
    ]


def attention(lengths, qkv, wait=()):
    t = qkv.shape[0]
    return call(
        attention_kernel,
        "attention",
        (HEADS // 2,),
        qkv_specs(t),
        col_spec(t, LANES),
        like((t, D), bf16),
        2 * 10**10,
        8 * t * D,
        table=lengths,
        wait=wait,
    )(lengths, qkv, qkv, qkv)


def attend_back(q, k, v, g, low, high):
    n = q.shape[0]
    g = jnp.where(inside(n, low, high, 0), g, jnp.zeros_like(g))
    qq = head_pair(q)
    gg = head_pair(g)
    st = contract(k, qq, 1, 1)
    st = st + jnp.where(inside(k.shape[0], low, high, 0), 0.0, NEG)
    p = jnp.exp(st - jnp.max(st, axis=0, keepdims=True))
    p = p * (1.0 / jnp.sum(p, axis=0, keepdims=True))
    dp = contract(v, gg, 1, 1)
    delta = jnp.sum(p * dp, axis=0, keepdims=True)
    ds = (p * (dp - delta)).astype(bf16)
    dv = contract(p.astype(bf16), gg, 1, 0)
    dk = contract(ds, qq, 1, 0)
    dq = contract(ds, k, 0, 0) * (HEAD_DIM**-0.5)
    return pair_heads(dq), dk, dv


def attention_back_kernel(len_ref, q_ref, k_ref, v_ref, g_ref, cos_ref, sin_ref, o_ref, sum_ref, *sums):
    row_len = q_ref.shape[0]
    for ref in sums:
        ref[...] = jnp.zeros_like(ref)
    parts = attend_back(
        q_ref[:QLEN, :], k_ref[:128, :], v_ref[:128, :], g_ref[:QLEN, :], 0, QLEN
    )
    for ref, x in zip(sums, parts):
        ref[: x.shape[0], :] = x

    def step(window, base, low, high):
        w = pl.ds(base, window)
        parts = attend_back(q_ref[w, :], k_ref[w, :], v_ref[w, :], g_ref[w, :], low, high)
        for ref, x in zip(sums, parts):
            ref[w, :] += x

    for_documents(len_ref, row_len, step)
    cosine, sine = cos_ref[...], sin_ref[...]
    for part in range(3):
        x = sums[part][...]
        if part < 2:
            x = x * cosine - swap_halves(x) * sine
        x = x.astype(bf16)
        o_ref[part] = x
        sum_ref[part] = column_sum(x.astype(f32))


def attention_back(lengths, qkv, g, cosine, sine, group, groups, wait=()):
    t = qkv.shape[0]
    table = whole_spec((t, LANES))
    pairs = HEADS // 2 // groups
    first = group * pairs
    per_part = D // LANES
    specs = [
        pl.BlockSpec((t, LANES), lambda i, _, p=p: (0, p * per_part + first + i)) for p in range(3)
    ]
    return call(
        attention_back_kernel,
        "attention_back",
        (pairs,),
        specs + [pl.BlockSpec((t, LANES), lambda i, _: (0, first + i)), table, table],
        [
            pl.BlockSpec((3, t, LANES), lambda i, _: (0, 0, i)),
            pl.BlockSpec((3, 1, LANES), lambda i, _: (0, 0, i)),
        ],
        [like((3, t, D // groups), bf16), like((3, 1, D // groups), f32)],
        5 * 10**10 // groups,
        14 * t * D // groups,
        [pltpu.VMEM((t, LANES), f32)] * 3,
        table=lengths,
        wait=wait,
    )(lengths, qkv, qkv, qkv, g, cosine, sine)


SCORE_TILE = 256


def doc_inside(doc_ref, d):
    return doc_ref[...] == d


def score_exps(docs, queries, mask):
    picked = jnp.where(mask, docs, jnp.zeros_like(docs))
    return picked, jnp.exp(contract(picked, queries, 1, 1) * score_scale)


def split_dot(hot, x):
    high = x.astype(bf16)
    rest = (x - high.astype(f32)).astype(bf16)
    return contract(hot, high, 1, 0) + contract(hot, rest, 1, 0)


def score_kernel(
    doc_ref, query_ref, id_ref, hot_ref, count_ref, pos_ref, sum_ref, score_ref, stat_ref
):
    docs = doc_ref[...]
    n_queries = score_ref.shape[2]
    live = lax.broadcasted_iota(jnp.int32, (8, n_queries), 0) < DPR
    for head, (lanes, mask) in enumerate(head_lanes()):
        scores = jnp.zeros((8, n_queries), f32)
        for at in range(0, query_ref.shape[0], SCORE_TILE):
            _, e = score_exps(docs[:, lanes], query_ref[at : at + SCORE_TILE, lanes], mask)
            total = split_dot(hot_ref[...], e)
            sum_ref[head, :, at : at + SCORE_TILE] = total
            smooth = jnp.log(total) - count_ref[:, :1]
            query = lax.broadcasted_iota(jnp.int32, (SCORE_TILE, n_queries), 1)
            hot = (id_ref[at : at + SCORE_TILE, :] == query).astype(f32)
            scores += lax.dot_general(
                jnp.where(lax.broadcasted_iota(jnp.int32, smooth.shape, 0) < DPR, smooth, 0.0),
                hot,
                (((1,), (0,)), ((), ())),
                precision=highest,
                preferred_element_type=f32,
            )
        score_ref[head] = scores
        top = jnp.max(jnp.where(live, scores, NEG), axis=0, keepdims=True)
        den = column_sum(jnp.where(live, jnp.exp(scores - top), 0.0))
        pos = column_sum(jnp.where(live, scores * pos_ref[...], 0.0))
        stat_ref[head] = jnp.concatenate([top, den, pos], axis=0)


def score_grad_kernel(
    doc_ref, query_ref, id_ref, index_ref, sum_ref, score_ref, stat_ref, pos_ref,
    keep_ref, send_ref, dd_ref, dq_ref,
):
    docs = doc_ref[...]
    n_queries = score_ref.shape[2]
    dd_ref[...] = jnp.zeros_like(dd_ref)
    dq_ref[...] = jnp.zeros_like(dq_ref)
    index = index_ref[...]
    for head, (lanes, mask) in enumerate(head_lanes()):
        stats = stat_ref[head]
        grad = jnp.exp(score_ref[head] - stats[0:1]) / stats[1:2] - pos_ref[...]
        for at in range(0, query_ref.shape[0], SCORE_TILE):
            queries = query_ref[at : at + SCORE_TILE, lanes]
            picked, e = score_exps(docs[:, lanes], queries, mask)
            query = lax.broadcasted_iota(jnp.int32, (n_queries, SCORE_TILE), 0)
            hot = (id_ref[:, at : at + SCORE_TILE] == query).astype(f32)
            spread = lax.dot_general(
                grad, hot, (((1,), (0,)), ((), ())), precision=highest, preferred_element_type=f32
            )
            coef = score_scale * spread / sum_ref[head, :, at : at + SCORE_TILE]
            wide = jnp.zeros_like(e)
            for d in range(DPR):
                wide = jnp.where(index == d, coef[d : d + 1], wide)
            back = (e * wide).astype(bf16)
            dd_ref[:, lanes] += jnp.where(mask, contract(back, queries, 1, 0), 0.0)
            dq_ref[at : at + SCORE_TILE, lanes] += contract(back, picked, 0, 0)
    half = keep_ref.shape[0]
    keep_ref[...] = dq_ref[:half, :]
    send_ref[...] = dq_ref[half:, :].astype(send_ref.dtype)


def score_stats(docs, queries, ids, hot, counts, positive, wait=()):
    n, e = docs.shape
    n_tokens = queries.shape[0]
    n_queries = n_tokens // QLEN
    return call(
        score_kernel,
        "scores",
        (1,),
        [
            whole_spec((n, e)),
            whole_spec((n_tokens, e)),
            whole_spec((n_tokens, 1)),
            whole_spec((8, n)),
            whole_spec((8, LANES)),
            whole_spec((8, n_queries)),
        ],
        [
            whole_spec((3, 8, n_tokens)),
            whole_spec((3, 8, n_queries)),
            whole_spec((3, 3, n_queries)),
        ],
        [
            like((3, 8, n_tokens), f32),
            like((3, 8, n_queries), f32),
            like((3, 3, n_queries), f32),
        ],
        12 * n * n_tokens * e,
        10**6,
        wait=wait,
    )(docs, queries, ids, hot, counts, positive)


def score_grads(docs, queries, ids, index, sums, scores, stats, positive, wait=()):
    n, e = docs.shape
    n_tokens = queries.shape[0]
    n_queries = n_tokens // QLEN
    return call(
        score_grad_kernel,
        "score_grads",
        (1,),
        [
            whole_spec((n, e)),
            whole_spec((n_tokens, e)),
            whole_spec((1, n_tokens)),
            whole_spec((n, 1)),
            whole_spec((3, 8, n_tokens)),
            whole_spec((3, 8, n_queries)),
            whole_spec((3, 3, n_queries)),
            whole_spec((8, n_queries)),
        ],
        [whole_spec((n_tokens // 2, e)), whole_spec((n_tokens // 2, e)), whole_spec((n, e))],
        [like((n_tokens // 2, e), f32), like((n_tokens // 2, e), bf16), like((n, e), f32)],
        24 * n * n_tokens * e,
        10**6,
        [pltpu.VMEM((n_tokens, e), f32)],
        wait=wait,
    )(docs, queries, ids, index, sums, scores, stats, positive)


def layout(lengths, row_len, q_tokens):
    count = lengths.shape[0]
    before = jnp.arange(count)[:, None] <= jnp.arange(count)[None, :]
    ends = jnp.sum(jnp.where(before, lengths[:, None], 0), axis=0)
    offset = jnp.arange(row_len, dtype=jnp.int32) - q_tokens
    doc = jnp.sum((offset[:, None] >= ends[None, :]).astype(jnp.int32), axis=1)
    chosen = (doc[:, None] == jnp.arange(count, dtype=jnp.int32)[None, :]).astype(
        jnp.int32
    )
    begin = jnp.sum(chosen * (ends - lengths)[None, :], axis=1)
    is_query = offset < 0
    position = jnp.where(is_query, (offset + q_tokens) % QLEN, offset - begin)
    return position, doc


def combine_stats(one, two):
    top = jnp.maximum(one[:, 0], two[:, 0])
    den = one[:, 1] * jnp.exp(one[:, 0] - top) + two[:, 1] * jnp.exp(two[:, 0] - top)
    return jnp.stack([top, den, one[:, 2] + two[:, 2]], axis=1)


def reduce_stats(stats):
    n_rows, n_z, _, _ = sizes()
    moves = [[dict(swap_core=True)]]
    moves.append([dict(row_masks=(m, m)) for m in range(1, n_rows)])
    moves.append([dict(z_mask=m) for m in range(1, n_z)])
    for level in moves:
        parts = [exchange(stats, **move) for move in level]
        for part in parts:
            stats = combine_stats(stats, part)
    return stats


def on_device(
    tokens,
    lengths,
    positives,
    w_qkv,
    b_qkv,
    w_out,
    b_out,
    norm1_gain,
    norm1_bias,
    w_up,
    b_up,
    w_down,
    b_down,
    norm2_gain,
    norm2_bias,
    w_proj,
):
    n_rows, n_z, _, _ = sizes()
    n_devices = n_rows * n_z * 2
    row, z, core = place()
    device = (row * n_z + z) * 2 + core
    table = piece_table()
    row_len = tokens.shape[0]
    q_tokens = QPR * QLEN

    own_lengths = lax.dynamic_index_in_dim(lengths, device, 0, keepdims=False)
    position, doc_index = layout(own_lengths, row_len, q_tokens)
    documents = document_table(own_lengths)
    half = HEAD_DIM // 2
    frequency = 10000.0 ** (-jnp.arange(half, dtype=f32) / half)
    angles = position.astype(f32)[:, None] * frequency[None, :]
    cosine, sine = jnp.cos(angles), jnp.sin(angles)
    cosine = jnp.concatenate([cosine] * 4, axis=1)
    sine = jnp.concatenate([-sine, sine] * 2, axis=1)
    doc_index = jnp.where(jnp.arange(row_len) < q_tokens, -1, doc_index)
    slots = jnp.arange(8, dtype=jnp.int32)
    hot = (slots[:, None] == doc_index[None, :]).astype(bf16)
    counts = jnp.broadcast_to(
        jnp.log(jnp.pad(own_lengths, (0, 8 - DPR), constant_values=1).astype(f32))[:, None],
        (8, LANES),
    )
    positive = (
        (positives[None, :] == device * DPR + slots[:, None]) & (slots < DPR)[:, None]
    ).astype(f32)
    query_ids = relative_order()[:, None] * QPR + jnp.arange(q_tokens, dtype=jnp.int32)[None, :] // QLEN
    query_ids = query_ids.reshape(-1, 1)
    query_row = query_ids.reshape(1, -1)
    doc_column = doc_index[:, None]
    early = [hot, counts, positive, query_ids, query_row, doc_column]
    proj_width = -(-w_proj.shape[1] // LANES) * LANES
    w_first = jnp.concatenate(
        [w_qkv, w_out, jnp.pad(w_proj, ((0, 0), (0, proj_width - w_proj.shape[1])))], axis=1
    )
    g_qkv, g_up, g_down = (Gather(w) for w in (w_first, w_up, w_down))
    g_qkv.all_z((), ((), early))
    tokens_half = tuple(halves(table, tokens, n_rows, n_z, wait=[g_qkv.held]))
    g_qkv.all_rows([(), [tokens_half[0]]], ())
    first, last = g_qkv.own, g_qkv.pieces[-1]
    vectors = (b_qkv, b_out, norm1_gain, norm1_bias, b_up, b_down, norm2_gain, norm2_bias)
    widths = [v.shape[0] for v in vectors]
    packed = jnp.concatenate(vectors)
    packed = jnp.pad(packed, (0, -packed.shape[0] % LANES)).reshape(-1, LANES)
    packed = gather_small(packed, g_qkv.received + [first[0], last]).reshape(n_devices, -1)
    full_bqkv, full_bout, gain_one, bias_one, full_bup, full_bdown, gain_two, bias_two = unpack(
        packed, widths
    )
    g_up.all_z([[g_qkv.held]], [[], [last]])
    first_all = g_qkv.whole(table)

    qkv, full_qkv = project_qkv(
        tokens, first_all.columns(0, 3 * D), full_bqkv, cosine, sine, wait=[tokens_half[0]]
    )
    g_up.own_rows([last], [qkv])
    attended = attention(documents, qkv, wait=g_up.own)
    g_up.other_rows([qkv], [attended])
    g_down.all_z([[g_up.held], [qkv]], [[qkv], [attended]])
    hat1, rstd1, hidden_low, full_out = out_norm(
        attended, first_all.columns(3 * D, D), full_bout, tokens, gain_one, bias_one, wait=[*g_up.pieces, g_down.held]
    )

    w_up_all = g_up.whole(table, [[attended]], [[attended]])
    part = up_gelu(hidden_low, w_up_all, full_bup)
    g_down.own_rows([attended], [part[0]])
    g_down.other_rows([part[0]])
    act, slope, full_up = up_gelu(hidden_low, w_up_all, full_bup, part, wait=g_down.own)
    w_down_all = g_down.whole(table, [[part[0]], [act]], [[act]])
    hat2, rstd2, result_low, raw, vecs, full_down, full_proj = down_norm(
        act,
        w_down_all,
        full_bdown,
        hat1,
        gain_one,
        bias_one,
        gain_two,
        bias_two,
        first_all.columns(4 * D, proj_width),
    )
    full_qkv, full_out, full_up, full_down, full_proj = (
        w.reshape(-1, w.shape[-1]) for w in (full_qkv, full_out, full_up, full_down, full_proj)
    )

    query_all = gather_relative(vecs[:q_tokens]).reshape(n_devices * q_tokens, -1)
    sums, doc_scores, stats = score_stats(
        vecs, query_all, query_ids, hot, counts, positive
    )
    stats = reduce_stats(stats)
    query_count = n_z * 2 * QPR
    losses = lax.dynamic_slice_in_dim(
        stats[:, 0] + jnp.log(stats[:, 1]) - stats[:, 2], row * query_count, query_count, 1
    )
    query_keep, query_send, doc_grads = score_grads(
        vecs, query_all, query_row, doc_column, sums, doc_scores, stats, positive
    )
    doc_part = head_back(doc_grads, raw, full_proj, hat2, rstd2, gain_two)
    blocks = lambda x: x.reshape(n_rows, n_z, q_tokens, -1)
    query_grad = scatter_relative(blocks(query_keep), blocks(query_send), [doc_part[2]])
    resid_two_grad, branch_grad, raw_grad, sums2 = head_back(
        doc_grads, raw, full_proj, hat2, rstd2, gain_two, query_grad, doc_part[:3]
    )
    sums2 = sums2 + doc_part[3]

    def sib_half(name, operands, tile, dtype=bf16, wait=()):
        return weight_half(name + "_sib", table, operands, n_rows, n_z, tile, other_type=dtype, wait=wait)

    def own_half(name, operands, tile, sib, wide=False, wait=()):
        other = exchange(sib, swap_core=True)
        return Scatter(*weight_half(name, table, operands, n_rows, n_z, tile, other, wait=wait), wide)

    def attention_part(i, wait):
        return attention_back(documents, qkv, attended_grad, cosine, sine, i, 2, wait=wait)

    whole_lanes = act.shape[1] // n_devices % LANES == 0
    if whole_lanes:
        down_sib = weight_pieces("grad_down_sib", table, act, branch_grad, n_rows, n_z)
    else:
        down_sib = sib_half("grad_down", [(act, branch_grad)], 512)
    inner_grad, grad_bup = act_back(branch_grad, full_down, slope, wait=[down_sib])
    if whole_lanes:
        other = exchange(down_sib, swap_core=True)
        parts = weight_pieces(
            "grad_down", table, act, branch_grad, n_rows, n_z, other, wait=[grad_bup]
        )
        down = Scatter(*parts, True)
    else:
        down = own_half("grad_down", [(act, branch_grad)], 512, down_sib, True, wait=[grad_bup])
    up_sib = sib_half("grad_up", [(hidden_low, inner_grad)], 1024, f32, wait=[down.send])
    resid_one_grad, out_grad, attended_grad, sums1 = hidden_back(
        inner_grad, full_up, resid_two_grad, hat1, rstd1, gain_one, full_out, wait=[up_sib]
    )
    d2 = down.step(sums1)
    up = own_half("grad_up", [(hidden_low, inner_grad)], 1024, up_sib, wait=[sums1, d2])
    d3 = down.step(up.send)
    out_pairs = [(attended, out_grad), (result_low, raw_grad)]
    out_sib = sib_half("grad_out", out_pairs, None, wait=[up.send])
    grad_a, sums_a = attention_part(0, [out_sib, d3])
    d4 = down.step(sums_a)
    u2 = up.step(sums_a)
    sib_a = sib_half("grad_qkv", [(tokens_half, grad_a)], 512, wait=[d4, u2])
    out = own_half("grad_out", out_pairs, None, out_sib, True, wait=[sib_a])
    grad_b, sums_b = attention_part(1, [out.send, d4, u2])
    o2 = out.step(sums_b)
    u3 = up.step(sums_b)
    sum_down = down.finish(sums_b)
    sib_b = sib_half("grad_qkv", [(tokens_half, grad_b)], 512, wait=[sum_down])
    qkv_a = own_half("grad_qkv", [(tokens_half, grad_a)], 512, sib_a, wait=[sib_b, o2, u3])
    o3 = out.step(qkv_a.send)
    u4 = up.step(qkv_a.send)
    qkv_b = own_half("grad_qkv", [(tokens_half, grad_b)], 512, sib_b, wait=[qkv_a.send, o3, u4])
    a2 = qkv_a.step(qkv_b.send)
    o4 = out.step(qkv_b.send)
    input_grad = input_back([grad_a, grad_b], full_qkv, resid_one_grad, wait=[qkv_b.send, a2, o4])
    sum_up = up.finish(input_grad)
    sum_out = out.finish(input_grad)
    b2 = qkv_b.step(input_grad)
    qkv_a.step(input_grad)
    grads = [sums_a[i] if j == 0 else sums_b[i] for i in range(3) for j in range(2)]
    grad_bqkv = jnp.concatenate(grads, axis=1)
    small = pack(
        [grad_bqkv, sums1[2:3], sums1[0:1], sums1[1:2], grad_bup, sums2[2:3], sums2[0:1], sums2[1:2]],
        n_devices,
        wait=[b2, sum_up, sum_out],
    )
    while qkv_b.stages[0][0] == "row":
        qkv_b.step(small)
    while qkv_a.stages[0][0] == "row":
        qkv_a.step()
    q3 = qkv_a.merge(qkv_b).send
    sum_out, sum_proj = sum_out[:, :D], sum_out[:, D : D + w_proj.shape[1]]
    q4 = qkv_a.step()
    small = scatter_small(
        small.reshape(n_devices, -1, LANES), f32, [[], [q3], [q3], [q3], [q4]]
    ).reshape(-1)
    sum_qkv = qkv_a.finish()
    width = D // 2
    sum_qkv = jnp.concatenate(
        [sum_qkv[:, at * width : (at + 1) * width] for at in (0, 3, 1, 4, 2, 5)], axis=1
    )
    pieces = []
    at = 0
    for width in widths:
        pieces.append(small[at : at + width])
        at += width
    s_bqkv, s_bout, s_gain1, s_bias1, s_bup, s_bdown, s_gain2, s_bias2 = pieces
    return (
        losses,
        result_low,
        input_grad,
        sum_qkv,
        s_bqkv,
        sum_out,
        s_bout,
        s_gain1,
        s_bias1,
        sum_up,
        s_bup,
        sum_down,
        s_bdown,
        s_gain2,
        s_bias2,
        sum_proj,
    )


def solution(mesh):
    shard = P(AXES, None)
    vec = P(AXES)
    in_specs = (
        shard,
        P(),
        P(),
        shard,
        vec,
        shard,
        vec,
        vec,
        vec,
        shard,
        vec,
        shard,
        vec,
        vec,
        vec,
        shard,
    )
    out_specs = (P(None, "row"), shard) + (shard,) + in_specs[3:]
    return jax.shard_map(
        on_device, mesh=mesh, in_specs=in_specs, out_specs=out_specs, check_vma=False
    )
```
